32 devices in a mesh: grp: 4 (over y, x), box: 8 (over z, core).
Axes of the slice: x: 2, y: 2, z: 4, core: 2. Of those that a mesh axis runs over, the one named last changes fastest.
Arguments:
- source: float32 [128, 8, 16, 128], P('grp', 'box'), may hold values from -6 to 6
- alpha_coef: float32 [128, 8, 16, 128], P('grp', 'box'), may hold values from 0.02 to 0.2
- beta_coef: float32 [128, 8, 16, 128], P('grp', 'box'), may hold values from 0.5 to 5
Outputs:
- solution: float32 [128, 8, 16, 128], P('grp', 'box')
The draws below stay inside these ranges and needn't reach their ends.
All inputs are finite; a program needn't handle non-finite values.
Results may differ from the reference program's by a relative error of at most 0.00002.
Values sent between devices are 32-bit elements; how exact they have to be, the bound alone decides.
No kernel may reach another device: no remote copies, remote signals or barrier semaphores. Data moves between devices by JAX's collectives and lax.ppermute only.
A program may use at most 128 MiB of HBM per device.

```python
import math
import jax
import jax.numpy as jnp
import numpy as np

CY = 16
NZ = 128
SWEEPS = 2
COARSE_SWEEPS = 4
NX = 128
NY = 128
N_BOX = 8


def block_levels(own_key, dims, pieces, low, high):
    loudness = 1.0
    for axis_at, blocks in pieces:
        heights = jax.random.uniform(jax.random.fold_in(jax.random.fold_in(own_key, 6), axis_at), (blocks,), jnp.float32, low / len(pieces), high / len(pieces))
        loudness = loudness * jnp.repeat(jnp.exp(heights), dims[axis_at] // blocks).reshape((-1,) + (1,) * (len(dims) - 1 - axis_at))
    return loudness


def centred(own_key, shape, scale, reach, cuts=(), held_as=jnp.bfloat16):
    entries = jax.random.normal(own_key, shape, jnp.float32) * scale
    if len(cuts) > 0:
        entries = block_levels(own_key, shape, cuts, -0.22, 0.18) * entries
    return jnp.clip(entries, min=-reach, max=reach).astype(held_as)


def setup_inputs(seed: int = 0) -> dict:
    keys = jax.random.split(jax.random.key(seed), 4)
    return {
        "source": centred(keys[0], (NX, N_BOX, CY, NZ), 1.0, 6.0, ((0, 4), (1, 8)), jnp.float32),
        "alpha_coef": jnp.clip(jnp.exp(math.log(0.2) - 2.3025851 * jax.random.uniform(keys[1], (NX, N_BOX, CY, NZ), jnp.float32) ** block_levels(keys[1], (NX, N_BOX, CY, NZ), ((0, 4), (1, 8)), -0.2, 0.2)), 0.02, 0.2),
        "beta_coef": jnp.clip(jnp.exp(math.log(5.0) - 2.3025851 * jax.random.uniform(keys[2], (NX, N_BOX, CY, NZ), jnp.float32) ** block_levels(keys[2], (NX, N_BOX, CY, NZ), ((0, 4), (1, 8)), -0.2, 0.2)), 0.5, 5.0),
    }


OMEGA = 0.7
SHIFTS = ((1, 0, 0), (-1, 0, 0), (0, 1, 0), (0, -1, 0), (0, 0, 1), (0, 0, -1))


def inner_view(padded, step_x, step_y, step_z):
    return padded[1 + step_x:padded.shape[0] - 1 + step_x, 1 + step_y:padded.shape[1] - 1 + step_y, 1 + step_z:padded.shape[2] - 1 + step_z]


def neighbours(field_pad, beta_pad):
    centre = inner_view(beta_pad, 0, 0, 0)
    diag_sum = jnp.zeros(centre.shape, jnp.float32)
    off_sum = jnp.zeros(centre.shape, jnp.float32)
    for shift in SHIFTS:
        face_coef = 0.5 * (centre + inner_view(beta_pad, shift[0], shift[1], shift[2]))
        diag_sum = diag_sum + face_coef
        off_sum = off_sum + face_coef * inner_view(field_pad, shift[0], shift[1], shift[2])
    return diag_sum, off_sum


def applied_global(field, alpha_c, beta_c, scale):
    diag_sum, off_sum = neighbours(jnp.pad(field, 1), jnp.pad(beta_c, 1))
    return alpha_c * field + scale * (diag_sum * field - off_sum), diag_sum


def jacobi_global(field, source, alpha_c, beta_c, scale):
    applied, diag_sum = applied_global(field, alpha_c, beta_c, scale)
    return field + OMEGA * (source - applied) / (alpha_c + scale * diag_sum)


def restrict(values):
    shaped = values.reshape(values.shape[0] // 2, 2, values.shape[1] // 2, 2, values.shape[2] // 2, 2)
    return jnp.sum(shaped, axis=(1, 3, 5)) * 0.125


def prolong(coarse):
    wide = jnp.broadcast_to(coarse[:, None, :, None, :, None], (coarse.shape[0], 2, coarse.shape[1], 2, coarse.shape[2], 2))
    return wide.reshape(2 * coarse.shape[0], 2 * coarse.shape[1], 2 * coarse.shape[2])


def block_order():
    return np.array([slot_pos ^ (slot_pos >> 1) for slot_pos in range(N_BOX)], dtype=np.int32)


def to_grid(values):
    return values[:, block_order()].reshape(NX, NY, NZ)


def from_grid(values):
    inverse = np.argsort(block_order()).astype(np.int32)
    return values.reshape(NX, N_BOX, CY, NZ)[:, inverse]


def reference(source, alpha_coef, beta_coef):
    source = to_grid(source)
    alpha_coef = to_grid(alpha_coef)
    beta_coef = to_grid(beta_coef)
    field0 = jnp.zeros(source.shape, jnp.float32)
    for sweep in range(SWEEPS):
        field0 = jacobi_global(field0, source, alpha_coef, beta_coef, 1.0)
    applied, unused = applied_global(field0, alpha_coef, beta_coef, 1.0)
    source1 = restrict(source - applied)
    alpha1 = restrict(alpha_coef)
    beta1 = restrict(beta_coef)
    field1 = jnp.zeros(source1.shape, jnp.float32)
    for sweep in range(SWEEPS):
        field1 = jacobi_global(field1, source1, alpha1, beta1, 0.25)
    applied, unused = applied_global(field1, alpha1, beta1, 0.25)
    source2 = restrict(source1 - applied)
    alpha2 = restrict(alpha1)
    beta2 = restrict(beta1)
    field2 = jnp.zeros(source2.shape, jnp.float32)
    for sweep in range(COARSE_SWEEPS):
        field2 = jacobi_global(field2, source2, alpha2, beta2, 0.0625)
    field1 = field1 + prolong(field2)
    for sweep in range(SWEEPS):
        field1 = jacobi_global(field1, source1, alpha1, beta1, 0.25)
    field0 = field0 + prolong(field1)
    for sweep in range(SWEEPS):
        field0 = jacobi_global(field0, source, alpha_coef, beta_coef, 1.0)
    return from_grid(field0)
```

```python
import functools

import jax
import jax.numpy as jnp
from jax import lax
from jax.experimental import pallas as pl
from jax.experimental.pallas import tpu as pltpu
from jax.sharding import PartitionSpec as P

OMEGA = 0.7
FRAME = 8
WIDE_F = 6
WIDE_B = 7
COARSE_X = 6
FINE_X = 3
LANES = 128
ANY = pl.BlockSpec(memory_space=pl.ANY)
VMEM = pl.BlockSpec(memory_space=pltpu.VMEM)
LIMIT = 56 * 1024 * 1024


def params():
    return pltpu.CompilerParams(vmem_limit_bytes=LIMIT)


def gray_position(code, bit_count):
    position = code
    for shift in range(1, bit_count):
        position = position ^ (code >> shift)
    return position


def box_parity():
    bit_count = lax.axis_size("box").bit_length() - 1
    return gray_position(lax.axis_index("box"), bit_count) & 1


def run_copies(pairs, sems):
    copies = [pltpu.make_async_copy(src, dst, sems.at[at]) for at, (src, dst) in enumerate(pairs)]
    for copy in copies:
        copy.start()
    return copies


def wait_copies(copies):
    for copy in copies:
        copy.wait()


def lane_ids(shape):
    return lax.broadcasted_iota(jnp.int32, shape, 1)


def y_next(row):
    return pltpu.roll(row, row.shape[0] - 1, 0)


def y_prev(row):
    return pltpu.roll(row, 1, 0)


def z_next(row, dist):
    return pltpu.roll(row, LANES - dist, 1)


def z_prev(row, dist):
    return pltpu.roll(row, dist, 1)


def coefficients(alpha, beta, beta_prev, beta_next, dist, scale):
    half = 0.5 * scale
    lane = lane_ids(beta.shape)
    inside = lane < LANES - dist
    up_z = jnp.where(inside, z_next(beta, dist), 0.0)
    down_z = jnp.where(lane >= dist, z_prev(beta, dist), 0.0)
    up_y = y_next(beta)
    face_x = half * (beta + beta_next)
    face_y = half * (beta + up_y)
    face_z = jnp.where(inside, half * (beta + up_z), 0.0)
    total = (beta_prev + beta_next) + (up_y + y_prev(beta)) + (up_z + down_z)
    diagonal = alpha + half * (6.0 * beta + total)
    inverse = jnp.where(alpha > 0.0, OMEGA / diagonal, 0.0)
    return face_x, face_y, face_z, diagonal, inverse


def off_sum(at, v, faces, dist):
    face_x, face_y, face_z = faces
    here = v[at]
    fy = face_y[at]
    fz = face_z[at]
    along_x = face_x[at] * v[at + 1] + face_x[at - 1] * v[at - 1]
    along_y = fy * y_next(here) + y_prev(fy * here)
    along_z = fz * z_next(here, dist) + z_prev(fz * here, dist)
    return here, along_x + along_y + along_z


def relaxed(at, v, f, inverse, faces, dist):
    here, off = off_sum(at, v, faces, dist)
    return (1.0 - OMEGA) * here + inverse[at] * (f[at] + off)


def rows_loop(low, high, step, fn):
    trips = (high - low) // step

    def trip(t, carry):
        base = low + t * step
        for k in range(step):
            fn(base + k)
        return carry

    lax.fori_loop(0, trips, trip, 0)
    for row in range(low + trips * step, high):
        fn(row)


def pair_sum_z(row, dist):
    lane = lane_ids(row.shape)
    first = (lane // dist) % 2 == 0
    return row + jnp.where(first, z_next(row, dist), z_prev(row, dist))


def strided_pair(ref, at, count):
    return ref[at, pl.ds(0, count, stride=2), :] + ref[at, pl.ds(1, count, stride=2), :]


def pack_x_kernel(f, a, b, up, down, sems):
    count = f.shape[0]
    pairs = []
    row = 0
    for ref, wide in ((f, WIDE_F), (a, WIDE_F), (b, WIDE_B)):
        pairs.append((ref.at[pl.ds(count - wide, wide)], up.at[pl.ds(row, wide)]))
        pairs.append((ref.at[pl.ds(0, wide)], down.at[pl.ds(row, wide)]))
        row += wide
    wait_copies(run_copies(pairs, sems))


def pack_y_kernel(f, a, b, low, high, to_even, to_odd, sems):
    count = f.shape[0]
    parity = box_parity()
    pairs = []
    for out, start in ((to_even, FRAME * (1 - parity)), (to_odd, FRAME * parity)):
        rows = pl.ds(pl.multiple_of(start, FRAME), FRAME)
        row = 0
        got = 0
        for ref, wide in ((f, WIDE_F), (a, WIDE_F), (b, WIDE_B)):
            pairs.append((low.at[pl.ds(got, wide), rows], out.at[pl.ds(row, wide)]))
            pairs.append((ref.at[:, rows], out.at[pl.ds(row + wide, count)]))
            pairs.append((high.at[pl.ds(got, wide), rows], out.at[pl.ds(row + wide + count, wide)]))
            row += count + 2 * wide
            got += wide
    wait_copies(run_copies(pairs, sems))


def down_kernel(
    f, a, b, low, high, from_even, from_odd,
    out_v, out_f, out_inv, out_fx, out_fy, out_fz,
    out_v1, out_f1, out_inv1, out_fx1, out_fy1, out_fz1,
    out_coarse, to_up, to_down,
    F, A, B, FX, FY, FZ, DG, IN, V, U,
    T, A1, B1, D1, W1, T1, T2, sems, out_sems,
):
    count = f.shape[0]
    depth = f.shape[1]
    parity = box_parity()
    own_y = pl.ds(FRAME, depth)
    even_y = pl.ds(pl.multiple_of((FRAME + depth) * (1 - parity), FRAME), FRAME)
    odd_y = pl.ds(pl.multiple_of((FRAME + depth) * parity, FRAME), FRAME)
    pairs = []
    row = 0
    got = 0
    for ref, wide, dst in ((f, WIDE_F, F), (a, WIDE_F, A), (b, WIDE_B, B)):
        span = count + 2 * wide
        pairs.append((ref, dst.at[pl.ds(FRAME, count), own_y]))
        pairs.append((low.at[pl.ds(got, wide)], dst.at[pl.ds(FRAME - wide, wide), own_y]))
        pairs.append((high.at[pl.ds(got, wide)], dst.at[pl.ds(FRAME + count, wide), own_y]))
        for src, rows in ((from_even, even_y), (from_odd, odd_y)):
            pairs.append((src.at[pl.ds(row, span)], dst.at[pl.ds(FRAME - wide, span), rows]))
        row += span
        got += wide
    wait_copies(run_copies(pairs, sems))

    faces = (FX, FY, FZ)
    end = count + 2 * FRAME

    FX[1] = 0.5 * (B[1] + B[2])

    def coef_row(i):
        fx, fy, fz, dg, inv = coefficients(A[i], B[i], B[i - 1], B[i + 1], 1, 1.0)
        FX[i] = fx
        FY[i] = fy
        FZ[i] = fz
        DG[i] = dg
        IN[i] = inv
        V[i] = inv * F[i]

    rows_loop(2, end - 2, 2, coef_row)

    kept = pl.ds(FRAME - 2, count + 4)
    outs = [(F, out_f), (IN, out_inv), (FX, out_fx), (FY, out_fy), (FZ, out_fz)]
    out_copies = run_copies([(src.at[kept], dst) for src, dst in outs], out_sems)

    def sweep_row(i):
        U[i] = relaxed(i, V, F, IN, faces, 1)

    rows_loop(3, end - 3, 2, sweep_row)
    last = pltpu.make_async_copy(U.at[kept], out_v, out_sems.at[5])
    last.start()
    out_copies.append(last)

    def residual(i):
        here, off = off_sum(i, U, faces, 1)
        return F[i] - DG[i] * here + off

    half_rows = (depth + 2 * FRAME) // 2

    def restrict_row(j):
        T[j] = residual(2 * j) + residual(2 * j + 1)

    rows_loop(2, end // 2 - 2, 1, restrict_row)

    def level1_source(j):
        out_f1[j] = 0.125 * pair_sum_z(strided_pair(T, j, half_rows), 1)

    rows_loop(2, end // 2 - 2, 2, level1_source)

    def level1_coef(j):
        for src, dst in ((A, A1), (B, B1)):
            both = strided_pair(src, 2 * j, half_rows) + strided_pair(src, 2 * j + 1, half_rows)
            dst[j] = 0.125 * pair_sum_z(both, 1)

    rows_loop(1, end // 2 - 1, 2, level1_coef)

    faces1 = (out_fx1, out_fy1, out_fz1)
    end1 = end // 2
    out_fx1[1] = 0.125 * (B1[1] + B1[2])

    def coef_row1(i):
        fx, fy, fz, dg, inv = coefficients(A1[i], B1[i], B1[i - 1], B1[i + 1], 2, 0.25)
        out_fx1[i] = fx
        out_fy1[i] = fy
        out_fz1[i] = fz
        D1[i] = dg
        out_inv1[i] = inv
        W1[i] = inv * out_f1[i]

    rows_loop(2, end1 - 2, 4, coef_row1)

    def sweep_row1(i):
        out_v1[i] = relaxed(i, W1, out_f1, out_inv1, faces1, 2)

    rows_loop(3, end1 - 3, 3, sweep_row1)

    def residual1(i):
        here, off = off_sum(i, out_v1, faces1, 2)
        return out_f1[i] - D1[i] * here + off

    first1 = FRAME // 2
    count1 = count // 2
    count2 = count // 4
    quarter_rows = half_rows // 2
    lane = lane_ids((1, LANES))

    def coarse_row(x):
        i = first1 + 2 * x
        T1[0, x] = residual1(i) + residual1(i + 1)
        T1[1, x] = A1[i] + A1[i + 1]
        T1[2, x] = B1[i] + B1[i + 1]

    rows_loop(0, count2, 1, coarse_row)
    own2 = FRAME // 4
    depth2 = depth // 4

    def coarse_pack(x):
        for k in range(3):
            both = T1[k, x, pl.ds(0, quarter_rows, stride=2), :] + T1[k, x, pl.ds(1, quarter_rows, stride=2), :]
            value = 0.125 * pair_sum_z(both, 2)
            packed = jnp.zeros((1, LANES), jnp.float32)
            for y in range(depth2):
                packed = packed + jnp.where(lane % depth2 == y, value[own2 + y:own2 + y + 1], 0.0)
            out_coarse[x, k:k + 1] = packed

    rows_loop(0, count2, 1, coarse_pack)

    own1 = slice(first1, first1 + depth // 2)
    for k in range(COARSE_X):
        to_up[k, 0:3] = out_coarse[count2 - COARSE_X + k, 0:3]
        to_down[k, 0:3] = out_coarse[k, 0:3]
    for k in range(FINE_X):
        to_up[COARSE_X + k] = out_v1[first1 + count1 - FINE_X + k, own1]
        to_down[COARSE_X + k] = out_v1[first1 + k, own1]
    wait_copies(out_copies)


def pack_coarse_kernel(coarse, v1, low, high, to_even, to_odd):
    parity = box_parity()
    count2 = coarse.shape[0]
    first1 = FRAME // 2
    depth1 = 8
    count1 = 2 * count2
    for out, top in ((to_even, parity == 0), (to_odd, parity == 1)):
        for k in range(COARSE_X):
            out[k, 0:3] = low[k, 0:3]
            out[COARSE_X + count2 + k, 0:3] = high[k, 0:3]
        for k in range(count2):
            out[COARSE_X + k, 0:3] = coarse[k, 0:3]

        def facing(tile):
            return jnp.where(top, tile[depth1 - FINE_X:], tile[:FINE_X])

        for k in range(FINE_X):
            out[k, 3:3 + FINE_X] = facing(low[COARSE_X + k])
            out[FINE_X + count1 + k, 3:3 + FINE_X] = facing(high[COARSE_X + k])
        for k in range(count1):
            out[FINE_X + k, 3:3 + FINE_X] = facing(v1[first1 + k, first1:first1 + depth1])


def up_kernel(
    own, near_even, near_odd, far_even, far_odd, low, high,
    in_v, in_f, in_inv, in_fx, in_fy, in_fz,
    in_v1, in_f1, in_inv1, in_fx1, in_fy1, in_fz1,
    out,
    V, F, IN, FX, FY, FZ, U,
    V1, F1, IN1, FX1, FY1, FZ1, U1,
    R, S2, A2, B2, FX2, FY2, FZ2, IN2, V2, U2, PT, P0,
    sems, state_sems,
):
    parity = box_parity()
    below = 1 + 2 * (1 - parity)
    copies = run_copies(
        [
            (own, R.at[2]),
            (near_even, R.at[below]),
            (near_odd, R.at[4 - below]),
            (far_even, R.at[4 * (1 - parity)]),
            (far_odd, R.at[4 * parity]),
        ],
        sems,
    )
    states = run_copies(
        [
            (in_v1, V1), (in_f1, F1), (in_inv1, IN1), (in_fx1, FX1), (in_fy1, FY1), (in_fz1, FZ1),
            (in_v, V), (in_f, F), (in_inv, IN), (in_fx, FX), (in_fy, FY), (in_fz, FZ),
        ],
        state_sems,
    )
    wait_copies(copies)

    rows2 = B2.shape[1]
    span2 = B2.shape[0]
    sub = lax.broadcasted_iota(jnp.int32, (rows2, LANES), 0)
    lane = lane_ids((rows2, LANES))
    block = (sub + 2) // 4
    mine = lane % 4 == (sub + 2) % 4
    last_of_four = lane % 4 == 3

    def unpack_row(x):
        for k, dst in enumerate((S2, A2, B2)):
            packed = jnp.broadcast_to(R[0, x, k:k + 1], (rows2, LANES))
            for slot in range(1, 5):
                packed = jnp.where(block == slot, jnp.broadcast_to(R[slot, x, k:k + 1], (rows2, LANES)), packed)
            t = jnp.where(mine, packed, 0.0)
            t = t + z_prev(t, 1)
            t = t + z_prev(t, 2)
            t = jnp.where(last_of_four, t, 0.0)
            t = t + z_next(t, 1)
            dst[x] = t + z_next(t, 2)

    rows_loop(0, span2, 2, unpack_row)
    FX2[0] = 0.5 * 0.0625 * (B2[0] + B2[1])

    def coef_row2(i):
        fx, fy, fz, dg, inv = coefficients(A2[i], B2[i], B2[i - 1], B2[i + 1], 4, 0.0625)
        FX2[i] = fx
        FY2[i] = fy
        FZ2[i] = fz
        IN2[i] = inv
        V2[i] = inv * S2[i]

    rows_loop(1, span2 - 1, 2, coef_row2)
    faces2 = (FX2, FY2, FZ2)
    src, dst = V2, U2
    for sweep in range(1, 4):

        def sweep_row2(i, src=src, dst=dst):
            dst[i] = relaxed(i, src, S2, IN2, faces2, 4)

        rows_loop(1 + sweep, span2 - 1 - sweep, 2, sweep_row2)
        src, dst = dst, src
    coarse = src

    first1 = FRAME // 2
    depth1 = 8
    span1 = V1.shape[0]
    own_rows = pl.ds(first1, depth1)
    wait_copies(states[:6])
    for k in range(FINE_X):
        V1[first1 - FINE_X + k, own_rows] = low[COARSE_X + k]
        V1[span1 - first1 + k, own_rows] = high[COARSE_X + k]

    def add_coarse(x):
        half = coarse[x + COARSE_X - first1 // 2, first1:first1 + depth1]
        PT[x, pl.ds(0, depth1, stride=2), :] = half
        PT[x, pl.ds(1, depth1, stride=2), :] = half

    rows_loop(0, span1 // 2, 2, add_coarse)

    def rim_row(x):
        i = x + first1 - FINE_X
        V1[i, first1 - FINE_X:first1] = R[1, x, 3:3 + FINE_X]
        V1[i, first1 + depth1:first1 + depth1 + FINE_X] = R[3, x, 3:3 + FINE_X]

    rows_loop(0, span1 - 2 * (first1 - FINE_X), 2, rim_row)

    def corrected_row(x):
        add = PT[x]
        V1[2 * x] = V1[2 * x] + add
        V1[2 * x + 1] = V1[2 * x + 1] + add

    rows_loop(0, span1 // 2, 2, corrected_row)
    faces1 = (FX1, FY1, FZ1)

    def sweep_a1(i):
        U1[i] = relaxed(i, V1, F1, IN1, faces1, 2)

    rows_loop(2, span1 - 2, 4, sweep_a1)

    def sweep_b1(i):
        V1[i] = relaxed(i, U1, F1, IN1, faces1, 2)

    rows_loop(3, span1 - 3, 3, sweep_b1)

    span = V.shape[0]
    rows1 = V1.shape[1]
    wait_copies(states[6:])

    def widen(x):
        row = V1[x + first1 - 1]
        P0[x, pl.ds(0, rows1, stride=2), :] = row
        P0[x, pl.ds(1, rows1, stride=2), :] = row

    rows_loop(0, span // 2, 2, widen)

    def corrected0(x):
        add = P0[x]
        V[2 * x] = V[2 * x] + add
        V[2 * x + 1] = V[2 * x + 1] + add

    rows_loop(0, span // 2, 2, corrected0)
    faces = (FX, FY, FZ)

    def sweep_a(i):
        U[i] = relaxed(i, V, F, IN, faces, 1)

    rows_loop(1, span - 1, 2, sweep_a)
    depth = out.shape[1]

    def sweep_b(i):
        out[i - 2] = relaxed(i, U, F, IN, faces, 1)[FRAME:FRAME + depth]

    rows_loop(2, span - 2, 2, sweep_b)


def body(source, alpha, beta):
    f = source[:, 0]
    a = alpha[:, 0]
    b = beta[:, 0]
    count, depth, lanes = f.shape
    groups = lax.axis_size("grp")
    blocks = lax.axis_size("box")
    code = [p ^ (p >> 1) for p in range(blocks)]
    up_perm = [(i, i + 1) for i in range(groups - 1)]
    down_perm = [(i + 1, i) for i in range(groups - 1)]
    even_perm = [(code[p], code[p ^ 1]) for p in range(blocks)]
    odd_perm = [(code[p], code[((p - 1) ^ 1) + 1]) for p in range(1, blocks - 1)]

    def arr(*shape):
        return jax.ShapeDtypeStruct(shape, jnp.float32)

    def vm(*shape):
        return pltpu.VMEM(shape, jnp.float32)

    dma = pltpu.SemaphoreType.DMA
    x_rows = 2 * WIDE_F + WIDE_B
    up, down = pl.pallas_call(
        pack_x_kernel,
        out_shape=[arr(x_rows, depth, lanes)] * 2,
        in_specs=[ANY] * 3,
        out_specs=[ANY] * 2,
        scratch_shapes=[dma((6,))],
        compiler_params=params(),
    )(f, a, b)
    low = lax.ppermute(up, "grp", up_perm)
    high = lax.ppermute(down, "grp", down_perm)

    y_rows = 3 * count + 2 * x_rows
    to_even, to_odd = pl.pallas_call(
        pack_y_kernel,
        out_shape=[arr(y_rows, FRAME, lanes)] * 2,
        in_specs=[ANY] * 5,
        out_specs=[ANY] * 2,
        scratch_shapes=[dma((18,))],
        compiler_params=params(),
    )(f, a, b, low, high)
    from_even = lax.ppermute(to_even, "box", even_perm)
    from_odd = lax.ppermute(to_odd, "box", odd_perm)

    framed = (count + 2 * FRAME, depth + 2 * FRAME, lanes)
    framed1 = (framed[0] // 2, framed[1] // 2, lanes)
    kept = (count + 4, framed[1], lanes)
    count2 = count // 4
    x2_tiles = COARSE_X + FINE_X
    results = pl.pallas_call(
        down_kernel,
        out_shape=[arr(*kept)] * 6 + [arr(*framed1)] * 6
        + [arr(count2, 8, lanes)] + [arr(x2_tiles, 8, lanes)] * 2,
        in_specs=[ANY] * 7,
        out_specs=[ANY] * 6 + [VMEM] * 9,
        scratch_shapes=[vm(*framed)] * 10
        + [vm(framed1[0], framed[1], lanes)] + [vm(*framed1)] * 4
        + [vm(3, count2, framed1[1], lanes), vm(8, 128), dma((15,)), dma((6,))],
        compiler_params=params(),
    )(f, a, b, low, high, from_even, from_odd)
    state0 = results[:6]
    state1 = results[6:12]
    coarse, to_up, to_down = results[12:]

    low2 = lax.ppermute(to_up, "grp", up_perm)
    high2 = lax.ppermute(to_down, "grp", down_perm)
    span = framed1[0] - 2 * (FRAME // 2 - FINE_X)
    even2, odd2 = pl.pallas_call(
        pack_coarse_kernel,
        out_shape=[arr(span, 8, lanes)] * 2,
        in_specs=[VMEM] * 4,
        out_specs=[VMEM] * 2,
        compiler_params=params(),
    )(coarse, state1[0], low2, high2)
    near_even = lax.ppermute(even2, "box", even_perm)
    near_odd = lax.ppermute(odd2, "box", odd_perm)
    far_odd = lax.ppermute(near_even, "box", odd_perm)
    far_even = lax.ppermute(near_odd, "box", even_perm)

    framed2 = (count2 + 2 * COARSE_X, depth // 4 + 2 * COARSE_X, lanes)
    out = pl.pallas_call(
        up_kernel,
        out_shape=arr(count, depth, lanes),
        in_specs=[ANY] * 5 + [VMEM] * 2 + [ANY] * 12,
        out_specs=VMEM,
        scratch_shapes=[vm(*kept)] * 7 + [vm(*framed1)] * 7
        + [vm(5, span, 8, lanes)] + [vm(*framed2)] * 9
        + [vm(framed1[0] // 2, framed1[1], lanes), vm(kept[0] // 2, kept[1], lanes)]
        + [dma((5,)), dma((12,))],
        compiler_params=params(),
    )(even2, near_even, near_odd, far_even, far_odd, low2, high2, *state0, *state1)
    return out[:, None]


def solution(mesh):
    spec = P("grp", "box", None, None)
    return jax.shard_map(body, mesh=mesh, in_specs=(spec,) * 3, out_specs=spec, check_vma=False)
```

```python
import functools

import jax
import jax.numpy as jnp
from jax import lax
from jax.experimental import pallas as pl
from jax.experimental.pallas import tpu as pltpu
from jax.sharding import PartitionSpec as P

OMEGA = 0.7
FRAME = 8
WIDE_F = 6
WIDE_B = 7
COARSE_X = 6
FINE_X = 3
LANES = 128
ANY = pl.BlockSpec(memory_space=pl.ANY)
VMEM = pl.BlockSpec(memory_space=pltpu.VMEM)
LIMIT = 16 * 1024 * 1024


def params():
    return pltpu.CompilerParams(vmem_limit_bytes=LIMIT)


def gray_position(code, bit_count):
    position = code
    for shift in range(1, bit_count):
        position = position ^ (code >> shift)
    return position


def box_parity():
    bit_count = lax.axis_size("box").bit_length() - 1
    return gray_position(lax.axis_index("box"), bit_count) & 1


def run_copies(pairs, sems):
    copies = [pltpu.make_async_copy(src, dst, sems.at[at]) for at, (src, dst) in enumerate(pairs)]
    for copy in copies:
        copy.start()
    return copies


def wait_copies(copies):
    for copy in copies:
        copy.wait()


def lane_ids(shape):
    return lax.broadcasted_iota(jnp.int32, shape, 1)


def y_next(row):
    return pltpu.roll(row, row.shape[0] - 1, 0)


def y_prev(row):
    return pltpu.roll(row, 1, 0)


def z_next(row, dist):
    return pltpu.roll(row, LANES - dist, 1)


def z_prev(row, dist):
    return pltpu.roll(row, dist, 1)


def coefficients(alpha, beta, beta_prev, beta_next, dist, scale):
    half = 0.5 * scale
    lane = lane_ids(beta.shape)
    inside = lane < LANES - dist
    up_z = jnp.where(inside, z_next(beta, dist), 0.0)
    down_z = jnp.where(lane >= dist, z_prev(beta, dist), 0.0)
    up_y = y_next(beta)
    face_x = half * (beta + beta_next)
    face_y = half * (beta + up_y)
    face_z = jnp.where(inside, half * (beta + up_z), 0.0)
    total = (beta_prev + beta_next) + (up_y + y_prev(beta)) + (up_z + down_z)
    diagonal = alpha + half * (6.0 * beta + total)
    inverse = jnp.where(alpha > 0.0, OMEGA / diagonal, 0.0)
    return face_x, face_y, face_z, diagonal, inverse


def off_sum(at, v, faces, dist):
    face_x, face_y, face_z = faces
    here = v[at]
    fy = face_y[at]
    fz = face_z[at]
    along_x = face_x[at] * v[at + 1] + face_x[at - 1] * v[at - 1]
    along_y = fy * y_next(here) + y_prev(fy * here)
    along_z = fz * z_next(here, dist) + z_prev(fz * here, dist)
    return here, along_x + along_y + along_z


def relaxed(at, v, f, inverse, faces, dist):
    here, off = off_sum(at, v, faces, dist)
    return (1.0 - OMEGA) * here + inverse[at] * (f[at] + off)


def rows_loop(low, high, step, fn):
    trips = (high - low) // step

    def run(rows):
        stores = [item for row in rows for item in fn(row)]
        for ref, at, value in stores:
            ref[at] = value

    def trip(t, carry):
        base = low + t * step
        run([base + k for k in range(step)])
        return carry

    lax.fori_loop(0, trips, trip, 0)
    rest = list(range(low + trips * step, high))
    if rest:
        run(rest)


def pair_sum_z(row, dist):
    lane = lane_ids(row.shape)
    first = (lane // dist) % 2 == 0
    return row + jnp.where(first, z_next(row, dist), z_prev(row, dist))


def strided_pair(ref, at, count):
    return ref[at, pl.ds(0, count, stride=2), :] + ref[at, pl.ds(1, count, stride=2), :]


def pack_x_kernel(f, a, b, up, down, sems):
    count = f.shape[0]
    pairs = []
    row = 0
    for ref, wide in ((f, WIDE_F), (a, WIDE_F), (b, WIDE_B)):
        pairs.append((ref.at[pl.ds(count - wide, wide)], up.at[pl.ds(row, wide)]))
        pairs.append((ref.at[pl.ds(0, wide)], down.at[pl.ds(row, wide)]))
        row += wide
    wait_copies(run_copies(pairs, sems))


def pack_y_kernel(f, a, b, low, high, to_even, to_odd, sems):
    count = f.shape[0]
    parity = box_parity()
    pairs = []
    for out, start in ((to_even, FRAME * (1 - parity)), (to_odd, FRAME * parity)):
        rows = pl.ds(pl.multiple_of(start, FRAME), FRAME)
        row = 0
        got = 0
        for ref, wide in ((f, WIDE_F), (a, WIDE_F), (b, WIDE_B)):
            pairs.append((low.at[pl.ds(got, wide), rows], out.at[pl.ds(row, wide)]))
            pairs.append((ref.at[:, rows], out.at[pl.ds(row + wide, count)]))
            pairs.append((high.at[pl.ds(got, wide), rows], out.at[pl.ds(row + wide + count, wide)]))
            row += count + 2 * wide
            got += wide
    wait_copies(run_copies(pairs, sems))


def down_kernel(
    f, a, b, low, high, from_even, from_odd,
    out_v, out_f, out_inv, out_fx, out_fy, out_fz,
    out_v1, out_f1, out_inv1, out_fx1, out_fy1, out_fz1,
    out_coarse, to_up, to_down,
    F, A, B, FX, FY, FZ, DG, IN, V, U,
    T, A1, B1, D1, W1, T1, T2, sems, out_sems,
):
    count = f.shape[0]
    depth = f.shape[1]
    parity = box_parity()
    own_y = pl.ds(FRAME, depth)
    even_y = pl.ds(pl.multiple_of((FRAME + depth) * (1 - parity), FRAME), FRAME)
    odd_y = pl.ds(pl.multiple_of((FRAME + depth) * parity, FRAME), FRAME)
    pairs = []
    row = 0
    got = 0
    for ref, wide, dst in ((f, WIDE_F, F), (a, WIDE_F, A), (b, WIDE_B, B)):
        span = count + 2 * wide
        pairs.append((ref, dst.at[pl.ds(FRAME, count), own_y]))
        pairs.append((low.at[pl.ds(got, wide)], dst.at[pl.ds(FRAME - wide, wide), own_y]))
        pairs.append((high.at[pl.ds(got, wide)], dst.at[pl.ds(FRAME + count, wide), own_y]))
        for src, rows in ((from_even, even_y), (from_odd, odd_y)):
            pairs.append((src.at[pl.ds(row, span)], dst.at[pl.ds(FRAME - wide, span), rows]))
        row += span
        got += wide
    wait_copies(run_copies(pairs, sems))

    faces = (FX, FY, FZ)
    end = count + 2 * FRAME

    FX[1] = 0.5 * (B[1] + B[2])

    def coef_row(i):
        fx, fy, fz, dg, inv = coefficients(A[i], B[i], B[i - 1], B[i + 1], 1, 1.0)
        return [(FX, i, fx), (FY, i, fy), (FZ, i, fz), (DG, i, dg), (IN, i, inv), (V, i, inv * F[i])]

    rows_loop(2, end - 2, 11, coef_row)

    kept = pl.ds(FRAME - 2, count + 4)
    outs = [(F, out_f), (IN, out_inv), (FX, out_fx), (FY, out_fy), (FZ, out_fz)]
    out_copies = run_copies([(src.at[kept], dst) for src, dst in outs], out_sems)

    def sweep_row(i):
        return [(U, i, relaxed(i, V, F, IN, faces, 1))]

    rows_loop(3, end - 3, 14, sweep_row)
    last = pltpu.make_async_copy(U.at[kept], out_v, out_sems.at[5])
    last.start()
    out_copies.append(last)

    def residual(i):
        here, off = off_sum(i, U, faces, 1)
        return F[i] - DG[i] * here + off

    half_rows = (depth + 2 * FRAME) // 2

    def restrict_row(j):
        return [(T, j, residual(2 * j) + residual(2 * j + 1))]

    rows_loop(2, end // 2 - 2, 5, restrict_row)

    def level1_source(j):
        return [(out_f1, j, 0.125 * pair_sum_z(strided_pair(T, j, half_rows), 1))]

    rows_loop(2, end // 2 - 2, 10, level1_source)

    def level1_coef(j):
        stores = []
        for src, dst in ((A, A1), (B, B1)):
            both = strided_pair(src, 2 * j, half_rows) + strided_pair(src, 2 * j + 1, half_rows)
            stores.append((dst, j, 0.125 * pair_sum_z(both, 1)))
        return stores

    rows_loop(1, end // 2 - 1, 11, level1_coef)

    faces1 = (out_fx1, out_fy1, out_fz1)
    end1 = end // 2
    out_fx1[1] = 0.125 * (B1[1] + B1[2])

    def coef_row1(i):
        fx, fy, fz, dg, inv = coefficients(A1[i], B1[i], B1[i - 1], B1[i + 1], 2, 0.25)
        return [
            (out_fx1, i, fx), (out_fy1, i, fy), (out_fz1, i, fz),
            (D1, i, dg), (out_inv1, i, inv), (W1, i, inv * out_f1[i]),
        ]

    rows_loop(2, end1 - 2, 10, coef_row1)

    def sweep_row1(i):
        return [(out_v1, i, relaxed(i, W1, out_f1, out_inv1, faces1, 2))]

    rows_loop(3, end1 - 3, 18, sweep_row1)

    def residual1(i):
        here, off = off_sum(i, out_v1, faces1, 2)
        return out_f1[i] - D1[i] * here + off

    first1 = FRAME // 2
    count1 = count // 2
    count2 = count // 4
    quarter_rows = half_rows // 2
    lane = lane_ids((1, LANES))

    def coarse_row(x):
        i = first1 + 2 * x
        return [
            (T1, (0, x), residual1(i) + residual1(i + 1)),
            (T1, (1, x), A1[i] + A1[i + 1]),
            (T1, (2, x), B1[i] + B1[i + 1]),
        ]

    rows_loop(0, count2, 8, coarse_row)
    own2 = FRAME // 4
    depth2 = depth // 4

    def coarse_pack(x):
        stores = []
        for k in range(3):
            both = T1[k, x, pl.ds(0, quarter_rows, stride=2), :] + T1[k, x, pl.ds(1, quarter_rows, stride=2), :]
            value = 0.125 * pair_sum_z(both, 2)
            packed = jnp.zeros((1, LANES), jnp.float32)
            for y in range(depth2):
                packed = packed + jnp.where(lane % depth2 == y, value[own2 + y:own2 + y + 1], 0.0)
            stores.append((out_coarse, (x, slice(k, k + 1)), packed))
        return stores

    rows_loop(0, count2, 8, coarse_pack)

    own1 = slice(first1, first1 + depth // 2)
    for k in range(COARSE_X):
        to_up[k, 0:3] = out_coarse[count2 - COARSE_X + k, 0:3]
        to_down[k, 0:3] = out_coarse[k, 0:3]
    for k in range(FINE_X):
        to_up[COARSE_X + k] = out_v1[first1 + count1 - FINE_X + k, own1]
        to_down[COARSE_X + k] = out_v1[first1 + k, own1]
    wait_copies(out_copies)


def pack_coarse_kernel(coarse, v1, low, high, to_even, to_odd):
    parity = box_parity()
    count2 = coarse.shape[0]
    first1 = FRAME // 2
    depth1 = 8
    count1 = 2 * count2
    for out, top in ((to_even, parity == 0), (to_odd, parity == 1)):
        for k in range(COARSE_X):
            out[k, 0:3] = low[k, 0:3]
            out[COARSE_X + count2 + k, 0:3] = high[k, 0:3]
        for k in range(count2):
            out[COARSE_X + k, 0:3] = coarse[k, 0:3]

        def facing(tile):
            return jnp.where(top, tile[depth1 - FINE_X:], tile[:FINE_X])

        for k in range(FINE_X):
            out[k, 3:3 + FINE_X] = facing(low[COARSE_X + k])
            out[FINE_X + count1 + k, 3:3 + FINE_X] = facing(high[COARSE_X + k])
        for k in range(count1):
            out[FINE_X + k, 3:3 + FINE_X] = facing(v1[first1 + k, first1:first1 + depth1])


def up_kernel(
    own, near_even, near_odd, far_even, far_odd, low, high,
    in_v, F, IN, FX, FY, FZ,
    in_v1, F1, IN1, FX1, FY1, FZ1,
    out,
    V, U, V1, U1,
    R, S2, A2, B2, FX2, FY2, FZ2, IN2, V2, U2, PT, P0,
    sems,
):
    parity = box_parity()
    below = 1 + 2 * (1 - parity)
    copies = run_copies(
        [
            (own, R.at[2]),
            (near_even, R.at[below]),
            (near_odd, R.at[4 - below]),
            (far_even, R.at[4 * (1 - parity)]),
            (far_odd, R.at[4 * parity]),
        ],
        sems,
    )
    wait_copies(copies)

    rows2 = B2.shape[1]
    span2 = B2.shape[0]
    sub = lax.broadcasted_iota(jnp.int32, (rows2, LANES), 0)
    lane = lane_ids((rows2, LANES))
    block = (sub + 2) // 4
    mine = lane % 4 == (sub + 2) % 4
    last_of_four = lane % 4 == 3

    def unpack_row(x):
        stores = []
        for k, dst in enumerate((S2, A2, B2)):
            packed = jnp.broadcast_to(R[0, x, k:k + 1], (rows2, LANES))
            for slot in range(1, 5):
                packed = jnp.where(block == slot, jnp.broadcast_to(R[slot, x, k:k + 1], (rows2, LANES)), packed)
            t = jnp.where(mine, packed, 0.0)
            t = t + z_prev(t, 1)
            t = t + z_prev(t, 2)
            t = jnp.where(last_of_four, t, 0.0)
            t = t + z_next(t, 1)
            stores.append((dst, x, t + z_next(t, 2)))
        return stores

    rows_loop(0, span2, 5, unpack_row)
    FX2[0] = 0.5 * 0.0625 * (B2[0] + B2[1])

    def coef_row2(i):
        fx, fy, fz, dg, inv = coefficients(A2[i], B2[i], B2[i - 1], B2[i + 1], 4, 0.0625)
        return [(FX2, i, fx), (FY2, i, fy), (FZ2, i, fz), (IN2, i, inv), (V2, i, inv * S2[i])]

    rows_loop(1, span2 - 1, 9, coef_row2)
    faces2 = (FX2, FY2, FZ2)
    src, dst = V2, U2
    for sweep in range(1, 4):

        def sweep_row2(i, src=src, dst=dst):
            return [(dst, i, relaxed(i, src, S2, IN2, faces2, 4))]

        rows_loop(1 + sweep, span2 - 1 - sweep, 9 - sweep, sweep_row2)
        src, dst = dst, src
    coarse = src

    first1 = FRAME // 2
    depth1 = 8
    span1 = V1.shape[0]
    own_rows = pl.ds(first1, depth1)

    def own_row(x):
        i = first1 + x
        return [(V1, (i, own_rows), in_v1[i, own_rows])]

    rows_loop(0, span1 - 2 * first1, 16, own_row)
    for k in range(FINE_X):
        V1[first1 - FINE_X + k, own_rows] = low[COARSE_X + k]
        V1[span1 - first1 + k, own_rows] = high[COARSE_X + k]

    def add_coarse(x):
        half = coarse[x + COARSE_X - first1 // 2, first1:first1 + depth1]
        return [(PT, (x, pl.ds(k, depth1, stride=2)), half) for k in range(2)]

    rows_loop(0, span1 // 2, 12, add_coarse)

    def rim_row(x):
        i = x + first1 - FINE_X
        return [
            (V1, (i, slice(first1 - FINE_X, first1)), R[1, x, 3:3 + FINE_X]),
            (V1, (i, slice(first1 + depth1, first1 + depth1 + FINE_X)), R[3, x, 3:3 + FINE_X]),
        ]

    rows_loop(0, span1 - 2 * (first1 - FINE_X), 22, rim_row)

    def corrected_row(x):
        add = PT[x]
        return [(V1, 2 * x + k, V1[2 * x + k] + add) for k in range(2)]

    rows_loop(0, span1 // 2, 12, corrected_row)
    faces1 = (FX1, FY1, FZ1)

    def sweep_a1(i):
        return [(U1, i, relaxed(i, V1, F1, IN1, faces1, 2))]

    rows_loop(2, span1 - 2, 10, sweep_a1)

    def sweep_b1(i):
        return [(V1, i, relaxed(i, U1, F1, IN1, faces1, 2))]

    rows_loop(3, span1 - 3, 18, sweep_b1)

    span = V.shape[0]
    rows1 = V1.shape[1]

    def widen(x):
        row = V1[x + first1 - 1]
        return [(P0, (x, pl.ds(k, rows1, stride=2)), row) for k in range(2)]

    rows_loop(0, span // 2, 18, widen)

    def corrected0(x):
        add = P0[x]
        return [(V, 2 * x + k, in_v[2 * x + k] + add) for k in range(2)]

    rows_loop(0, span // 2, 9, corrected0)
    faces = (FX, FY, FZ)

    def sweep_a(i):
        return [(U, i, relaxed(i, V, F, IN, faces, 1))]

    rows_loop(1, span - 1, 17, sweep_a)
    depth = out.shape[1]

    def sweep_b(i):
        return [(out, i - 2, relaxed(i, U, F, IN, faces, 1)[FRAME:FRAME + depth])]

    rows_loop(2, span - 2, 16, sweep_b)


def body(source, alpha, beta):
    f = source[:, 0]
    a = alpha[:, 0]
    b = beta[:, 0]
    count, depth, lanes = f.shape
    groups = lax.axis_size("grp")
    blocks = lax.axis_size("box")
    code = [p ^ (p >> 1) for p in range(blocks)]
    up_perm = [(i, i + 1) for i in range(groups - 1)]
    down_perm = [(i + 1, i) for i in range(groups - 1)]
    even_perm = [(code[p], code[p ^ 1]) for p in range(blocks)]
    odd_perm = [(code[p], code[((p - 1) ^ 1) + 1]) for p in range(1, blocks - 1)]

    def arr(*shape):
        return jax.ShapeDtypeStruct(shape, jnp.float32)

    def vm(*shape):
        return pltpu.VMEM(shape, jnp.float32)

    dma = pltpu.SemaphoreType.DMA
    x_rows = 2 * WIDE_F + WIDE_B
    up, down = pl.pallas_call(
        pack_x_kernel,
        out_shape=[arr(x_rows, depth, lanes)] * 2,
        in_specs=[ANY] * 3,
        out_specs=[VMEM] * 2,
        scratch_shapes=[dma((6,))],
        compiler_params=params(),
    )(f, a, b)
    low = lax.ppermute(up, "grp", up_perm)
    high = lax.ppermute(down, "grp", down_perm)

    y_rows = 3 * count + 2 * x_rows
    to_even, to_odd = pl.pallas_call(
        pack_y_kernel,
        out_shape=[arr(y_rows, FRAME, lanes)] * 2,
        in_specs=[ANY] * 5,
        out_specs=[VMEM] * 2,
        scratch_shapes=[dma((18,))],
        compiler_params=params(),
    )(f, a, b, low, high)
    from_even = lax.ppermute(to_even, "box", even_perm)
    from_odd = lax.ppermute(to_odd, "box", odd_perm)

    framed = (count + 2 * FRAME, depth + 2 * FRAME, lanes)
    framed1 = (framed[0] // 2, framed[1] // 2, lanes)
    kept = (count + 4, framed[1], lanes)
    count2 = count // 4
    x2_tiles = COARSE_X + FINE_X
    results = pl.pallas_call(
        down_kernel,
        out_shape=[arr(*kept)] * 6 + [arr(*framed1)] * 6
        + [arr(count2, 8, lanes)] + [arr(x2_tiles, 8, lanes)] * 2,
        in_specs=[ANY] * 7,
        out_specs=[ANY] * 6 + [VMEM] * 9,
        scratch_shapes=[vm(*framed)] * 10
        + [vm(framed1[0], framed[1], lanes)] + [vm(*framed1)] * 4
        + [vm(3, count2, framed1[1], lanes), vm(8, 128), dma((15,)), dma((6,))],
        compiler_params=params(),
    )(f, a, b, low, high, from_even, from_odd)
    state0 = results[:6]
    state1 = results[6:12]
    coarse, to_up, to_down = results[12:]

    low2 = lax.ppermute(to_up, "grp", up_perm)
    high2 = lax.ppermute(to_down, "grp", down_perm)
    span = framed1[0] - 2 * (FRAME // 2 - FINE_X)
    even2, odd2 = pl.pallas_call(
        pack_coarse_kernel,
        out_shape=[arr(span, 8, lanes)] * 2,
        in_specs=[VMEM] * 4,
        out_specs=[VMEM] * 2,
        compiler_params=params(),
    )(coarse, state1[0], low2, high2)
    near_even = lax.ppermute(even2, "box", even_perm)
    near_odd = lax.ppermute(odd2, "box", odd_perm)
    far_odd = lax.ppermute(near_even, "box", odd_perm)
    far_even = lax.ppermute(near_odd, "box", even_perm)

    framed2 = (count2 + 2 * COARSE_X, depth // 4 + 2 * COARSE_X, lanes)
    out = pl.pallas_call(
        up_kernel,
        out_shape=arr(count, depth, lanes),
        in_specs=[ANY] * 5 + [VMEM] * 14,
        out_specs=VMEM,
        scratch_shapes=[vm(*kept)] * 2 + [vm(*framed1)] * 2
        + [vm(5, span, 8, lanes)] + [vm(*framed2)] * 9
        + [vm(framed1[0] // 2, framed1[1], lanes), vm(kept[0] // 2, kept[1], lanes)]
        + [dma((5,))],
        compiler_params=params(),
    )(even2, near_even, near_odd, far_even, far_odd, low2, high2, *state0, *state1)
    return out[:, None]


def solution(mesh):
    spec = P("grp", "box", None, None)
    return jax.shard_map(body, mesh=mesh, in_specs=(spec,) * 3, out_specs=spec, check_vma=False)
```

```python
import jax
import jax.numpy as jnp
from jax import lax
from jax.experimental import pallas as pl
from jax.experimental.pallas import tpu as pltpu
from jax.sharding import PartitionSpec as P

OMEGA = 0.7
FRAME = 8
WIDE_F = 6
WIDE_B = 7
COARSE_X = 6
FINE_X = 3
LANES = 128
ANY = pl.BlockSpec(memory_space=pl.ANY)
HBM = pl.BlockSpec(memory_space=pltpu.HBM)
VMEM = pl.BlockSpec(memory_space=pltpu.VMEM)
LIMIT = 16 * 1024 * 1024


def params():
    return pltpu.CompilerParams(vmem_limit_bytes=LIMIT)


def gray_position(code, bit_count):
    position = code
    for shift in range(1, bit_count):
        position = position ^ (code >> shift)
    return position


def box_position():
    bit_count = lax.axis_size("box").bit_length() - 1
    return gray_position(lax.axis_index("box"), bit_count)


def run_copies(pairs, sems):
    copies = [pltpu.make_async_copy(src, dst, sems.at[at]) for at, (src, dst) in enumerate(pairs)]
    for copy in copies:
        copy.start()
    return copies


def wait_copies(copies):
    for copy in copies:
        copy.wait()


def lane_ids(shape):
    return lax.broadcasted_iota(jnp.int32, shape, 1)


def y_next(row):
    return pltpu.roll(row, row.shape[0] - 1, 0)


def y_prev(row):
    return pltpu.roll(row, 1, 0)


def z_next(row, dist):
    return pltpu.roll(row, LANES - dist, 1)


def z_prev(row, dist):
    return pltpu.roll(row, dist, 1)


def coefficients(alpha, beta, beta_prev, beta_next, dist, scale):
    half = 0.5 * scale
    lane = lane_ids(beta.shape)
    inside = lane < LANES - dist
    up_z = jnp.where(inside, z_next(beta, dist), 0.0)
    down_z = jnp.where(lane >= dist, z_prev(beta, dist), 0.0)
    up_y = y_next(beta)
    face_x = half * (beta + beta_next)
    face_y = half * (beta + up_y)
    face_z = jnp.where(inside, half * (beta + up_z), 0.0)
    total = (beta_prev + beta_next) + (up_y + y_prev(beta)) + (up_z + down_z)
    diagonal = alpha + half * (6.0 * beta + total)
    inverse = jnp.where(alpha > 0.0, OMEGA / diagonal, 0.0)
    return face_x, face_y, face_z, diagonal, inverse


def off_sum(at, v, faces, dist):
    face_x, face_y, face_z = faces
    here = v[at]
    fy = face_y[at]
    fz = face_z[at]
    along_x = face_x[at] * v[at + 1] + face_x[at - 1] * v[at - 1]
    along_y = fy * y_next(here) + y_prev(fy * here)
    along_z = fz * z_next(here, dist) + z_prev(fz * here, dist)
    return here, along_x + along_y + along_z


def relaxed(at, v, f, inverse, faces, dist):
    here, off = off_sum(at, v, faces, dist)
    return (1.0 - OMEGA) * here + inverse[at] * (f[at] + off)


def rows_loop(low, high, step, fn):
    trips = (high - low) // step

    def run(rows):
        stores = [item for row in rows for item in fn(row)]
        for ref, at, value in stores:
            ref[at] = value

    def trip(t, carry):
        base = low + t * step
        run([base + k for k in range(step)])
        return carry

    lax.fori_loop(0, trips, trip, 0)
    rest = list(range(low + trips * step, high))
    if rest:
        run(rest)


def pair_sum_z(row, dist):
    lane = lane_ids(row.shape)
    first = (lane // dist) % 2 == 0
    return row + jnp.where(first, z_next(row, dist), z_prev(row, dist))


def strided_pair(ref, at, count):
    return ref[at, pl.ds(0, count, stride=2), :] + ref[at, pl.ds(1, count, stride=2), :]


def zero(ref, *at):
    ref[at] = jnp.zeros_like(ref[at])


def pack_faces_kernel(f, a, b, x_up, x_down, y_up, y_down, sems):
    count, depth = f.shape[:2]
    pairs = []
    row = 0
    for k, (ref, wide) in enumerate(((f, WIDE_F), (a, WIDE_F), (b, WIDE_B))):
        pairs.append((ref.at[pl.ds(count - wide, wide)], x_up.at[pl.ds(row, wide)]))
        pairs.append((ref.at[pl.ds(0, wide)], x_down.at[pl.ds(row, wide)]))
        pairs.append((ref.at[:, pl.ds(depth - FRAME, FRAME)], y_up.at[pl.ds(k * count, count)]))
        pairs.append((ref.at[:, pl.ds(0, FRAME)], y_down.at[pl.ds(k * count, count)]))
        row += wide
    wait_copies(run_copies(pairs, sems))


def pack_corners_kernel(low, high, up, down, sems):
    rows, depth = low.shape[:2]
    pairs = []
    for k, ref in enumerate((low, high)):
        pairs.append((ref.at[:, pl.ds(depth - FRAME, FRAME)], up.at[pl.ds(k * rows, rows)]))
        pairs.append((ref.at[:, pl.ds(0, FRAME)], down.at[pl.ds(k * rows, rows)]))
    wait_copies(run_copies(pairs, sems))


def down_kernel(
    f, a, b, low, high, y_low, y_high, c_low, c_high,
    out_v, out_f, out_inv, out_fx, out_fy, out_fz,
    out_v1, out_f1, out_inv1, out_fx1, out_fy1, out_fz1,
    out_coarse, to_up, to_down,
    F, A, B, FX, FY, FZ, DG, IN, V, U,
    T, A1, B1, D1, W1, T1, T2, sems, out_sems,
):
    count = f.shape[0]
    depth = f.shape[1]
    own_y = pl.ds(FRAME, depth)
    low_y = pl.ds(0, FRAME)
    high_y = pl.ds(FRAME + depth, FRAME)
    own_x = pl.ds(FRAME, count)
    x_rows = low.shape[0]
    pairs = []
    got = 0
    for k, (ref, wide, dst) in enumerate(((f, WIDE_F, F), (a, WIDE_F, A), (b, WIDE_B, B))):
        layers = pl.ds(got, wide)
        layers_too = pl.ds(x_rows + got, wide)
        low_x = pl.ds(FRAME - wide, wide)
        high_x = pl.ds(FRAME + count, wide)
        block = pl.ds(k * count, count)
        pairs += [
            (ref, dst.at[own_x, own_y]),
            (low.at[layers], dst.at[low_x, own_y]),
            (high.at[layers], dst.at[high_x, own_y]),
            (y_low.at[block], dst.at[own_x, low_y]),
            (y_high.at[block], dst.at[own_x, high_y]),
            (c_low.at[layers], dst.at[low_x, low_y]),
            (c_low.at[layers_too], dst.at[high_x, low_y]),
            (c_high.at[layers], dst.at[low_x, high_y]),
            (c_high.at[layers_too], dst.at[high_x, high_y]),
        ]
        got += wide
    wait_copies(run_copies(pairs, sems))

    group = lax.axis_index("grp")
    position = box_position()
    for edge, x, y in (
        (group == 0, slice(0, FRAME), slice(None)),
        (group == lax.axis_size("grp") - 1, slice(FRAME + count, None), slice(None)),
        (position == 0, slice(None), slice(0, FRAME)),
        (position == lax.axis_size("box") - 1, slice(None), slice(FRAME + depth, None)),
    ):

        @pl.when(edge)
        def _(x=x, y=y):
            for ref in (F, A, B):
                zero(ref, x, y)

    faces = (FX, FY, FZ)
    end = count + 2 * FRAME

    FX[1] = 0.5 * (B[1] + B[2])

    def coef_row(i):
        fx, fy, fz, dg, inv = coefficients(A[i], B[i], B[i - 1], B[i + 1], 1, 1.0)
        return [(FX, i, fx), (FY, i, fy), (FZ, i, fz), (DG, i, dg), (IN, i, inv), (V, i, inv * F[i])]

    rows_loop(2, end - 2, 11, coef_row)

    kept = pl.ds(FRAME - 2, count + 4)
    outs = [(F, out_f), (IN, out_inv), (FX, out_fx), (FY, out_fy), (FZ, out_fz)]
    out_copies = run_copies([(src.at[kept], dst) for src, dst in outs], out_sems)

    def sweep_row(i):
        return [(U, i, relaxed(i, V, F, IN, faces, 1))]

    rows_loop(3, end - 3, 14, sweep_row)
    last = pltpu.make_async_copy(U.at[kept], out_v, out_sems.at[5])
    last.start()
    out_copies.append(last)

    def residual(i):
        here, off = off_sum(i, U, faces, 1)
        return F[i] - DG[i] * here + off

    half_rows = (depth + 2 * FRAME) // 2

    def restrict_row(j):
        return [(T, j, residual(2 * j) + residual(2 * j + 1))]

    rows_loop(2, end // 2 - 2, 5, restrict_row)

    def level1_source(j):
        return [(out_f1, j, 0.125 * pair_sum_z(strided_pair(T, j, half_rows), 1))]

    rows_loop(2, end // 2 - 2, 10, level1_source)

    def level1_coef(j):
        stores = []
        for src, dst in ((A, A1), (B, B1)):
            both = strided_pair(src, 2 * j, half_rows) + strided_pair(src, 2 * j + 1, half_rows)
            stores.append((dst, j, 0.125 * pair_sum_z(both, 1)))
        return stores

    rows_loop(1, end // 2 - 1, 11, level1_coef)

    faces1 = (out_fx1, out_fy1, out_fz1)
    end1 = end // 2
    out_fx1[1] = 0.125 * (B1[1] + B1[2])

    def coef_row1(i):
        fx, fy, fz, dg, inv = coefficients(A1[i], B1[i], B1[i - 1], B1[i + 1], 2, 0.25)
        return [
            (out_fx1, i, fx), (out_fy1, i, fy), (out_fz1, i, fz),
            (D1, i, dg), (out_inv1, i, inv), (W1, i, inv * out_f1[i]),
        ]

    rows_loop(2, end1 - 2, 10, coef_row1)

    def sweep_row1(i):
        return [(out_v1, i, relaxed(i, W1, out_f1, out_inv1, faces1, 2))]

    rows_loop(3, end1 - 3, 18, sweep_row1)

    def residual1(i):
        here, off = off_sum(i, out_v1, faces1, 2)
        return out_f1[i] - D1[i] * here + off

    first1 = FRAME // 2
    count1 = count // 2
    count2 = count // 4
    quarter_rows = half_rows // 2
    lane = lane_ids((1, LANES))

    def coarse_row(x):
        i = first1 + 2 * x
        return [
            (T1, (0, x), residual1(i) + residual1(i + 1)),
            (T1, (1, x), A1[i] + A1[i + 1]),
            (T1, (2, x), B1[i] + B1[i + 1]),
        ]

    rows_loop(0, count2, 8, coarse_row)
    own2 = FRAME // 4
    depth2 = depth // 4

    def coarse_pack(x):
        stores = []
        for k in range(3):
            both = T1[k, x, pl.ds(0, quarter_rows, stride=2), :] + T1[k, x, pl.ds(1, quarter_rows, stride=2), :]
            value = 0.125 * pair_sum_z(both, 2)
            packed = jnp.zeros((1, LANES), jnp.float32)
            for y in range(depth2):
                packed = packed + jnp.where(lane % depth2 == y, value[own2 + y:own2 + y + 1], 0.0)
            stores.append((out_coarse, (x, slice(k, k + 1)), packed))
        return stores

    rows_loop(0, count2, 8, coarse_pack)

    own1 = slice(first1, first1 + depth // 2)
    for k in range(COARSE_X):
        to_up[k, 0:3] = out_coarse[count2 - COARSE_X + k, 0:3]
        to_down[k, 0:3] = out_coarse[k, 0:3]
    for k in range(FINE_X):
        to_up[COARSE_X + k] = out_v1[first1 + count1 - FINE_X + k, own1]
        to_down[COARSE_X + k] = out_v1[first1 + k, own1]
    wait_copies(out_copies)


def pack_coarse_kernel(coarse, v1, low, high, up, down):
    count2 = coarse.shape[0]
    first1 = FRAME // 2
    depth1 = 8
    count1 = 2 * count2
    for out, face in ((up, slice(depth1 - FINE_X, depth1)), (down, slice(0, FINE_X))):
        for k in range(COARSE_X):
            out[k, 0:3] = low[k, 0:3]
            out[COARSE_X + count2 + k, 0:3] = high[k, 0:3]
        for k in range(count2):
            out[COARSE_X + k, 0:3] = coarse[k, 0:3]
        for k in range(FINE_X):
            out[k, 3:3 + FINE_X] = low[COARSE_X + k, face]
            out[FINE_X + count1 + k, 3:3 + FINE_X] = high[COARSE_X + k, face]
        for k in range(count1):
            out[FINE_X + k, 3:3 + FINE_X] = v1[first1 + k, slice(first1 + face.start, first1 + face.stop)]


def up_kernel(
    far_low, near_low, own, near_high, far_high, low, high,
    in_v, F, IN, FX, FY, FZ,
    in_v1, F1, IN1, FX1, FY1, FZ1,
    out,
    V, U, V1, U1,
    R, S2, A2, B2, FX2, FY2, FZ2, IN2, V2, U2, PT, P0,
    sems,
):
    sources = (far_low, near_low, own, near_high, far_high)
    wait_copies(run_copies([(src, R.at[slot]) for slot, src in enumerate(sources)], sems))
    group = lax.axis_index("grp")
    position = box_position()
    groups = lax.axis_size("grp")
    blocks = lax.axis_size("box")
    for edge, at in (
        (position < 2, (0,)),
        (position < 1, (1,)),
        (position >= blocks - 1, (3,)),
        (position >= blocks - 2, (4,)),
        (group == 0, (slice(None), slice(0, FINE_X))),
        (group == 0, (slice(None), slice(FINE_X, COARSE_X), slice(0, 3))),
        (group == groups - 1, (slice(None), slice(R.shape[1] - FINE_X, None))),
        (group == groups - 1, (slice(None), slice(B2.shape[0] - COARSE_X, R.shape[1] - FINE_X), slice(0, 3))),
    ):

        @pl.when(edge)
        def _(at=at):
            zero(R, *at)

    rows2 = B2.shape[1]
    span2 = B2.shape[0]
    sub = lax.broadcasted_iota(jnp.int32, (rows2, LANES), 0)
    lane = lane_ids((rows2, LANES))
    block = (sub + 2) // 4
    mine = lane % 4 == (sub + 2) % 4
    last_of_four = lane % 4 == 3

    def unpack_row(x):
        stores = []
        for k, dst in enumerate((S2, A2, B2)):
            packed = jnp.broadcast_to(R[0, x, k:k + 1], (rows2, LANES))
            for slot in range(1, 5):
                packed = jnp.where(block == slot, jnp.broadcast_to(R[slot, x, k:k + 1], (rows2, LANES)), packed)
            t = jnp.where(mine, packed, 0.0)
            t = t + z_prev(t, 1)
            t = t + z_prev(t, 2)
            t = jnp.where(last_of_four, t, 0.0)
            t = t + z_next(t, 1)
            stores.append((dst, x, t + z_next(t, 2)))
        return stores

    rows_loop(0, span2, 5, unpack_row)
    FX2[0] = 0.5 * 0.0625 * (B2[0] + B2[1])

    def coef_row2(i):
        fx, fy, fz, dg, inv = coefficients(A2[i], B2[i], B2[i - 1], B2[i + 1], 4, 0.0625)
        return [(FX2, i, fx), (FY2, i, fy), (FZ2, i, fz), (IN2, i, inv), (V2, i, inv * S2[i])]

    rows_loop(1, span2 - 1, 9, coef_row2)
    faces2 = (FX2, FY2, FZ2)
    src, dst = V2, U2
    for sweep in range(1, 4):

        def sweep_row2(i, src=src, dst=dst):
            return [(dst, i, relaxed(i, src, S2, IN2, faces2, 4))]

        rows_loop(1 + sweep, span2 - 1 - sweep, 9 - sweep, sweep_row2)
        src, dst = dst, src
    coarse = src

    first1 = FRAME // 2
    depth1 = 8
    span1 = V1.shape[0]
    own_rows = pl.ds(first1, depth1)

    def own_row(x):
        i = first1 + x
        return [(V1, (i, own_rows), in_v1[i, own_rows])]

    rows_loop(0, span1 - 2 * first1, 16, own_row)
    for k in range(FINE_X):
        V1[first1 - FINE_X + k, own_rows] = jnp.where(group > 0, low[COARSE_X + k], 0.0)
        V1[span1 - first1 + k, own_rows] = jnp.where(group < groups - 1, high[COARSE_X + k], 0.0)

    def add_coarse(x):
        half = coarse[x + COARSE_X - first1 // 2, first1:first1 + depth1]
        return [(PT, (x, pl.ds(k, depth1, stride=2)), half) for k in range(2)]

    rows_loop(0, span1 // 2, 12, add_coarse)

    def rim_row(x):
        i = x + first1 - FINE_X
        return [
            (V1, (i, slice(first1 - FINE_X, first1)), R[1, x, 3:3 + FINE_X]),
            (V1, (i, slice(first1 + depth1, first1 + depth1 + FINE_X)), R[3, x, 3:3 + FINE_X]),
        ]

    rows_loop(0, span1 - 2 * (first1 - FINE_X), 22, rim_row)

    def corrected_row(x):
        add = PT[x]
        return [(V1, 2 * x + k, V1[2 * x + k] + add) for k in range(2)]

    rows_loop(0, span1 // 2, 12, corrected_row)
    faces1 = (FX1, FY1, FZ1)

    def sweep_a1(i):
        return [(U1, i, relaxed(i, V1, F1, IN1, faces1, 2))]

    rows_loop(2, span1 - 2, 10, sweep_a1)

    def sweep_b1(i):
        return [(V1, i, relaxed(i, U1, F1, IN1, faces1, 2))]

    rows_loop(3, span1 - 3, 18, sweep_b1)

    span = V.shape[0]
    rows1 = V1.shape[1]

    def widen(x):
        row = V1[x + first1 - 1]
        return [(P0, (x, pl.ds(k, rows1, stride=2)), row) for k in range(2)]

    rows_loop(0, span // 2, 18, widen)

    def corrected0(x):
        add = P0[x]
        return [(V, 2 * x + k, in_v[2 * x + k] + add) for k in range(2)]

    rows_loop(0, span // 2, 9, corrected0)
    faces = (FX, FY, FZ)

    def sweep_a(i):
        return [(U, i, relaxed(i, V, F, IN, faces, 1))]

    rows_loop(1, span - 1, 17, sweep_a)
    depth = out.shape[1]

    def sweep_b(i):
        return [(out, i - 2, relaxed(i, U, F, IN, faces, 1)[FRAME:FRAME + depth])]

    rows_loop(2, span - 2, 16, sweep_b)


def body(source, alpha, beta):
    f = source[:, 0]
    a = alpha[:, 0]
    b = beta[:, 0]
    count, depth, lanes = f.shape
    groups = lax.axis_size("grp")
    blocks = lax.axis_size("box")
    code = [p ^ (p >> 1) for p in range(blocks)]

    def along_x(array, by):
        return lax.ppermute(array, "grp", [(i, (i + by) % groups) for i in range(groups)])

    def along_y(array, by):
        return lax.ppermute(array, "box", [(code[p], code[(p + by) % blocks]) for p in range(blocks)])

    def arr(*shape):
        return jax.ShapeDtypeStruct(shape, jnp.float32)

    def vm(*shape):
        return pltpu.VMEM(shape, jnp.float32)

    dma = pltpu.SemaphoreType.DMA
    x_rows = 2 * WIDE_F + WIDE_B
    faces_out = [arr(x_rows, depth, lanes)] * 2 + [arr(3 * count, FRAME, lanes)] * 2
    x_up, x_down, y_up, y_down = pl.pallas_call(
        pack_faces_kernel,
        out_shape=faces_out,
        in_specs=[HBM] * 3,
        out_specs=[VMEM] * 4,
        scratch_shapes=[dma((12,))],
        compiler_params=params(),
    )(f, a, b)
    low = along_x(x_up, 1)
    high = along_x(x_down, -1)
    y_low = along_y(y_up, 1)
    y_high = along_y(y_down, -1)

    c_up, c_down = pl.pallas_call(
        pack_corners_kernel,
        out_shape=[arr(2 * x_rows, FRAME, lanes)] * 2,
        in_specs=[ANY] * 2,
        out_specs=[VMEM] * 2,
        scratch_shapes=[dma((4,))],
        compiler_params=params(),
    )(low, high)
    c_low = along_y(c_up, 1)
    c_high = along_y(c_down, -1)

    framed = (count + 2 * FRAME, depth + 2 * FRAME, lanes)
    framed1 = (framed[0] // 2, framed[1] // 2, lanes)
    kept = (count + 4, framed[1], lanes)
    count2 = count // 4
    x2_tiles = COARSE_X + FINE_X
    results = pl.pallas_call(
        down_kernel,
        out_shape=[arr(*kept)] * 6 + [arr(*framed1)] * 6
        + [arr(count2, 8, lanes)] + [arr(x2_tiles, 8, lanes)] * 2,
        in_specs=[ANY] * 9,
        out_specs=[ANY] * 6 + [VMEM] * 9,
        scratch_shapes=[vm(*framed)] * 10
        + [vm(framed1[0], framed[1], lanes)] + [vm(*framed1)] * 4
        + [vm(3, count2, framed1[1], lanes), vm(8, 128), dma((27,)), dma((6,))],
        compiler_params=params(),
    )(f, a, b, low, high, y_low, y_high, c_low, c_high)
    state0 = results[:6]
    state1 = results[6:12]
    coarse, to_up, to_down = results[12:]

    low2 = along_x(to_up, 1)
    high2 = along_x(to_down, -1)
    span = framed1[0] - 2 * (FRAME // 2 - FINE_X)
    up2, down2 = pl.pallas_call(
        pack_coarse_kernel,
        out_shape=[arr(span, 8, lanes)] * 2,
        in_specs=[VMEM] * 4,
        out_specs=[VMEM] * 2,
        compiler_params=params(),
    )(coarse, state1[0], low2, high2)
    near_low = along_y(up2, 1)
    near_high = along_y(down2, -1)
    far_low = along_y(up2, 2)
    far_high = along_y(down2, -2)

    framed2 = (count2 + 2 * COARSE_X, depth // 4 + 2 * COARSE_X, lanes)
    out = pl.pallas_call(
        up_kernel,
        out_shape=arr(count, depth, lanes),
        in_specs=[ANY] * 5 + [VMEM] * 14,
        out_specs=VMEM,
        scratch_shapes=[vm(*kept)] * 2 + [vm(*framed1)] * 2
        + [vm(5, span, 8, lanes)] + [vm(*framed2)] * 9
        + [vm(framed1[0] // 2, framed1[1], lanes), vm(kept[0] // 2, kept[1], lanes)]
        + [dma((5,))],
        compiler_params=params(),
    )(far_low, near_low, up2, near_high, far_high, low2, high2, *state0, *state1)
    return out[:, None]


def solution(mesh):
    spec = P("grp", "box", None, None)
    return jax.shard_map(body, mesh=mesh, in_specs=(spec,) * 3, out_specs=spec, check_vma=False)
```

```python
import jax
import jax.numpy as jnp
from jax import lax
from jax.experimental import pallas as pl
from jax.experimental.pallas import tpu as pltpu
from jax.sharding import PartitionSpec as P

OMEGA = 0.7
FRAME = 8
WIDE_F = 6
WIDE_B = 7
COARSE_X = 6
FINE_X = 3
LANES = 128
ANY = pl.BlockSpec(memory_space=pl.ANY)
HBM = pl.BlockSpec(memory_space=pltpu.HBM)
VMEM = pl.BlockSpec(memory_space=pltpu.VMEM)
LIMIT = 16 * 1024 * 1024


def params():
    return pltpu.CompilerParams(vmem_limit_bytes=LIMIT)


def gray_position(code, bit_count):
    position = code
    for shift in range(1, bit_count):
        position = position ^ (code >> shift)
    return position


def box_position():
    bit_count = lax.axis_size("box").bit_length() - 1
    return gray_position(lax.axis_index("box"), bit_count)


def run_copies(pairs, sems):
    copies = [pltpu.make_async_copy(src, dst, sems.at[at]) for at, (src, dst) in enumerate(pairs)]
    for copy in copies:
        copy.start()
    return copies


def wait_copies(copies):
    for copy in copies:
        copy.wait()


def lane_ids(shape):
    return lax.broadcasted_iota(jnp.int32, shape, 1)


def y_next(row):
    return pltpu.roll(row, row.shape[0] - 1, 0)


def y_prev(row):
    return pltpu.roll(row, 1, 0)


def z_next(row, dist):
    return pltpu.roll(row, LANES - dist, 1)


def z_prev(row, dist):
    return pltpu.roll(row, dist, 1)


def coefficients(alpha, beta, beta_prev, beta_next, dist, scale):
    half = 0.5 * scale
    lane = lane_ids(beta.shape)
    inside = lane < LANES - dist
    up_z = jnp.where(inside, z_next(beta, dist), 0.0)
    down_z = jnp.where(lane >= dist, z_prev(beta, dist), 0.0)
    up_y = y_next(beta)
    face_x = half * (beta + beta_next)
    face_y = half * (beta + up_y)
    face_z = jnp.where(inside, half * (beta + up_z), 0.0)
    total = (beta_prev + beta_next) + (up_y + y_prev(beta)) + (up_z + down_z)
    diagonal = alpha + half * (6.0 * beta + total)
    inverse = jnp.where(alpha > 0.0, OMEGA / diagonal, 0.0)
    return face_x, face_y, face_z, diagonal, inverse


def off_sum(at, v, faces, dist):
    face_x, face_y, face_z = faces
    here = v[at]
    fy = face_y[at]
    fz = face_z[at]
    along_x = face_x[at] * v[at + 1] + face_x[at - 1] * v[at - 1]
    along_y = fy * y_next(here) + y_prev(fy * here)
    along_z = fz * z_next(here, dist) + z_prev(fz * here, dist)
    return here, along_x + along_y + along_z


def relaxed(at, v, f, inverse, faces, dist):
    here, off = off_sum(at, v, faces, dist)
    return (1.0 - OMEGA) * here + inverse[at] * (f[at] + off)


def rows_loop(low, high, step, fn):
    trips = (high - low) // step

    def run(rows):
        stores = [item for row in rows for item in fn(row)]
        for ref, at, value in stores:
            ref[at] = value

    def trip(t, carry):
        base = low + t * step
        run([base + k for k in range(step)])
        return carry

    lax.fori_loop(0, trips, trip, 0)
    rest = list(range(low + trips * step, high))
    if rest:
        run(rest)


def pair_sum_z(row, dist):
    lane = lane_ids(row.shape)
    first = (lane // dist) % 2 == 0
    return row + jnp.where(first, z_next(row, dist), z_prev(row, dist))


def strided_pair(ref, at, count):
    return ref[at, pl.ds(0, count, stride=2), :] + ref[at, pl.ds(1, count, stride=2), :]


def zero(ref, *at):
    ref[at] = jnp.zeros_like(ref[at])


def pack_faces_kernel(f, a, b, x_up, x_down, y_up, y_down, sems):
    count, depth = f.shape[:2]
    pairs = []
    row = 0
    for k, (ref, wide) in enumerate(((f, WIDE_F), (a, WIDE_F), (b, WIDE_B))):
        pairs.append((ref.at[pl.ds(count - wide, wide)], x_up.at[pl.ds(row, wide)]))
        pairs.append((ref.at[pl.ds(0, wide)], x_down.at[pl.ds(row, wide)]))
        pairs.append((ref.at[:, pl.ds(depth - FRAME, FRAME)], y_up.at[pl.ds(k * count, count)]))
        pairs.append((ref.at[:, pl.ds(0, FRAME)], y_down.at[pl.ds(k * count, count)]))
        row += wide
    wait_copies(run_copies(pairs, sems))


def pack_corners_kernel(low, high, up, down, sems):
    rows, depth = low.shape[:2]
    pairs = []
    for k, ref in enumerate((low, high)):
        pairs.append((ref.at[:, pl.ds(depth - FRAME, FRAME)], up.at[pl.ds(k * rows, rows)]))
        pairs.append((ref.at[:, pl.ds(0, FRAME)], down.at[pl.ds(k * rows, rows)]))
    wait_copies(run_copies(pairs, sems))


def down_kernel(
    f, a, b, low, high, y_low, y_high, c_low, c_high,
    U, F, IN, FX, FY, FZ,
    out_v1, out_f1, out_inv1, out_fx1, out_fy1, out_fz1,
    out_coarse, to_up, to_down,
    A, B, DG, V, T, A1, B1, D1, W1, T1, sems,
):
    count = f.shape[0]
    depth = f.shape[1]
    own_y = pl.ds(FRAME, depth)
    low_y = pl.ds(0, FRAME)
    high_y = pl.ds(FRAME + depth, FRAME)
    own_x = pl.ds(FRAME, count)
    x_rows = low.shape[0]
    pairs = []
    got = 0
    for k, (ref, wide, dst) in enumerate(((f, WIDE_F, F), (a, WIDE_F, A), (b, WIDE_B, B))):
        layers = pl.ds(got, wide)
        layers_too = pl.ds(x_rows + got, wide)
        low_x = pl.ds(FRAME - wide, wide)
        high_x = pl.ds(FRAME + count, wide)
        block = pl.ds(k * count, count)
        pairs += [
            (ref, dst.at[own_x, own_y]),
            (low.at[layers], dst.at[low_x, own_y]),
            (high.at[layers], dst.at[high_x, own_y]),
            (y_low.at[block], dst.at[own_x, low_y]),
            (y_high.at[block], dst.at[own_x, high_y]),
            (c_low.at[layers], dst.at[low_x, low_y]),
            (c_low.at[layers_too], dst.at[high_x, low_y]),
            (c_high.at[layers], dst.at[low_x, high_y]),
            (c_high.at[layers_too], dst.at[high_x, high_y]),
        ]
        got += wide
    wait_copies(run_copies(pairs, sems))

    group = lax.axis_index("grp")
    position = box_position()
    for edge, x, y in (
        (group == 0, slice(0, FRAME), slice(None)),
        (group == lax.axis_size("grp") - 1, slice(FRAME + count, None), slice(None)),
        (position == 0, slice(None), slice(0, FRAME)),
        (position == lax.axis_size("box") - 1, slice(None), slice(FRAME + depth, None)),
    ):

        @pl.when(edge)
        def _(x=x, y=y):
            for ref in (F, A, B):
                zero(ref, x, y)

    faces = (FX, FY, FZ)
    end = count + 2 * FRAME

    FX[1] = 0.5 * (B[1] + B[2])

    def coef_row(i):
        fx, fy, fz, dg, inv = coefficients(A[i], B[i], B[i - 1], B[i + 1], 1, 1.0)
        return [(FX, i, fx), (FY, i, fy), (FZ, i, fz), (DG, i, dg), (IN, i, inv), (V, i, inv * F[i])]

    rows_loop(2, end - 2, 11, coef_row)

    def sweep_row(i):
        return [(U, i, relaxed(i, V, F, IN, faces, 1))]

    rows_loop(3, end - 3, 14, sweep_row)
    def residual(i):
        here, off = off_sum(i, U, faces, 1)
        return F[i] - DG[i] * here + off

    half_rows = (depth + 2 * FRAME) // 2

    def restrict_row(j):
        return [(T, j, residual(2 * j) + residual(2 * j + 1))]

    rows_loop(2, end // 2 - 2, 5, restrict_row)

    def level1_source(j):
        return [(out_f1, j, 0.125 * pair_sum_z(strided_pair(T, j, half_rows), 1))]

    rows_loop(2, end // 2 - 2, 10, level1_source)

    def level1_coef(j):
        stores = []
        for src, dst in ((A, A1), (B, B1)):
            both = strided_pair(src, 2 * j, half_rows) + strided_pair(src, 2 * j + 1, half_rows)
            stores.append((dst, j, 0.125 * pair_sum_z(both, 1)))
        return stores

    rows_loop(1, end // 2 - 1, 11, level1_coef)

    faces1 = (out_fx1, out_fy1, out_fz1)
    end1 = end // 2
    out_fx1[1] = 0.125 * (B1[1] + B1[2])

    def coef_row1(i):
        fx, fy, fz, dg, inv = coefficients(A1[i], B1[i], B1[i - 1], B1[i + 1], 2, 0.25)
        return [
            (out_fx1, i, fx), (out_fy1, i, fy), (out_fz1, i, fz),
            (D1, i, dg), (out_inv1, i, inv), (W1, i, inv * out_f1[i]),
        ]

    rows_loop(2, end1 - 2, 10, coef_row1)

    def sweep_row1(i):
        return [(out_v1, i, relaxed(i, W1, out_f1, out_inv1, faces1, 2))]

    rows_loop(3, end1 - 3, 18, sweep_row1)

    def residual1(i):
        here, off = off_sum(i, out_v1, faces1, 2)
        return out_f1[i] - D1[i] * here + off

    first1 = FRAME // 2
    count1 = count // 2
    count2 = count // 4
    quarter_rows = half_rows // 2
    lane = lane_ids((1, LANES))

    def coarse_row(x):
        i = first1 + 2 * x
        return [
            (T1, (0, x), residual1(i) + residual1(i + 1)),
            (T1, (1, x), A1[i] + A1[i + 1]),
            (T1, (2, x), B1[i] + B1[i + 1]),
        ]

    rows_loop(0, count2, 8, coarse_row)
    own2 = FRAME // 4
    depth2 = depth // 4

    def coarse_pack(x):
        stores = []
        for k in range(3):
            both = T1[k, x, pl.ds(0, quarter_rows, stride=2), :] + T1[k, x, pl.ds(1, quarter_rows, stride=2), :]
            value = 0.125 * pair_sum_z(both, 2)
            packed = jnp.zeros((1, LANES), jnp.float32)
            for y in range(depth2):
                packed = packed + jnp.where(lane % depth2 == y, value[own2 + y:own2 + y + 1], 0.0)
            stores.append((out_coarse, pl.ds(k * count2 + x, 1), packed))
        return stores

    rows_loop(0, count2, 8, coarse_pack)

    own1 = slice(first1, first1 + depth // 2)
    for k in range(3):
        rows = slice(k * COARSE_X, (k + 1) * COARSE_X)
        to_up[rows] = out_coarse[(k + 1) * count2 - COARSE_X:(k + 1) * count2]
        to_down[rows] = out_coarse[k * count2:k * count2 + COARSE_X]
    for k in range(FINE_X):
        rows = slice(3 * COARSE_X + k * depth // 2, 3 * COARSE_X + (k + 1) * depth // 2)
        to_up[rows] = out_v1[first1 + count1 - FINE_X + k, own1]
        to_down[rows] = out_v1[first1 + k, own1]


def pack_coarse_kernel(coarse, v1, low, high, far, near_up, near_down):
    count2 = coarse.shape[0] // 3
    span2 = count2 + 2 * COARSE_X
    first1 = FRAME // 2
    depth1 = v1.shape[1] - FRAME
    count1 = 2 * count2
    for k in range(3):
        row = k * span2
        part = slice(k * COARSE_X, (k + 1) * COARSE_X)
        far[row:row + COARSE_X] = low[part]
        far[row + COARSE_X:row + COARSE_X + count2] = coarse[k * count2:(k + 1) * count2]
        far[row + COARSE_X + count2:row + span2] = high[part]
    rows = far.shape[0]
    for out, face in ((near_up, depth1 - FINE_X), (near_down, 0)):
        out[0:rows] = far[...]
        row = rows
        for k in range(FINE_X):
            start = 3 * COARSE_X + k * depth1 + face
            out[row:row + FINE_X] = low[start:start + FINE_X]
            last = row + FINE_X * (FINE_X + count1)
            out[last:last + FINE_X] = high[start:start + FINE_X]
            row += FINE_X
        for k in range(count1):
            out[row:row + FINE_X] = v1[first1 + k, first1 + face:first1 + face + FINE_X]
            row += FINE_X


def up_kernel(
    far_low, near_low, own, near_high, far_high, low, high,
    in_v, F, IN, FX, FY, FZ,
    in_v1, F1, IN1, FX1, FY1, FZ1,
    out,
    V, U, V1, U1,
    S2, A2, B2, FX2, FY2, FZ2, IN2, V2, U2, PT, P0,
):
    sources = (far_low, near_low, own, near_high, far_high)
    group = lax.axis_index("grp")
    position = box_position()
    last_group = lax.axis_size("grp") - 1
    last_block = lax.axis_size("box") - 1
    depth = out.shape[1]

    rows2 = B2.shape[1]
    span2 = B2.shape[0]
    sub = lax.broadcasted_iota(jnp.int32, (rows2, LANES), 0)
    lane = lane_ids((rows2, LANES))
    block = (sub + 2) // 4
    cell = position * (depth // 4) + sub - COARSE_X
    inside = (cell >= 0) & (cell < (last_block + 1) * (depth // 4))
    mine = (lane % 4 == (sub + 2) % 4) & inside
    last_of_four = lane % 4 == 3

    def unpack_row(x):
        stores = []
        for k, dst in enumerate((S2, A2, B2)):
            row = pl.ds(k * span2 + x, 1)
            packed = jnp.broadcast_to(sources[0][row], (rows2, LANES))
            for slot in range(1, 5):
                packed = jnp.where(block == slot, jnp.broadcast_to(sources[slot][row], (rows2, LANES)), packed)
            t = jnp.where(mine, packed, 0.0)
            t = t + z_prev(t, 1)
            t = t + z_prev(t, 2)
            t = jnp.where(last_of_four, t, 0.0)
            t = t + z_next(t, 1)
            stores.append((dst, x, t + z_next(t, 2)))
        return stores

    rows_loop(0, span2, 5, unpack_row)
    for edge, rows in ((group == 0, slice(0, COARSE_X)), (group == last_group, slice(span2 - COARSE_X, span2))):

        @pl.when(edge)
        def _(rows=rows):
            zero(A2, rows)
            zero(B2, rows)

    FX2[0] = 0.5 * 0.0625 * (B2[0] + B2[1])

    def coef_row2(i):
        fx, fy, fz, dg, inv = coefficients(A2[i], B2[i], B2[i - 1], B2[i + 1], 4, 0.0625)
        return [(FX2, i, fx), (FY2, i, fy), (FZ2, i, fz), (IN2, i, inv), (V2, i, inv * S2[i])]

    rows_loop(1, span2 - 1, 9, coef_row2)
    faces2 = (FX2, FY2, FZ2)
    src, dst = V2, U2
    for sweep in range(1, 4):

        def sweep_row2(i, src=src, dst=dst):
            return [(dst, i, relaxed(i, src, S2, IN2, faces2, 4))]

        rows_loop(1 + sweep, span2 - 1 - sweep, 9 - sweep, sweep_row2)
        src, dst = dst, src
    coarse = src

    first1 = FRAME // 2
    depth1 = depth // 2
    span1 = V1.shape[0]
    own_rows = pl.ds(first1, depth1)

    def own_row(x):
        i = first1 + x
        return [(V1, (i, own_rows), in_v1[i, own_rows])]

    rows_loop(0, span1 - 2 * first1, 16, own_row)
    for k in range(FINE_X):
        tile = pl.ds(3 * COARSE_X + k * depth1, depth1)
        V1[first1 - FINE_X + k, own_rows] = low[tile]
        V1[span1 - first1 + k, own_rows] = high[tile]

    def add_coarse(x):
        half = coarse[x + COARSE_X - first1 // 2, first1:first1 + depth1]
        return [(PT, (x, pl.ds(k, depth1, stride=2)), half) for k in range(2)]

    rows_loop(0, span1 // 2, 12, add_coarse)

    rim = far_low.shape[0]

    def rim_row(x):
        i = x + first1 - FINE_X
        part = pl.ds(rim + FINE_X * x, FINE_X)
        return [
            (V1, (i, slice(first1 - FINE_X, first1)), jnp.where(position > 0, near_low[part], 0.0)),
            (
                V1,
                (i, slice(first1 + depth1, first1 + depth1 + FINE_X)),
                jnp.where(position < last_block, near_high[part], 0.0),
            ),
        ]

    rows_loop(0, span1 - 2 * (first1 - FINE_X), 22, rim_row)
    for edge, rows in ((group == 0, slice(0, first1)), (group == last_group, slice(span1 - first1, span1))):

        @pl.when(edge)
        def _(rows=rows):
            zero(V1, rows)

    def corrected_row(x):
        add = PT[x]
        return [(V1, 2 * x + k, V1[2 * x + k] + add) for k in range(2)]

    rows_loop(0, span1 // 2, 12, corrected_row)
    faces1 = (FX1, FY1, FZ1)

    def sweep_a1(i):
        return [(U1, i, relaxed(i, V1, F1, IN1, faces1, 2))]

    rows_loop(2, span1 - 2, 10, sweep_a1)

    def sweep_b1(i):
        return [(V1, i, relaxed(i, U1, F1, IN1, faces1, 2))]

    rows_loop(3, span1 - 3, 18, sweep_b1)

    span = V.shape[0]
    rows1 = V1.shape[1]
    start = FRAME - 2

    def widen(x):
        row = V1[x + start // 2]
        return [(P0, (x, pl.ds(k, rows1, stride=2)), row) for k in range(2)]

    rows_loop(0, (span - 2 * start) // 2, 18, widen)

    def corrected0(x):
        add = P0[x]
        i = start + 2 * x
        return [(V, i + k, in_v[i + k] + add) for k in range(2)]

    rows_loop(0, (span - 2 * start) // 2, 9, corrected0)
    faces = (FX, FY, FZ)

    def sweep_a(i):
        return [(U, i, relaxed(i, V, F, IN, faces, 1))]

    rows_loop(start + 1, span - start - 1, 17, sweep_a)

    def sweep_b(i):
        rows = pl.ds(FRAME, depth)
        here = U[i, rows]
        fz = FZ[i, rows]
        along_x = FX[i, rows] * U[i + 1, rows] + FX[i - 1, rows] * U[i - 1, rows]
        before = pl.ds(FRAME - 1, depth)
        along_y = FY[i, rows] * U[i, pl.ds(FRAME + 1, depth)] + FY[i, before] * U[i, before]
        along_z = fz * z_next(here, 1) + z_prev(fz * here, 1)
        off = along_x + along_y + along_z
        return [(out, i - FRAME, (1.0 - OMEGA) * here + IN[i, rows] * (F[i, rows] + off))]

    rows_loop(FRAME, span - FRAME, 16, sweep_b)


def body(source, alpha, beta):
    f = source[:, 0]
    a = alpha[:, 0]
    b = beta[:, 0]
    count, depth, lanes = f.shape
    groups = lax.axis_size("grp")
    blocks = lax.axis_size("box")
    code = [p ^ (p >> 1) for p in range(blocks)]

    def along_x(array, by):
        return lax.ppermute(array, "grp", [(i, (i + by) % groups) for i in range(groups)])

    def along_y(array, by):
        return lax.ppermute(array, "box", [(code[p], code[(p + by) % blocks]) for p in range(blocks)])

    def arr(*shape):
        return jax.ShapeDtypeStruct(shape, jnp.float32)

    def vm(*shape):
        return pltpu.VMEM(shape, jnp.float32)

    dma = pltpu.SemaphoreType.DMA
    x_rows = 2 * WIDE_F + WIDE_B
    faces_out = [arr(x_rows, depth, lanes)] * 2 + [arr(3 * count, FRAME, lanes)] * 2
    x_up, x_down, y_up, y_down = pl.pallas_call(
        pack_faces_kernel,
        out_shape=faces_out,
        in_specs=[HBM] * 3,
        out_specs=[VMEM] * 4,
        scratch_shapes=[dma((12,))],
        compiler_params=params(),
    )(*[pltpu.with_memory_space_constraint(t, pltpu.HBM) for t in (f, a, b)])
    low = along_x(x_up, 1)
    high = along_x(x_down, -1)
    y_low = along_y(y_up, 1)
    y_high = along_y(y_down, -1)

    c_up, c_down = pl.pallas_call(
        pack_corners_kernel,
        out_shape=[arr(2 * x_rows, FRAME, lanes)] * 2,
        in_specs=[ANY] * 2,
        out_specs=[VMEM] * 2,
        scratch_shapes=[dma((4,))],
        compiler_params=params(),
    )(low, high)
    c_low = along_y(c_up, 1)
    c_high = along_y(c_down, -1)

    framed = (count + 2 * FRAME, depth + 2 * FRAME, lanes)
    framed1 = (framed[0] // 2, framed[1] // 2, lanes)
    count2 = count // 4
    x2_rows = 3 * COARSE_X + FINE_X * depth // 2
    x2_rows += -x2_rows % 8
    results = pl.pallas_call(
        down_kernel,
        out_shape=[arr(*framed)] * 6 + [arr(*framed1)] * 6
        + [arr(3 * count2, lanes)] + [arr(x2_rows, lanes)] * 2,
        in_specs=[ANY] * 9,
        out_specs=[VMEM] * 15,
        scratch_shapes=[vm(*framed)] * 4
        + [vm(framed1[0], framed[1], lanes)] + [vm(*framed1)] * 4
        + [vm(3, count2, framed1[1], lanes), dma((27,))],
        compiler_params=params(),
    )(f, a, b, low, high, y_low, y_high, c_low, c_high)
    state0 = results[:6]
    state1 = results[6:12]
    coarse, to_up, to_down = results[12:]

    low2 = along_x(to_up, 1)
    high2 = along_x(to_down, -1)
    far_rows = 3 * (count2 + 2 * COARSE_X)
    far_rows += -far_rows % 8
    near_rows = far_rows + FINE_X * (count // 2 + 2 * FINE_X)
    near_rows += -near_rows % 8
    far, near_up, near_down = pl.pallas_call(
        pack_coarse_kernel,
        out_shape=[arr(far_rows, lanes)] + [arr(near_rows, lanes)] * 2,
        in_specs=[VMEM] * 4,
        out_specs=[VMEM] * 3,
        compiler_params=params(),
    )(coarse, state1[0], low2, high2)
    near_low = along_y(near_up, 1)
    near_high = along_y(near_down, -1)
    far_low = along_y(far, 2)
    far_high = along_y(far, -2)

    framed2 = (count2 + 2 * COARSE_X, depth // 4 + 2 * COARSE_X, lanes)
    out = pl.pallas_call(
        up_kernel,
        out_shape=arr(count, depth, lanes),
        in_specs=[VMEM] * 19,
        out_specs=VMEM,
        scratch_shapes=[vm(*framed)] * 2 + [vm(*framed1)] * 2 + [vm(*framed2)] * 9
        + [vm(framed1[0] // 2, framed1[1], lanes), vm(count // 2 + 2, framed[1], lanes)],
        compiler_params=params(),
    )(far_low, near_low, far, near_high, far_high, low2, high2, *state0, *state1)
    return out[:, None]


def solution(mesh):
    spec = P("grp", "box", None, None)
    return jax.shard_map(body, mesh=mesh, in_specs=(spec,) * 3, out_specs=spec, check_vma=False)
```

```python
import jax
import jax.numpy as jnp
from jax import lax
from jax.experimental import pallas as pl
from jax.experimental.pallas import tpu as pltpu
from jax.sharding import PartitionSpec as P

OMEGA = 0.7
FRAME = 8
WIDE_F = 6
WIDE_B = 7
COARSE_X = 6
FINE_X = 3
LANES = 128
ANY = pl.BlockSpec(memory_space=pl.ANY)
HBM = pl.BlockSpec(memory_space=pltpu.HBM)
VMEM = pl.BlockSpec(memory_space=pltpu.VMEM)
LIMIT = 16 * 1024 * 1024


def params():
    return pltpu.CompilerParams(vmem_limit_bytes=LIMIT)


def gray_position(code, bit_count):
    position = code
    for shift in range(1, bit_count):
        position = position ^ (code >> shift)
    return position


def box_position():
    bit_count = lax.axis_size("box").bit_length() - 1
    return gray_position(lax.axis_index("box"), bit_count)


def run_copies(pairs, sems):
    copies = [pltpu.make_async_copy(src, dst, sems.at[at]) for at, (src, dst) in enumerate(pairs)]
    for copy in copies:
        copy.start()
    return copies


def wait_copies(copies):
    for copy in copies:
        copy.wait()


def lane_ids(shape):
    return lax.broadcasted_iota(jnp.int32, shape, 1)


def y_next(row):
    return pltpu.roll(row, row.shape[0] - 1, 0)


def y_prev(row):
    return pltpu.roll(row, 1, 0)


def z_next(row, dist):
    return pltpu.roll(row, LANES - dist, 1)


def z_prev(row, dist):
    return pltpu.roll(row, dist, 1)


def coefficients(alpha, beta, beta_prev, beta_next, dist, scale):
    half = 0.5 * scale
    lane = lane_ids(beta.shape)
    inside = lane < LANES - dist
    up_z = jnp.where(inside, z_next(beta, dist), 0.0)
    down_z = jnp.where(lane >= dist, z_prev(beta, dist), 0.0)
    up_y = y_next(beta)
    face_x = half * (beta + beta_next)
    face_y = half * (beta + up_y)
    face_z = jnp.where(inside, half * (beta + up_z), 0.0)
    total = (beta_prev + beta_next) + (up_y + y_prev(beta)) + (up_z + down_z)
    diagonal = alpha + half * (6.0 * beta + total)
    inverse = jnp.where(alpha > 0.0, OMEGA / diagonal, 0.0)
    return face_x, face_y, face_z, diagonal, inverse


def off_sum(at, v, faces, dist):
    face_x, face_y, face_z = faces
    here = v[at]
    fy = face_y[at]
    fz = face_z[at]
    along_x = face_x[at] * v[at + 1] + face_x[at - 1] * v[at - 1]
    along_y = fy * y_next(here) + y_prev(fy * here)
    along_z = fz * z_next(here, dist) + z_prev(fz * here, dist)
    return here, along_x + along_y + along_z


def relaxed(at, v, f, inverse, faces, dist):
    here, off = off_sum(at, v, faces, dist)
    return (1.0 - OMEGA) * here + inverse[at] * (f[at] + off)


def rows_loop(low, high, step, fn):
    trips = (high - low) // step

    def run(rows):
        stores = [item for row in rows for item in fn(row)]
        for ref, at, value in stores:
            ref[at] = value

    def trip(t, carry):
        base = low + t * step
        run([base + k for k in range(step)])
        return carry

    lax.fori_loop(0, trips, trip, 0)
    rest = list(range(low + trips * step, high))
    if rest:
        run(rest)


def pair_sum_z(row, dist):
    lane = lane_ids(row.shape)
    first = (lane // dist) % 2 == 0
    return row + jnp.where(first, z_next(row, dist), z_prev(row, dist))


def strided_pair(ref, at, count):
    return ref[at, pl.ds(0, count, stride=2), :] + ref[at, pl.ds(1, count, stride=2), :]


def zero(ref, *at):
    ref[at] = jnp.zeros_like(ref[at])


WIDES = (WIDE_F, WIDE_F, WIDE_B)


def face_pieces(count):
    pieces = []
    at = 0
    for k, wide in enumerate(WIDES):
        for x in range(count):
            pieces.append((k, x, wide, at))
            at += wide
    return pieces, at + -at % 8


def corner_pieces():
    pieces = []
    at = 0
    for side in range(2):
        start = 0
        for k, wide in enumerate(WIDES):
            for layer in range(wide):
                distance = layer + 1 if side else wide - layer
                layers = min(wide, wide + 2 - distance)
                pieces.append((side, k, start + layer, layers, at))
                at += layers
            start += wide
    return pieces, at + -at % 8


def pack_faces_kernel(f, a, b, F, A, B, x_up, x_down, y_up, y_down, sems):
    count, depth = f.shape[:2]
    own = (pl.ds(FRAME, count), pl.ds(FRAME, depth))
    frames = (F, A, B)
    copies = run_copies([(src, dst.at[own]) for src, dst in zip((f, a, b), frames)], sems)
    pieces, _ = face_pieces(count)
    row = 0
    for k, (ref, wide) in enumerate(zip(frames, WIDES)):
        copies[k].wait()
        for layer in range(wide):
            x_up[row + layer] = ref[FRAME + count - wide + layer, FRAME:FRAME + depth]
            x_down[row + layer] = ref[FRAME + layer, FRAME:FRAME + depth]
        row += wide
        for at_k, x, layers, at in pieces:
            if at_k == k:
                y_up[at:at + layers] = ref[FRAME + x, FRAME + depth - layers:FRAME + depth]
                y_down[at:at + layers] = ref[FRAME + x, FRAME:FRAME + layers]


def pack_corners_kernel(low, high, up, down):
    depth = low.shape[1]
    for side, _, row, layers, at in corner_pieces()[0]:
        ref = (low, high)[side]
        up[at:at + layers] = ref[row, depth - layers:depth]
        down[at:at + layers] = ref[row, 0:layers]


def down_rows(F, A, B, FX, FY, FZ, DG, IN, V, U, T):
    faces = (FX, FY, FZ)

    def coef_row(i):
        fx, fy, fz, dg, inv = coefficients(A[i], B[i], B[i - 1], B[i + 1], 1, 1.0)
        return [(FX, i, fx), (FY, i, fy), (FZ, i, fz), (DG, i, dg), (IN, i, inv), (V, i, inv * F[i])]

    def sweep_row(i):
        return [(U, i, relaxed(i, V, F, IN, faces, 1))]

    def residual(i):
        here, off = off_sum(i, U, faces, 1)
        return F[i] - DG[i] * here + off

    def restrict_row(j):
        return [(T, j, residual(2 * j) + residual(2 * j + 1))]

    return coef_row, sweep_row, restrict_row


def down_inner_kernel(y_low, y_high, F_in, A_in, B_in, F, A, B, FX, FY, FZ, DG, IN, V, U, T):
    end = F.shape[0]
    depth = F.shape[1] - 2 * FRAME
    count = end - 2 * FRAME
    frames = (F, A, B)
    for k, x, layers, at in face_pieces(count)[0]:
        frames[k][FRAME + x, FRAME - layers:FRAME] = y_low[at:at + layers]
        frames[k][FRAME + x, FRAME + depth:FRAME + depth + layers] = y_high[at:at + layers]
    zero_y_edges(frames, depth)
    coef_row, sweep_row, restrict_row = down_rows(F, A, B, FX, FY, FZ, DG, IN, V, U, T)
    rows_loop(FRAME + 1, end - FRAME - 1, 10, coef_row)
    rows_loop(FRAME + 2, end - FRAME - 2, 14, sweep_row)
    rows_loop(FRAME // 2 + 2, (end - FRAME) // 2 - 2, 6, restrict_row)


def zero_y_edges(frames, depth):
    position = box_position()
    for edge, y in (
        (position == 0, slice(0, FRAME)),
        (position == lax.axis_size("box") - 1, slice(FRAME + depth, FRAME + depth + FRAME)),
    ):

        @pl.when(edge)
        def _(y=y):
            for ref in frames:
                zero(ref, slice(None), y)


def down_kernel(
    low, high, c_low, c_high,
    F_in, A_in, B_in, FX_in, FY_in, FZ_in, DG_in, IN_in, V_in, U_in, T_in,
    F, A, B, FX, FY, FZ, DG, IN, V, U, T,
    out_v1, out_f1, out_inv1, out_fx1, out_fy1, out_fz1,
    out_coarse, to_up, to_down,
    A1, B1, D1, W1, T1,
):
    count = F.shape[0] - 2 * FRAME
    depth = F.shape[1] - 2 * FRAME
    frames = (F, A, B)
    start = 0
    for k, wide in enumerate(WIDES):
        for layer in range(wide):
            frames[k][FRAME - wide + layer, FRAME:FRAME + depth] = low[start + layer]
            frames[k][FRAME + count + layer, FRAME:FRAME + depth] = high[start + layer]
        start += wide
    starts = (0, WIDE_F, 2 * WIDE_F)
    for side, k, row, layers, at in corner_pieces()[0]:
        x = row - starts[k] + (FRAME + count if side else FRAME - WIDES[k])
        frames[k][x, FRAME - layers:FRAME] = c_low[at:at + layers]
        frames[k][x, FRAME + depth:FRAME + depth + layers] = c_high[at:at + layers]
    zero_y_edges(frames, depth)
    group = lax.axis_index("grp")
    for edge, x in (
        (group == 0, slice(0, FRAME)),
        (group == lax.axis_size("grp") - 1, slice(FRAME + count, FRAME + count + FRAME)),
    ):

        @pl.when(edge)
        def _(x=x):
            for ref in frames:
                zero(ref, x)

    end = count + 2 * FRAME
    coef_row, sweep_row, restrict_row = down_rows(F, A, B, FX, FY, FZ, DG, IN, V, U, T)

    FX[1] = 0.5 * (B[1] + B[2])
    for margin, fn in ((2, coef_row), (3, sweep_row)):
        rows_loop(margin, FRAME + margin - 1, 7, fn)
        rows_loop(end - FRAME - margin + 1, end - margin, 7, fn)
    rows_loop(2, FRAME // 2 + 2, 4, restrict_row)
    rows_loop((end - FRAME) // 2 - 2, end // 2 - 2, 4, restrict_row)
    half_rows = (depth + 2 * FRAME) // 2

    def level1_source(j):
        return [(out_f1, j, 0.125 * pair_sum_z(strided_pair(T, j, half_rows), 1))]

    rows_loop(2, end // 2 - 2, 10, level1_source)

    def level1_coef(j):
        stores = []
        for src, dst in ((A, A1), (B, B1)):
            both = strided_pair(src, 2 * j, half_rows) + strided_pair(src, 2 * j + 1, half_rows)
            stores.append((dst, j, 0.125 * pair_sum_z(both, 1)))
        return stores

    rows_loop(1, end // 2 - 1, 11, level1_coef)

    faces1 = (out_fx1, out_fy1, out_fz1)
    end1 = end // 2
    out_fx1[1] = 0.125 * (B1[1] + B1[2])

    def coef_row1(i):
        fx, fy, fz, dg, inv = coefficients(A1[i], B1[i], B1[i - 1], B1[i + 1], 2, 0.25)
        return [
            (out_fx1, i, fx), (out_fy1, i, fy), (out_fz1, i, fz),
            (D1, i, dg), (out_inv1, i, inv), (W1, i, inv * out_f1[i]),
        ]

    rows_loop(2, end1 - 2, 10, coef_row1)

    def sweep_row1(i):
        return [(out_v1, i, relaxed(i, W1, out_f1, out_inv1, faces1, 2))]

    rows_loop(3, end1 - 3, 18, sweep_row1)

    def residual1(i):
        here, off = off_sum(i, out_v1, faces1, 2)
        return out_f1[i] - D1[i] * here + off

    first1 = FRAME // 2
    count1 = count // 2
    count2 = count // 4
    quarter_rows = half_rows // 2
    lane = lane_ids((1, LANES))

    def coarse_row(x):
        i = first1 + 2 * x
        return [
            (T1, (0, x), residual1(i) + residual1(i + 1)),
            (T1, (1, x), A1[i] + A1[i + 1]),
            (T1, (2, x), B1[i] + B1[i + 1]),
        ]

    rows_loop(0, count2, 8, coarse_row)
    own2 = FRAME // 4
    depth2 = depth // 4

    def coarse_pack(x):
        stores = []
        for k in range(3):
            both = T1[k, x, pl.ds(0, quarter_rows, stride=2), :] + T1[k, x, pl.ds(1, quarter_rows, stride=2), :]
            value = 0.125 * pair_sum_z(both, 2)
            packed = jnp.zeros((1, LANES), jnp.float32)
            for y in range(depth2):
                packed = packed + jnp.where(lane % depth2 == y, value[own2 + y:own2 + y + 1], 0.0)
            stores.append((out_coarse, pl.ds(k * count2 + x, 1), packed))
        return stores

    rows_loop(0, count2, 8, coarse_pack)

    own1 = slice(first1, first1 + depth // 2)
    for k in range(3):
        rows = slice(k * COARSE_X, (k + 1) * COARSE_X)
        to_up[rows] = out_coarse[(k + 1) * count2 - COARSE_X:(k + 1) * count2]
        to_down[rows] = out_coarse[k * count2:k * count2 + COARSE_X]
    for k in range(FINE_X):
        rows = slice(3 * COARSE_X + k * depth // 2, 3 * COARSE_X + (k + 1) * depth // 2)
        to_up[rows] = out_v1[first1 + count1 - FINE_X + k, own1]
        to_down[rows] = out_v1[first1 + k, own1]


def pack_coarse_kernel(coarse, v1, low, high, far, near_up, near_down):
    count2 = coarse.shape[0] // 3
    span2 = count2 + 2 * COARSE_X
    first1 = FRAME // 2
    depth1 = v1.shape[1] - FRAME
    count1 = 2 * count2
    for k in range(3):
        row = k * span2
        part = slice(k * COARSE_X, (k + 1) * COARSE_X)
        far[row:row + COARSE_X] = low[part]
        far[row + COARSE_X:row + COARSE_X + count2] = coarse[k * count2:(k + 1) * count2]
        far[row + COARSE_X + count2:row + span2] = high[part]
    rows = far.shape[0]
    for out, face in ((near_up, depth1 - FINE_X), (near_down, 0)):
        out[0:rows] = far[...]
        row = rows
        for k in range(FINE_X):
            start = 3 * COARSE_X + k * depth1 + face
            out[row:row + FINE_X] = low[start:start + FINE_X]
            last = row + FINE_X * (FINE_X + count1)
            out[last:last + FINE_X] = high[start:start + FINE_X]
            row += FINE_X
        for k in range(count1):
            out[row:row + FINE_X] = v1[first1 + k, first1 + face:first1 + face + FINE_X]
            row += FINE_X


def up_kernel(
    far_low, near_low, own, near_high, far_high, low, high,
    in_v, F, IN, FX, FY, FZ,
    in_v1, F1, IN1, FX1, FY1, FZ1,
    out,
    V, U, V1, U1,
    S2, A2, B2, FX2, FY2, FZ2, IN2, V2, U2, PT, P0,
):
    sources = (far_low, near_low, own, near_high, far_high)
    group = lax.axis_index("grp")
    position = box_position()
    last_group = lax.axis_size("grp") - 1
    last_block = lax.axis_size("box") - 1
    depth = out.shape[1]

    rows2 = B2.shape[1]
    span2 = B2.shape[0]
    sub = lax.broadcasted_iota(jnp.int32, (rows2, LANES), 0)
    lane = lane_ids((rows2, LANES))
    block = (sub + 2) // 4
    cell = position * (depth // 4) + sub - COARSE_X
    inside = (cell >= 0) & (cell < (last_block + 1) * (depth // 4))
    mine = (lane % 4 == (sub + 2) % 4) & inside
    last_of_four = lane % 4 == 3

    def unpack_row(x):
        stores = []
        for k, dst in enumerate((S2, A2, B2)):
            row = pl.ds(k * span2 + x, 1)
            packed = jnp.broadcast_to(sources[0][row], (rows2, LANES))
            for slot in range(1, 5):
                packed = jnp.where(block == slot, jnp.broadcast_to(sources[slot][row], (rows2, LANES)), packed)
            t = jnp.where(mine, packed, 0.0)
            t = t + z_prev(t, 1)
            t = t + z_prev(t, 2)
            t = jnp.where(last_of_four, t, 0.0)
            t = t + z_next(t, 1)
            stores.append((dst, x, t + z_next(t, 2)))
        return stores

    rows_loop(0, span2, 5, unpack_row)
    for edge, rows in ((group == 0, slice(0, COARSE_X)), (group == last_group, slice(span2 - COARSE_X, span2))):

        @pl.when(edge)
        def _(rows=rows):
            zero(A2, rows)
            zero(B2, rows)

    FX2[0] = 0.5 * 0.0625 * (B2[0] + B2[1])

    def coef_row2(i):
        fx, fy, fz, dg, inv = coefficients(A2[i], B2[i], B2[i - 1], B2[i + 1], 4, 0.0625)
        return [(FX2, i, fx), (FY2, i, fy), (FZ2, i, fz), (IN2, i, inv), (V2, i, inv * S2[i])]

    rows_loop(1, span2 - 1, 9, coef_row2)
    faces2 = (FX2, FY2, FZ2)
    src, dst = V2, U2
    for sweep in range(1, 4):

        def sweep_row2(i, src=src, dst=dst):
            return [(dst, i, relaxed(i, src, S2, IN2, faces2, 4))]

        rows_loop(1 + sweep, span2 - 1 - sweep, 9 - sweep, sweep_row2)
        src, dst = dst, src
    coarse = src

    first1 = FRAME // 2
    depth1 = depth // 2
    span1 = V1.shape[0]
    own_rows = pl.ds(first1, depth1)

    def own_row(x):
        i = first1 + x
        return [(V1, (i, own_rows), in_v1[i, own_rows])]

    rows_loop(0, span1 - 2 * first1, 16, own_row)
    for k in range(FINE_X):
        tile = pl.ds(3 * COARSE_X + k * depth1, depth1)
        V1[first1 - FINE_X + k, own_rows] = low[tile]
        V1[span1 - first1 + k, own_rows] = high[tile]

    def add_coarse(x):
        half = coarse[x + COARSE_X - first1 // 2, first1:first1 + depth1]
        return [(PT, (x, pl.ds(k, depth1, stride=2)), half) for k in range(2)]

    rows_loop(0, span1 // 2, 12, add_coarse)

    rim = far_low.shape[0]

    def rim_row(x):
        i = x + first1 - FINE_X
        part = pl.ds(rim + FINE_X * x, FINE_X)
        return [
            (V1, (i, slice(first1 - FINE_X, first1)), jnp.where(position > 0, near_low[part], 0.0)),
            (
                V1,
                (i, slice(first1 + depth1, first1 + depth1 + FINE_X)),
                jnp.where(position < last_block, near_high[part], 0.0),
            ),
        ]

    rows_loop(0, span1 - 2 * (first1 - FINE_X), 22, rim_row)
    for edge, rows in ((group == 0, slice(0, first1)), (group == last_group, slice(span1 - first1, span1))):

        @pl.when(edge)
        def _(rows=rows):
            zero(V1, rows)

    def corrected_row(x):
        add = PT[x]
        return [(V1, 2 * x + k, V1[2 * x + k] + add) for k in range(2)]

    rows_loop(0, span1 // 2, 12, corrected_row)
    faces1 = (FX1, FY1, FZ1)

    def sweep_a1(i):
        return [(U1, i, relaxed(i, V1, F1, IN1, faces1, 2))]

    rows_loop(2, span1 - 2, 10, sweep_a1)

    def sweep_b1(i):
        return [(V1, i, relaxed(i, U1, F1, IN1, faces1, 2))]

    rows_loop(3, span1 - 3, 18, sweep_b1)

    span = V.shape[0]
    rows1 = V1.shape[1]
    start = FRAME - 2

    def widen(x):
        row = V1[x + start // 2]
        return [(P0, (x, pl.ds(k, rows1, stride=2)), row) for k in range(2)]

    rows_loop(0, (span - 2 * start) // 2, 18, widen)

    def corrected0(x):
        add = P0[x]
        i = start + 2 * x
        return [(V, i + k, in_v[i + k] + add) for k in range(2)]

    rows_loop(0, (span - 2 * start) // 2, 9, corrected0)
    faces = (FX, FY, FZ)

    def sweep_a(i):
        return [(U, i, relaxed(i, V, F, IN, faces, 1))]

    rows_loop(start + 1, span - start - 1, 17, sweep_a)

    def sweep_b(i):
        rows = pl.ds(FRAME, depth)
        here = U[i, rows]
        fz = FZ[i, rows]
        along_x = FX[i, rows] * U[i + 1, rows] + FX[i - 1, rows] * U[i - 1, rows]
        before = pl.ds(FRAME - 1, depth)
        along_y = FY[i, rows] * U[i, pl.ds(FRAME + 1, depth)] + FY[i, before] * U[i, before]
        along_z = fz * z_next(here, 1) + z_prev(fz * here, 1)
        off = along_x + along_y + along_z
        return [(out, i - FRAME, (1.0 - OMEGA) * here + IN[i, rows] * (F[i, rows] + off))]

    rows_loop(FRAME, span - FRAME, 16, sweep_b)


def body(source, alpha, beta):
    f = source[:, 0]
    a = alpha[:, 0]
    b = beta[:, 0]
    count, depth, lanes = f.shape
    groups = lax.axis_size("grp")
    blocks = lax.axis_size("box")
    code = [p ^ (p >> 1) for p in range(blocks)]

    def along_x(array, by):
        return lax.ppermute(array, "grp", [(i, (i + by) % groups) for i in range(groups)])

    def along_y(array, by):
        return lax.ppermute(array, "box", [(code[p], code[(p + by) % blocks]) for p in range(blocks)])

    def arr(*shape):
        return jax.ShapeDtypeStruct(shape, jnp.float32)

    def vm(*shape):
        return pltpu.VMEM(shape, jnp.float32)

    dma = pltpu.SemaphoreType.DMA
    x_rows = 2 * WIDE_F + WIDE_B
    framed = (count + 2 * FRAME, depth + 2 * FRAME, lanes)
    y_rows = face_pieces(count)[1]
    c_rows = corner_pieces()[1]
    *frames, x_up, x_down, y_up, y_down = pl.pallas_call(
        pack_faces_kernel,
        out_shape=[arr(*framed)] * 3 + [arr(x_rows, depth, lanes)] * 2 + [arr(y_rows, lanes)] * 2,
        in_specs=[HBM] * 3,
        out_specs=[VMEM] * 7,
        scratch_shapes=[dma((3,))],
        compiler_params=params(),
    )(*[pltpu.with_memory_space_constraint(t, pltpu.HBM) for t in (f, a, b)])
    low = along_x(x_up, 1)
    high = along_x(x_down, -1)
    y_low = along_y(y_up, 1)
    y_high = along_y(y_down, -1)

    c_up, c_down = pl.pallas_call(
        pack_corners_kernel,
        out_shape=[arr(c_rows, lanes)] * 2,
        in_specs=[VMEM] * 2,
        out_specs=[VMEM] * 2,
        compiler_params=params(),
    )(low, high)
    c_low = along_y(c_up, 1)
    c_high = along_y(c_down, -1)

    framed1 = (framed[0] // 2, framed[1] // 2, lanes)
    level0 = [arr(*framed)] * 10 + [arr(framed1[0], framed[1], lanes)]
    level0 = pl.pallas_call(
        down_inner_kernel,
        out_shape=level0,
        in_specs=[VMEM] * 5,
        out_specs=[VMEM] * 11,
        input_output_aliases={2 + k: k for k in range(3)},
        compiler_params=params(),
    )(y_low, y_high, *frames)
    count2 = count // 4
    x2_rows = 3 * COARSE_X + FINE_X * depth // 2
    x2_rows += -x2_rows % 8
    results = pl.pallas_call(
        down_kernel,
        out_shape=[arr(*t.shape) for t in level0] + [arr(*framed1)] * 6
        + [arr(3 * count2, lanes)] + [arr(x2_rows, lanes)] * 2,
        in_specs=[VMEM] * 15,
        out_specs=[VMEM] * 20,
        input_output_aliases={4 + k: k for k in range(11)},
        scratch_shapes=[vm(*framed1)] * 4 + [vm(3, count2, framed1[1], lanes)],
        compiler_params=params(),
    )(low, high, c_low, c_high, *level0)
    F, _, _, FX, FY, FZ, _, IN, _, U, _ = results[:11]
    state0 = (U, F, IN, FX, FY, FZ)
    state1 = results[11:17]
    coarse, to_up, to_down = results[17:]

    low2 = along_x(to_up, 1)
    high2 = along_x(to_down, -1)
    far_rows = 3 * (count2 + 2 * COARSE_X)
    far_rows += -far_rows % 8
    near_rows = far_rows + FINE_X * (count // 2 + 2 * FINE_X)
    near_rows += -near_rows % 8
    far, near_up, near_down = pl.pallas_call(
        pack_coarse_kernel,
        out_shape=[arr(far_rows, lanes)] + [arr(near_rows, lanes)] * 2,
        in_specs=[VMEM] * 4,
        out_specs=[VMEM] * 3,
        compiler_params=params(),
    )(coarse, state1[0], low2, high2)
    near_low = along_y(near_up, 1)
    near_high = along_y(near_down, -1)
    far_low = along_y(far, 2)
    far_high = along_y(far, -2)

    framed2 = (count2 + 2 * COARSE_X, depth // 4 + 2 * COARSE_X, lanes)
    out = pl.pallas_call(
        up_kernel,
        out_shape=arr(count, depth, lanes),
        in_specs=[VMEM] * 19,
        out_specs=VMEM,
        scratch_shapes=[vm(*framed)] * 2 + [vm(*framed1)] * 2 + [vm(*framed2)] * 9
        + [vm(framed1[0] // 2, framed1[1], lanes), vm(count // 2 + 2, framed[1], lanes)],
        compiler_params=params(),
    )(far_low, near_low, far, near_high, far_high, low2, high2, *state0, *state1)
    return out[:, None]


def solution(mesh):
    spec = P("grp", "box", None, None)
    return jax.shard_map(body, mesh=mesh, in_specs=(spec,) * 3, out_specs=spec, check_vma=False)
```

```python
import jax
import jax.numpy as jnp
from jax import lax
from jax.experimental import pallas as pl
from jax.experimental.pallas import tpu as pltpu
from jax.sharding import PartitionSpec as P

OMEGA = 0.7
FRAME = 8
WIDE_F = 6
WIDE_B = 7
COARSE_PITCH = 24
COARSE_X = 6
FINE_X = 3
LANES = 128
ANY = pl.BlockSpec(memory_space=pl.ANY)
HBM = pl.BlockSpec(memory_space=pltpu.HBM)
VMEM = pl.BlockSpec(memory_space=pltpu.VMEM)
LIMIT = 16 * 1024 * 1024


def params():
    return pltpu.CompilerParams(vmem_limit_bytes=LIMIT)


def gray_position(code, bit_count):
    position = code
    for shift in range(1, bit_count):
        position = position ^ (code >> shift)
    return position


def box_position():
    bit_count = lax.axis_size("box").bit_length() - 1
    return gray_position(lax.axis_index("box"), bit_count)


def even_position():
    return box_position() % 2 == 0


def run_copies(pairs, sems):
    copies = [pltpu.make_async_copy(src, dst, sems.at[at]) for at, (src, dst) in enumerate(pairs)]
    for copy in copies:
        copy.start()
    return copies


def wait_copies(copies):
    for copy in copies:
        copy.wait()


def lane_ids(shape):
    return lax.broadcasted_iota(jnp.int32, shape, 1)


def y_next(row):
    return pltpu.roll(row, row.shape[0] - 1, 0)


def y_prev(row):
    return pltpu.roll(row, 1, 0)


def z_next(row, dist):
    return pltpu.roll(row, LANES - dist, 1)


def z_prev(row, dist):
    return pltpu.roll(row, dist, 1)


def coefficients(alpha, beta, beta_prev, beta_next, dist, scale):
    half = 0.5 * scale
    lane = lane_ids(beta.shape)
    inside = lane < LANES - dist
    up_z = jnp.where(inside, z_next(beta, dist), 0.0)
    down_z = jnp.where(lane >= dist, z_prev(beta, dist), 0.0)
    up_y = y_next(beta)
    face_x = half * (beta + beta_next)
    face_y = half * (beta + up_y)
    face_z = jnp.where(inside, half * (beta + up_z), 0.0)
    total = (beta_prev + beta_next) + (up_y + y_prev(beta)) + (up_z + down_z)
    diagonal = alpha + half * (6.0 * beta + total)
    inverse = jnp.where(alpha > 0.0, OMEGA / diagonal, 0.0)
    return face_x, face_y, face_z, diagonal, inverse


def off_sum(at, v, faces, dist):
    face_x, face_y, face_z = faces
    here = v[at]
    fy = face_y[at]
    fz = face_z[at]
    along_x = face_x[at] * v[at + 1] + face_x[at - 1] * v[at - 1]
    along_y = fy * y_next(here) + y_prev(fy * here)
    along_z = fz * z_next(here, dist) + z_prev(fz * here, dist)
    return here, along_x + along_y + along_z


def relaxed(at, v, f, inverse, faces, dist):
    here, off = off_sum(at, v, faces, dist)
    return (1.0 - OMEGA) * here + inverse[at] * (f[at] + off)


def rows_loop(low, high, step, fn):
    trips = (high - low) // step

    def run(rows):
        stores = [item for row in rows for item in fn(row)]
        for ref, at, value in stores:
            ref[at] = value

    def trip(t, carry):
        base = low + t * step
        run([base + k for k in range(step)])
        return carry

    lax.fori_loop(0, trips, trip, 0)
    rest = list(range(low + trips * step, high))
    if rest:
        run(rest)


def pair_sum_z(row, dist):
    lane = lane_ids(row.shape)
    first = (lane // dist) % 2 == 0
    return row + jnp.where(first, z_next(row, dist), z_prev(row, dist))


def strided_pair(ref, at, count):
    return ref[at, pl.ds(0, count, stride=2), :] + ref[at, pl.ds(1, count, stride=2), :]


def zero(ref, *at):
    ref[at] = jnp.zeros_like(ref[at])


WIDES = (WIDE_F, WIDE_F, WIDE_B)


def face_pieces(count):
    pieces = []
    at = 0
    for k, wide in enumerate(WIDES):
        for x in range(count):
            pieces.append((k, x, wide, at))
            at += wide
    return pieces, at + -at % 8


def corner_pieces():
    pieces = []
    at = 0
    for side in range(2):
        start = 0
        for k, wide in enumerate(WIDES):
            for layer in range(wide):
                distance = layer + 1 if side else wide - layer
                layers = min(wide, wide + 2 - distance)
                pieces.append((side, k, start + layer, layers, at))
                at += layers
            start += wide
    return pieces, at + -at % 8


def pack_faces_kernel(f, a, b, F, A, B, x_up, x_down, y_up, y_down, sems):
    count, depth = f.shape[:2]
    own = (pl.ds(FRAME, count), pl.ds(FRAME, depth))
    frames = (F, A, B)
    copies = run_copies([(src, dst.at[own]) for src, dst in zip((f, a, b), frames)], sems)
    pieces, _ = face_pieces(count)
    row = 0
    for k, (ref, wide) in enumerate(zip(frames, WIDES)):
        copies[k].wait()
        for layer in range(wide):
            x_up[row + layer] = ref[FRAME + count - wide + layer, FRAME:FRAME + depth]
            x_down[row + layer] = ref[FRAME + layer, FRAME:FRAME + depth]
        row += wide
        for at_k, x, layers, at in pieces:
            if at_k == k:
                y_up[at:at + layers] = ref[FRAME + x, FRAME + depth - layers:FRAME + depth]
                y_down[at:at + layers] = ref[FRAME + x, FRAME:FRAME + layers]


def pack_corners_kernel(low, high, to_even, to_odd):
    depth = low.shape[1]
    even = even_position()
    for side, _, row, layers, at in corner_pieces()[0]:
        ref = (low, high)[side]
        up = ref[row, depth - layers:depth]
        down = ref[row, 0:layers]
        to_even[at:at + layers] = jnp.where(even, up, down)
        to_odd[at:at + layers] = jnp.where(even, down, up)


def down_rows(F, A, B, FX, FY, FZ, DG, IN, V, U, T, F1, A1, B1, FX1, FY1, FZ1, D1, IN1, W1, coarse):
    faces = (FX, FY, FZ)
    half_rows = F1.shape[1]
    count2 = coarse.shape[0] // 3
    first1 = FRAME // 2
    own2 = FRAME // 4
    depth2 = half_rows // 2 - 2 * own2
    lane = lane_ids((1, LANES))

    def coef_row(i):
        fx, fy, fz, dg, inv = coefficients(A[i], B[i], B[i - 1], B[i + 1], 1, 1.0)
        return [(FX, i, fx), (FY, i, fy), (FZ, i, fz), (DG, i, dg), (IN, i, inv), (V, i, inv * F[i])]

    def sweep_row(i):
        return [(U, i, relaxed(i, V, F, IN, faces, 1))]

    def residual(i):
        here, off = off_sum(i, U, faces, 1)
        return F[i] - DG[i] * here + off

    def restrict_row(j):
        return [(T, j, residual(2 * j) + residual(2 * j + 1))]

    def level1_source(j):
        return [(F1, j, 0.125 * pair_sum_z(strided_pair(T, j, half_rows), 1))]

    def level1_coef(j):
        stores = []
        for src, dst in ((A, A1), (B, B1)):
            both = strided_pair(src, 2 * j, half_rows) + strided_pair(src, 2 * j + 1, half_rows)
            stores.append((dst, j, 0.125 * pair_sum_z(both, 1)))
        return stores

    def coef_row1(i):
        fx, fy, fz, dg, inv = coefficients(A1[i], B1[i], B1[i - 1], B1[i + 1], 2, 0.25)
        return [(FX1, i, fx), (FY1, i, fy), (FZ1, i, fz), (D1, i, dg), (IN1, i, inv), (W1, i, inv * F1[i])]

    def coarse_pack(k, ref, at, x):
        rows = half_rows // 2
        both = ref[at, pl.ds(0, rows, stride=2), :] + ref[at, pl.ds(1, rows, stride=2), :]
        value = 0.125 * pair_sum_z(both, 2)
        packed = jnp.zeros((1, LANES), jnp.float32)
        for y in range(depth2):
            packed = packed + jnp.where(lane % depth2 == y, value[own2 + y:own2 + y + 1], 0.0)
        return (coarse, pl.ds(k * count2 + x, 1), packed)

    return coef_row, sweep_row, restrict_row, level1_source, level1_coef, coef_row1, coarse_pack


def down_inner_kernel(y_low, y_high, F_in, A_in, B_in, *refs):
    *refs, T1 = refs
    F, A, B = frames = refs[:3]
    A1, B1 = refs[12:14]
    end = F.shape[0]
    depth = F.shape[1] - 2 * FRAME
    count = end - 2 * FRAME
    for k, x, layers, at in face_pieces(count)[0]:
        frames[k][FRAME + x, FRAME - layers:FRAME] = y_low[at:at + layers]
        frames[k][FRAME + x, FRAME + depth:FRAME + depth + layers] = y_high[at:at + layers]
    zero_y_edges(frames, depth)
    coef_row, sweep_row, restrict_row, level1_source, level1_coef, coef_row1, coarse_pack = down_rows(*refs)
    first1 = FRAME // 2
    end1 = end // 2
    rows_loop(FRAME + 1, end - FRAME - 1, 10, coef_row)
    rows_loop(FRAME + 2, end - FRAME - 2, 14, sweep_row)
    rows_loop(first1 + 2, end1 - first1 - 2, 6, restrict_row)
    rows_loop(first1 + 2, end1 - first1 - 2, 12, level1_source)
    rows_loop(first1, end1 - first1, 8, level1_coef)
    rows_loop(first1 + 2, end1 - first1 - 2, 12, coef_row1)
    count2 = count // 4

    def coarse_sum(x):
        i = first1 + 2 * x
        return [(T1, x, A1[i] + A1[i + 1]), (T1, count2 + x, B1[i] + B1[i + 1])]

    rows_loop(0, count2, 8, coarse_sum)

    def coarse_rows(x):
        return [coarse_pack(1, T1, x, x), coarse_pack(2, T1, count2 + x, x)]

    rows_loop(0, count2, 8, coarse_rows)


def zero_y_edges(frames, depth):
    position = box_position()
    for edge, y in (
        (position == 0, slice(0, FRAME)),
        (position == lax.axis_size("box") - 1, slice(FRAME + depth, FRAME + depth + FRAME)),
    ):

        @pl.when(edge)
        def _(y=y):
            for ref in frames:
                zero(ref, slice(None), y)


def down_kernel(low, high, c_even, c_odd, *refs):
    refs = refs[21:]
    *refs, V1, to_up, to_down, T1 = refs
    F, A, B = frames = refs[:3]
    FX = refs[3]
    F1, A1, B1, FX1, FY1, FZ1, D1, IN1, W1, coarse = refs[11:]
    count = F.shape[0] - 2 * FRAME
    depth = F.shape[1] - 2 * FRAME
    even = even_position()
    start = 0
    for k, wide in enumerate(WIDES):
        for layer in range(wide):
            frames[k][FRAME - wide + layer, FRAME:FRAME + depth] = low[start + layer]
            frames[k][FRAME + count + layer, FRAME:FRAME + depth] = high[start + layer]
        start += wide
    starts = (0, WIDE_F, 2 * WIDE_F)
    for side, k, row, layers, at in corner_pieces()[0]:
        x = row - starts[k] + (FRAME + count if side else FRAME - WIDES[k])
        near_even = c_even[at:at + layers]
        near_odd = c_odd[at:at + layers]
        frames[k][x, FRAME - layers:FRAME] = jnp.where(even, near_odd, near_even)
        frames[k][x, FRAME + depth:FRAME + depth + layers] = jnp.where(even, near_even, near_odd)
    zero_y_edges(frames, depth)
    group = lax.axis_index("grp")
    for edge, x in (
        (group == 0, slice(0, FRAME)),
        (group == lax.axis_size("grp") - 1, slice(FRAME + count, FRAME + count + FRAME)),
    ):

        @pl.when(edge)
        def _(x=x):
            for ref in frames:
                zero(ref, x)

    end = count + 2 * FRAME
    coef_row, sweep_row, restrict_row, level1_source, level1_coef, coef_row1, coarse_pack = down_rows(*refs)
    first1 = FRAME // 2
    end1 = end // 2
    FX[1] = 0.5 * (B[1] + B[2])
    for margin, fn in ((2, coef_row), (3, sweep_row)):
        rows_loop(margin, FRAME + margin - 1, 7, fn)
        rows_loop(end - FRAME - margin + 1, end - margin, 7, fn)
    for fn in (restrict_row, level1_source):
        rows_loop(2, first1 + 2, 4, fn)
        rows_loop(end1 - first1 - 2, end1 - 2, 4, fn)
    rows_loop(1, first1, 3, level1_coef)
    rows_loop(end1 - first1, end1 - 1, 3, level1_coef)
    FX1[1] = 0.125 * (B1[1] + B1[2])
    rows_loop(2, first1 + 2, 4, coef_row1)
    rows_loop(end1 - first1 - 2, end1 - 2, 4, coef_row1)

    faces1 = (FX1, FY1, FZ1)

    def sweep_row1(i):
        return [(V1, i, relaxed(i, W1, F1, IN1, faces1, 2))]

    rows_loop(3, end1 - 3, 18, sweep_row1)

    def residual1(i):
        here, off = off_sum(i, V1, faces1, 2)
        return F1[i] - D1[i] * here + off

    count1 = count // 2
    count2 = count // 4

    def coarse_row(x):
        i = first1 + 2 * x
        return [(T1, x, residual1(i) + residual1(i + 1))]

    rows_loop(0, count2, 8, coarse_row)

    def coarse_source(x):
        return [coarse_pack(0, T1, x, x)]

    rows_loop(0, count2, 8, coarse_source)

    own1 = slice(first1, first1 + depth // 2)
    for k in range(3):
        rows = slice(k * COARSE_X, (k + 1) * COARSE_X)
        to_up[rows] = coarse[(k + 1) * count2 - COARSE_X:(k + 1) * count2]
        to_down[rows] = coarse[k * count2:k * count2 + COARSE_X]
    for k in range(FINE_X):
        rows = slice(3 * COARSE_X + k * depth // 2, 3 * COARSE_X + (k + 1) * depth // 2)
        to_up[rows] = V1[first1 + count1 - FINE_X + k, own1]
        to_down[rows] = V1[first1 + k, own1]


def pack_coarse_kernel(coarse, v1, low, high, far, to_even, to_odd):
    count2 = coarse.shape[0] // 3
    first1 = FRAME // 2
    depth1 = v1.shape[1] - FRAME
    count1 = 2 * count2
    for k in range(3):
        row = k * COARSE_PITCH
        part = slice(k * COARSE_X, (k + 1) * COARSE_X)
        far[row:row + COARSE_X] = low[part]
        far[row + COARSE_X:row + COARSE_X + count2] = coarse[k * count2:(k + 1) * count2]
        far[row + COARSE_X + count2:row + 2 * COARSE_X + count2] = high[part]
    rows = far.shape[0]
    to_even[0:rows] = far[...]
    to_odd[0:rows] = far[...]
    even = even_position()
    tiles = [low[3 * COARSE_X + k * depth1:3 * COARSE_X + (k + 1) * depth1] for k in range(FINE_X)]
    tiles += [v1[first1 + k, first1:first1 + depth1] for k in range(count1)]
    tiles += [high[3 * COARSE_X + k * depth1:3 * COARSE_X + (k + 1) * depth1] for k in range(FINE_X)]
    for k, tile in enumerate(tiles):
        part = slice(rows + k * FINE_X, rows + (k + 1) * FINE_X)
        up = tile[depth1 - FINE_X:]
        down = tile[:FINE_X]
        to_even[part] = jnp.where(even, up, down)
        to_odd[part] = jnp.where(even, down, up)


def coarse_solve(source, alpha, beta):
    shape = beta[0].shape
    lane = lane_ids(shape)
    first = lane % 4 == 0
    last = lane % 4 == 3
    inside = lane < LANES - 4
    nothing = jnp.zeros(shape, jnp.float32)

    def next_x(v):
        return pltpu.roll(v, shape[0] - 1, 0)

    def prev_x(v):
        return pltpu.roll(v, 1, 0)

    def next_y(vs):
        over = [pltpu.roll(v, 3, 1) for v in vs[1:]] + [nothing]
        return [jnp.where(last, o, pltpu.roll(v, LANES - 1, 1)) for o, v in zip(over, vs)]

    def prev_y(vs):
        over = [nothing] + [pltpu.roll(v, LANES - 3, 1) for v in vs[:-1]]
        return [jnp.where(first, o, pltpu.roll(v, 1, 1)) for o, v in zip(over, vs)]

    half = 0.5 * 0.0625
    coefs = []
    for a, b, b_next, b_prev in zip(alpha, beta, next_y(beta), prev_y(beta)):
        up_x = next_x(b)
        up_z = jnp.where(inside, z_next(b, 4), 0.0)
        down_z = jnp.where(lane >= 4, z_prev(b, 4), 0.0)
        total = (prev_x(b) + up_x) + (b_next + b_prev) + (up_z + down_z)
        diagonal = a + half * (6.0 * b + total)
        inverse = jnp.where(a > 0.0, OMEGA / diagonal, 0.0)
        face_z = jnp.where(inside, half * (b + up_z), 0.0)
        coefs.append((half * (b + up_x), half * (b + b_next), face_z, inverse))
    field = [c[3] * f for c, f in zip(coefs, source)]
    for _ in range(3):
        flux = prev_y([c[1] * v for c, v in zip(coefs, field)])
        new = []
        for (fx, fy, fz, inverse), v, v_next, back, f in zip(coefs, field, next_y(field), flux, source):
            off = fx * next_x(v) + prev_x(fx * v)
            off = off + (fy * v_next + back)
            off = off + (fz * z_next(v, 4) + z_prev(fz * v, 4))
            new.append((1.0 - OMEGA) * v + inverse * (f + off))
        field = new
    return field


def up_kernel(
    near_even, near_odd, far_even, far_odd, own, low, high,
    in_v, F, IN, FX, FY, FZ,
    in_v1, F1, IN1, FX1, FY1, FZ1,
    out,
    V, U, V1, U1, C2, P0, result, sems,
):
    group = lax.axis_index("grp")
    position = box_position()
    even = position % 2 == 0
    last_group = lax.axis_size("grp") - 1
    last_block = lax.axis_size("box") - 1
    count, depth = result.shape[:2]

    row2 = lax.broadcasted_iota(jnp.int32, (COARSE_PITCH, LANES), 0) - COARSE_X + group * (count // 4)
    in_x = (row2 >= 0) & (row2 < (last_group + 1) * (count // 4))
    arrays = []
    for k in range(3):
        rows = pl.ds(k * COARSE_PITCH, COARSE_PITCH)
        ne, no, fe, fo = near_even[rows], near_odd[rows], far_even[rows], far_odd[rows]
        blocks = (
            jnp.where(even, fo, fe), jnp.where(even, no, ne), own[rows],
            jnp.where(even, ne, no), jnp.where(even, fe, fo),
        )
        column = []
        for at, value in enumerate(blocks):
            place = position + (at - 2)
            column.append(jnp.where(in_x & ((place >= 0) & (place <= last_block)), value, 0.0))
        arrays.append(column)
    field2 = coarse_solve(*arrays)
    for at in range(3):
        C2[at] = field2[1 + at]

    first1 = FRAME // 2
    depth1 = depth // 2
    span1 = V1.shape[0]
    rows1 = V1.shape[1]
    own_rows = pl.ds(first1, depth1)

    def own_row(x):
        i = first1 + x
        return [(V1, (i, own_rows), in_v1[i, own_rows])]

    rows_loop(0, span1 - 2 * first1, 16, own_row)
    for k in range(FINE_X):
        tile = pl.ds(3 * COARSE_X + k * depth1, depth1)
        V1[first1 - FINE_X + k, own_rows] = low[tile]
        V1[span1 - first1 + k, own_rows] = high[tile]

    rim = own.shape[0]

    def rim_row(x):
        i = x + first1 - FINE_X
        part = pl.ds(rim + FINE_X * x, FINE_X)
        ne, no = near_even[part], near_odd[part]
        near_low = jnp.where(even, no, ne)
        near_high = jnp.where(even, ne, no)
        return [
            (V1, (i, slice(first1 - FINE_X, first1)), jnp.where(position > 0, near_low, 0.0)),
            (
                V1,
                (i, slice(first1 + depth1, first1 + depth1 + FINE_X)),
                jnp.where(position < last_block, near_high, 0.0),
            ),
        ]

    rows_loop(0, span1 - 2 * (first1 - FINE_X), 22, rim_row)
    for edge, rows in ((group == 0, slice(0, first1)), (group == last_group, slice(span1 - first1, span1))):

        @pl.when(edge)
        def _(rows=rows):
            zero(V1, rows)

    sub = lax.broadcasted_iota(jnp.int32, (rows1, LANES), 0)
    lane = lane_ids((rows1, LANES))
    block = (sub + 4) // 8
    mine = lane % 4 == (sub // 2 + 2) % 4
    last_of_four = lane % 4 == 3

    def corrected_row(x):
        row = pl.ds(x + COARSE_X - first1 // 2, 1)
        t = jnp.broadcast_to(C2[0, row], (rows1, LANES))
        for at in range(1, 3):
            t = jnp.where(block == at, jnp.broadcast_to(C2[at, row], (rows1, LANES)), t)
        t = jnp.where(mine, t, 0.0)
        t = t + z_prev(t, 1)
        t = t + z_prev(t, 2)
        t = jnp.where(last_of_four, t, 0.0)
        t = t + z_next(t, 1)
        t = t + z_next(t, 2)
        return [(V1, 2 * x + k, V1[2 * x + k] + t) for k in range(2)]

    rows_loop(0, span1 // 2, 12, corrected_row)
    faces1 = (FX1, FY1, FZ1)

    def sweep_a1(i):
        return [(U1, i, relaxed(i, V1, F1, IN1, faces1, 2))]

    rows_loop(2, span1 - 2, 10, sweep_a1)

    def sweep_b1(i):
        return [(V1, i, relaxed(i, U1, F1, IN1, faces1, 2))]

    rows_loop(3, span1 - 3, 18, sweep_b1)

    span = V.shape[0]
    start = FRAME - 2

    def widen(x):
        row = V1[x + start // 2]
        return [(P0, (x, pl.ds(k, rows1, stride=2)), row) for k in range(2)]

    rows_loop(0, (span - 2 * start) // 2, 18, widen)

    def corrected0(x):
        add = P0[x]
        i = start + 2 * x
        return [(V, i + k, in_v[i + k] + add) for k in range(2)]

    rows_loop(0, (span - 2 * start) // 2, 9, corrected0)
    faces = (FX, FY, FZ)

    def sweep_a(i):
        return [(U, i, relaxed(i, V, F, IN, faces, 1))]

    rows_loop(start + 1, span - start - 1, 17, sweep_a)

    def sweep_b(i):
        rows = pl.ds(FRAME, depth)
        here = U[i, rows]
        fz = FZ[i, rows]
        along_x = FX[i, rows] * U[i + 1, rows] + FX[i - 1, rows] * U[i - 1, rows]
        before = pl.ds(FRAME - 1, depth)
        along_y = FY[i, rows] * U[i, pl.ds(FRAME + 1, depth)] + FY[i, before] * U[i, before]
        along_z = fz * z_next(here, 1) + z_prev(fz * here, 1)
        off = along_x + along_y + along_z
        return [(result, i - FRAME, (1.0 - OMEGA) * here + IN[i, rows] * (F[i, rows] + off))]

    chunk = count // 4
    copies = []
    for k in range(4):
        rows_loop(FRAME + k * chunk, FRAME + (k + 1) * chunk, chunk, sweep_b)
        rows = pl.ds(k * chunk, chunk)
        copies.append(pltpu.make_async_copy(result.at[rows], out.at[rows], sems.at[k]))
        copies[-1].start()
    wait_copies(copies)


def body(source, alpha, beta):
    f = source[:, 0]
    a = alpha[:, 0]
    b = beta[:, 0]
    count, depth, lanes = f.shape
    groups = lax.axis_size("grp")
    blocks = lax.axis_size("box")
    code = [p ^ (p >> 1) for p in range(blocks)]

    def along_x(array, by):
        return lax.ppermute(array, "grp", [(i, (i + by) % groups) for i in range(groups)])

    def along_y(array, by):
        return lax.ppermute(array, "box", [(code[p], code[(p + by) % blocks]) for p in range(blocks)])

    def from_partner(array, even_by):
        return lax.ppermute(
            array,
            "box",
            [(code[(p + (even_by if p % 2 == 0 else -even_by)) % blocks], code[p]) for p in range(blocks)],
        )

    def arr(*shape):
        return jax.ShapeDtypeStruct(shape, jnp.float32)

    def vm(*shape):
        return pltpu.VMEM(shape, jnp.float32)

    dma = pltpu.SemaphoreType.DMA
    x_rows = 2 * WIDE_F + WIDE_B
    framed = (count + 2 * FRAME, depth + 2 * FRAME, lanes)
    y_rows = face_pieces(count)[1]
    c_rows = corner_pieces()[1]
    *frames, x_up, x_down, y_up, y_down = pl.pallas_call(
        pack_faces_kernel,
        out_shape=[arr(*framed)] * 3 + [arr(x_rows, depth, lanes)] * 2 + [arr(y_rows, lanes)] * 2,
        in_specs=[HBM] * 3,
        out_specs=[VMEM] * 7,
        scratch_shapes=[dma((3,))],
        compiler_params=params(),
    )(*[pltpu.with_memory_space_constraint(t, pltpu.HBM) for t in (f, a, b)])
    low = along_x(x_up, 1)
    high = along_x(x_down, -1)
    y_low = along_y(y_up, 1)
    y_high = along_y(y_down, -1)

    c_even, c_odd = pl.pallas_call(
        pack_corners_kernel,
        out_shape=[arr(c_rows, lanes)] * 2,
        in_specs=[VMEM] * 2,
        out_specs=[VMEM] * 2,
        compiler_params=params(),
    )(low, high)
    c_even = from_partner(c_even, 1)
    c_odd = from_partner(c_odd, -1)

    framed1 = (framed[0] // 2, framed[1] // 2, lanes)
    count2 = count // 4
    passed = [arr(*framed)] * 10 + [arr(framed1[0], framed[1], lanes)] + [arr(*framed1)] * 9 + [arr(3 * count2, lanes)]
    passed = pl.pallas_call(
        down_inner_kernel,
        out_shape=passed,
        in_specs=[VMEM] * 5,
        out_specs=[VMEM] * 21,
        input_output_aliases={2 + k: k for k in range(3)},
        scratch_shapes=[vm(2 * count2, framed1[1], lanes)],
        compiler_params=params(),
    )(y_low, y_high, *frames)
    x2_rows = 3 * COARSE_X + FINE_X * depth // 2
    x2_rows += -x2_rows % 8
    results = pl.pallas_call(
        down_kernel,
        out_shape=[arr(*t.shape) for t in passed] + [arr(*framed1)] + [arr(x2_rows, lanes)] * 2,
        in_specs=[VMEM] * 25,
        out_specs=[VMEM] * 24,
        input_output_aliases={4 + k: k for k in range(21)},
        scratch_shapes=[vm(count2, framed1[1], lanes)],
        compiler_params=params(),
    )(low, high, c_even, c_odd, *passed)
    F, _, _, FX, FY, FZ, _, IN, _, U, _, F1, _, _, FX1, FY1, FZ1, _, IN1, _, coarse, V1, to_up, to_down = results

    low2 = along_x(to_up, 1)
    high2 = along_x(to_down, -1)
    far_rows = 3 * COARSE_PITCH
    near_rows = far_rows + FINE_X * (count // 2 + 2 * FINE_X)
    near_rows += -near_rows % 8
    far, to_even, to_odd = pl.pallas_call(
        pack_coarse_kernel,
        out_shape=[arr(far_rows, lanes)] + [arr(near_rows, lanes)] * 2,
        in_specs=[VMEM] * 4,
        out_specs=[VMEM] * 3,
        compiler_params=params(),
    )(coarse, V1, low2, high2)
    near_even = from_partner(to_even, 1)
    near_odd = from_partner(to_odd, -1)
    far_even = from_partner(far, 2)
    far_odd = from_partner(far, -2)

    out = pl.pallas_call(
        up_kernel,
        out_shape=arr(count, depth, lanes),
        in_specs=[VMEM] * 19,
        out_specs=HBM,
        scratch_shapes=[vm(*framed)] * 2 + [vm(*framed1)] * 2
        + [vm(3, COARSE_PITCH, lanes), vm(count // 2 + 2, framed[1], lanes), vm(count, depth, lanes), dma((4,))],
        compiler_params=params(),
    )(
        near_even, near_odd, far_even, far_odd, far, low2, high2,
        U, F, IN, FX, FY, FZ, V1, F1, IN1, FX1, FY1, FZ1,
    )
    return out[:, None]


def solution(mesh):
    spec = P("grp", "box", None, None)
    return jax.shard_map(body, mesh=mesh, in_specs=(spec,) * 3, out_specs=spec, check_vma=False)
```

```python
import jax
import jax.numpy as jnp
from jax import lax
from jax.experimental import pallas as pl
from jax.experimental.pallas import tpu as pltpu
from jax.sharding import PartitionSpec as P

OMEGA = 0.7
FRAME = 8
WIDE_F = 6
WIDE_B = 7
COARSE_PITCH = 24
COARSE_X = 6
FINE_X = 3
LANES = 128
ANY = pl.BlockSpec(memory_space=pl.ANY)
HBM = pl.BlockSpec(memory_space=pltpu.HBM)
VMEM = pl.BlockSpec(memory_space=pltpu.VMEM)
LIMIT = 16 * 1024 * 1024


def params():
    return pltpu.CompilerParams(vmem_limit_bytes=LIMIT)


def gray_position(code, bit_count):
    position = code
    for shift in range(1, bit_count):
        position = position ^ (code >> shift)
    return position


def box_position():
    bit_count = lax.axis_size("box").bit_length() - 1
    return gray_position(lax.axis_index("box"), bit_count)


def even_position():
    return box_position() % 2 == 0


def even_group():
    return lax.axis_index("grp") % 2 == 0


def below_above(even, from_even, from_odd):
    return jnp.where(even, from_odd, from_even), jnp.where(even, from_even, from_odd)


def run_copies(pairs, sems):
    copies = [pltpu.make_async_copy(src, dst, sems.at[at]) for at, (src, dst) in enumerate(pairs)]
    for copy in copies:
        copy.start()
    return copies


def wait_copies(copies):
    for copy in copies:
        copy.wait()


def lane_ids(shape):
    return lax.broadcasted_iota(jnp.int32, shape, 1)


def y_next(row):
    return pltpu.roll(row, row.shape[0] - 1, 0)


def y_prev(row):
    return pltpu.roll(row, 1, 0)


def z_next(row, dist):
    return pltpu.roll(row, LANES - dist, 1)


def z_prev(row, dist):
    return pltpu.roll(row, dist, 1)


def coefficients(alpha, beta, beta_prev, beta_next, dist, scale):
    half = 0.5 * scale
    lane = lane_ids(beta.shape)
    inside = lane < LANES - dist
    up_z = jnp.where(inside, z_next(beta, dist), 0.0)
    down_z = jnp.where(lane >= dist, z_prev(beta, dist), 0.0)
    up_y = y_next(beta)
    face_x = half * (beta + beta_next)
    face_y = half * (beta + up_y)
    face_z = jnp.where(inside, half * (beta + up_z), 0.0)
    total = (beta_prev + beta_next) + (up_y + y_prev(beta)) + (up_z + down_z)
    diagonal = alpha + half * (6.0 * beta + total)
    inverse = jnp.where(alpha > 0.0, OMEGA / diagonal, 0.0)
    return face_x, face_y, face_z, diagonal, inverse


def off_sum(at, v, faces, dist):
    face_x, face_y, face_z = faces
    here = v[at]
    fy = face_y[at]
    fz = face_z[at]
    along_x = face_x[at] * v[at + 1] + face_x[at - 1] * v[at - 1]
    along_y = fy * y_next(here) + y_prev(fy * here)
    along_z = fz * z_next(here, dist) + z_prev(fz * here, dist)
    return here, along_x + along_y + along_z


def relaxed(at, v, f, inverse, faces, dist):
    here, off = off_sum(at, v, faces, dist)
    return (1.0 - OMEGA) * here + inverse[at] * (f[at] + off)


def rows_loop(low, high, step, fn):
    trips = (high - low) // step

    def run(rows):
        stores = [item for row in rows for item in fn(row)]
        for ref, at, value in stores:
            ref[at] = value

    def trip(t, carry):
        base = low + t * step
        run([base + k for k in range(step)])
        return carry

    lax.fori_loop(0, trips, trip, 0)
    rest = list(range(low + trips * step, high))
    if rest:
        run(rest)


def pair_sum_z(row, dist):
    lane = lane_ids(row.shape)
    first = (lane // dist) % 2 == 0
    return row + jnp.where(first, z_next(row, dist), z_prev(row, dist))


def strided_pair(ref, at, count):
    return ref[at, pl.ds(0, count, stride=2), :] + ref[at, pl.ds(1, count, stride=2), :]


def zero(ref, *at):
    ref[at] = jnp.zeros_like(ref[at])


WIDES = (WIDE_F, WIDE_F, WIDE_B)


def face_pieces(count):
    pieces = []
    at = 0
    for k, wide in enumerate(WIDES):
        for x in range(count):
            pieces.append((k, x, wide, at))
            at += wide
    return pieces, at + -at % 8


def corner_pieces():
    pieces = []
    at = 0
    for side in range(2):
        start = 0
        for k, wide in enumerate(WIDES):
            for layer in range(wide):
                distance = layer + 1 if side else wide - layer
                layers = min(wide, wide + 2 - distance)
                pieces.append((side, k, start + layer, layers, at))
                at += layers
            start += wide
    return pieces, at + -at % 8


def pack_faces_kernel(f, a, b, F, A, B, x_even, x_odd, y_even, y_odd, sems):
    count, depth = f.shape[:2]
    own = (pl.ds(FRAME, count), pl.ds(FRAME, depth))
    frames = (F, A, B)
    copies = run_copies([(src, dst.at[own]) for src, dst in zip((f, a, b), frames)], sems)
    pieces, _ = face_pieces(count)
    even = even_position()
    even_x = even_group()
    row = 0
    for k, (ref, wide) in enumerate(zip(frames, WIDES)):
        copies[k].wait()
        for layer in range(wide):
            up = ref[FRAME + count - wide + layer, FRAME:FRAME + depth]
            down = ref[FRAME + layer, FRAME:FRAME + depth]
            x_odd[row + layer], x_even[row + layer] = below_above(even_x, up, down)
        row += wide
        for at_k, x, layers, at in pieces:
            if at_k == k:
                up = ref[FRAME + x, FRAME + depth - layers:FRAME + depth]
                down = ref[FRAME + x, FRAME:FRAME + layers]
                y_odd[at:at + layers], y_even[at:at + layers] = below_above(even, up, down)


def pack_corners_kernel(x_even, x_odd, to_even, to_odd):
    depth = x_even.shape[1]
    even = even_position()
    even_x = even_group()
    for side, _, row, layers, at in corner_pieces()[0]:
        up_rows = slice(depth - layers, depth)
        up = below_above(even_x, x_even[row, up_rows], x_odd[row, up_rows])[side]
        down = below_above(even_x, x_even[row, 0:layers], x_odd[row, 0:layers])[side]
        to_odd[at:at + layers], to_even[at:at + layers] = below_above(even, up, down)


def down_rows(F, A, B, FX, FY, FZ, DG, IN, V, U, T, F1, A1, B1, FX1, FY1, FZ1, D1, IN1, W1, coarse):
    faces = (FX, FY, FZ)
    half_rows = F1.shape[1]
    count2 = coarse.shape[0] // 3
    first1 = FRAME // 2
    own2 = FRAME // 4
    depth2 = half_rows // 2 - 2 * own2
    lane = lane_ids((1, LANES))

    def coef_row(i):
        fx, fy, fz, dg, inv = coefficients(A[i], B[i], B[i - 1], B[i + 1], 1, 1.0)
        return [(FX, i, fx), (FY, i, fy), (FZ, i, fz), (DG, i, dg), (IN, i, inv), (V, i, inv * F[i])]

    def sweep_row(i):
        return [(U, i, relaxed(i, V, F, IN, faces, 1))]

    def residual(i):
        here, off = off_sum(i, U, faces, 1)
        return F[i] - DG[i] * here + off

    def restrict_row(j):
        return [(T, j, residual(2 * j) + residual(2 * j + 1))]

    def level1_source(j):
        return [(F1, j, 0.125 * pair_sum_z(strided_pair(T, j, half_rows), 1))]

    def level1_coef(j):
        stores = []
        for src, dst in ((A, A1), (B, B1)):
            both = strided_pair(src, 2 * j, half_rows) + strided_pair(src, 2 * j + 1, half_rows)
            stores.append((dst, j, 0.125 * pair_sum_z(both, 1)))
        return stores

    def coef_row1(i):
        fx, fy, fz, dg, inv = coefficients(A1[i], B1[i], B1[i - 1], B1[i + 1], 2, 0.25)
        return [(FX1, i, fx), (FY1, i, fy), (FZ1, i, fz), (D1, i, dg), (IN1, i, inv), (W1, i, inv * F1[i])]

    def coarse_pack(k, ref, at, x):
        rows = half_rows // 2
        both = ref[at, pl.ds(0, rows, stride=2), :] + ref[at, pl.ds(1, rows, stride=2), :]
        value = 0.125 * pair_sum_z(both, 2)
        packed = jnp.zeros((1, LANES), jnp.float32)
        for y in range(depth2):
            packed = packed + jnp.where(lane % depth2 == y, value[own2 + y:own2 + y + 1], 0.0)
        return (coarse, pl.ds(k * count2 + x, 1), packed)

    return coef_row, sweep_row, restrict_row, level1_source, level1_coef, coef_row1, coarse_pack


def down_inner_kernel(y_even, y_odd, F_in, A_in, B_in, *refs):
    *refs, T1 = refs
    F, A, B = frames = refs[:3]
    A1, B1 = refs[12:14]
    end = F.shape[0]
    depth = F.shape[1] - 2 * FRAME
    count = end - 2 * FRAME
    even = even_position()
    for k, x, layers, at in face_pieces(count)[0]:
        below, above = below_above(even, y_even[at:at + layers], y_odd[at:at + layers])
        frames[k][FRAME + x, FRAME - layers:FRAME] = below
        frames[k][FRAME + x, FRAME + depth:FRAME + depth + layers] = above
    zero_y_edges(frames, depth)
    coef_row, sweep_row, restrict_row, level1_source, level1_coef, coef_row1, coarse_pack = down_rows(*refs)
    first1 = FRAME // 2
    end1 = end // 2
    rows_loop(FRAME + 1, end - FRAME - 1, 10, coef_row)
    rows_loop(FRAME + 2, end - FRAME - 2, 14, sweep_row)
    rows_loop(first1 + 2, end1 - first1 - 2, 6, restrict_row)
    rows_loop(first1 + 2, end1 - first1 - 2, 12, level1_source)
    rows_loop(first1, end1 - first1, 8, level1_coef)
    rows_loop(first1 + 2, end1 - first1 - 2, 12, coef_row1)
    count2 = count // 4

    def coarse_sum(x):
        i = first1 + 2 * x
        return [(T1, x, A1[i] + A1[i + 1]), (T1, count2 + x, B1[i] + B1[i + 1])]

    rows_loop(0, count2, 8, coarse_sum)

    def coarse_rows(x):
        return [coarse_pack(1, T1, x, x), coarse_pack(2, T1, count2 + x, x)]

    rows_loop(0, count2, 8, coarse_rows)


def zero_y_edges(frames, depth):
    position = box_position()
    for edge, y in (
        (position == 0, slice(0, FRAME)),
        (position == lax.axis_size("box") - 1, slice(FRAME + depth, FRAME + depth + FRAME)),
    ):

        @pl.when(edge)
        def _(y=y):
            for ref in frames:
                zero(ref, slice(None), y)


def down_kernel(x_even, x_odd, c_even, c_odd, *refs):
    refs = refs[21:]
    *refs, V1, to_even, to_odd, T1 = refs
    F, A, B = frames = refs[:3]
    FX = refs[3]
    F1, A1, B1, FX1, FY1, FZ1, D1, IN1, W1, coarse = refs[11:]
    count = F.shape[0] - 2 * FRAME
    depth = F.shape[1] - 2 * FRAME
    even = even_position()
    even_x = even_group()
    start = 0
    for k, wide in enumerate(WIDES):
        for layer in range(wide):
            below, above = below_above(even_x, x_even[start + layer], x_odd[start + layer])
            frames[k][FRAME - wide + layer, FRAME:FRAME + depth] = below
            frames[k][FRAME + count + layer, FRAME:FRAME + depth] = above
        start += wide
    starts = (0, WIDE_F, 2 * WIDE_F)
    for side, k, row, layers, at in corner_pieces()[0]:
        x = row - starts[k] + (FRAME + count if side else FRAME - WIDES[k])
        below, above = below_above(even, c_even[at:at + layers], c_odd[at:at + layers])
        frames[k][x, FRAME - layers:FRAME] = below
        frames[k][x, FRAME + depth:FRAME + depth + layers] = above
    zero_y_edges(frames, depth)
    group = lax.axis_index("grp")
    for edge, x in (
        (group == 0, slice(0, FRAME)),
        (group == lax.axis_size("grp") - 1, slice(FRAME + count, FRAME + count + FRAME)),
    ):

        @pl.when(edge)
        def _(x=x):
            for ref in frames:
                zero(ref, x)

    end = count + 2 * FRAME
    coef_row, sweep_row, restrict_row, level1_source, level1_coef, coef_row1, coarse_pack = down_rows(*refs)
    first1 = FRAME // 2
    end1 = end // 2
    FX[1] = 0.5 * (B[1] + B[2])
    for margin, fn in ((2, coef_row), (3, sweep_row)):
        rows_loop(margin, FRAME + margin - 1, 7, fn)
        rows_loop(end - FRAME - margin + 1, end - margin, 7, fn)
    for fn in (restrict_row, level1_source):
        rows_loop(2, first1 + 2, 4, fn)
        rows_loop(end1 - first1 - 2, end1 - 2, 4, fn)
    rows_loop(1, first1, 3, level1_coef)
    rows_loop(end1 - first1, end1 - 1, 3, level1_coef)
    FX1[1] = 0.125 * (B1[1] + B1[2])
    rows_loop(2, first1 + 2, 4, coef_row1)
    rows_loop(end1 - first1 - 2, end1 - 2, 4, coef_row1)

    faces1 = (FX1, FY1, FZ1)

    def sweep_row1(i):
        return [(V1, i, relaxed(i, W1, F1, IN1, faces1, 2))]

    rows_loop(3, end1 - 3, 18, sweep_row1)

    def residual1(i):
        here, off = off_sum(i, V1, faces1, 2)
        return F1[i] - D1[i] * here + off

    count1 = count // 2
    count2 = count // 4

    def coarse_row(x):
        i = first1 + 2 * x
        return [(T1, x, residual1(i) + residual1(i + 1))]

    rows_loop(0, count2, 8, coarse_row)

    def coarse_source(x):
        return [coarse_pack(0, T1, x, x)]

    rows_loop(0, count2, 8, coarse_source)

    own1 = slice(first1, first1 + depth // 2)
    for k in range(3):
        rows = slice(k * COARSE_X, (k + 1) * COARSE_X)
        up = coarse[(k + 1) * count2 - COARSE_X:(k + 1) * count2]
        down = coarse[k * count2:k * count2 + COARSE_X]
        to_odd[rows], to_even[rows] = below_above(even_x, up, down)
    for k in range(FINE_X):
        rows = slice(3 * COARSE_X + k * depth // 2, 3 * COARSE_X + (k + 1) * depth // 2)
        up = V1[first1 + count1 - FINE_X + k, own1]
        down = V1[first1 + k, own1]
        to_odd[rows], to_even[rows] = below_above(even_x, up, down)


def pack_coarse_kernel(coarse, v1, x_even, x_odd, far, to_even, to_odd, low, high):
    low[...], high[...] = below_above(even_group(), x_even[...], x_odd[...])
    count2 = coarse.shape[0] // 3
    first1 = FRAME // 2
    depth1 = v1.shape[1] - FRAME
    count1 = 2 * count2
    for k in range(3):
        row = k * COARSE_PITCH
        part = slice(k * COARSE_X, (k + 1) * COARSE_X)
        far[row:row + COARSE_X] = low[part]
        far[row + COARSE_X:row + COARSE_X + count2] = coarse[k * count2:(k + 1) * count2]
        far[row + COARSE_X + count2:row + 2 * COARSE_X + count2] = high[part]
    rows = far.shape[0]
    to_even[0:rows] = far[...]
    to_odd[0:rows] = far[...]
    even = even_position()
    tiles = [low[3 * COARSE_X + k * depth1:3 * COARSE_X + (k + 1) * depth1] for k in range(FINE_X)]
    tiles += [v1[first1 + k, first1:first1 + depth1] for k in range(count1)]
    tiles += [high[3 * COARSE_X + k * depth1:3 * COARSE_X + (k + 1) * depth1] for k in range(FINE_X)]
    for k, tile in enumerate(tiles):
        part = slice(rows + k * FINE_X, rows + (k + 1) * FINE_X)
        up = tile[depth1 - FINE_X:]
        down = tile[:FINE_X]
        to_odd[part], to_even[part] = below_above(even, up, down)


def coarse_solve(source, alpha, beta):
    shape = beta[0].shape
    lane = lane_ids(shape)
    first = lane % 4 == 0
    last = lane % 4 == 3
    inside = lane < LANES - 4
    nothing = jnp.zeros(shape, jnp.float32)

    def next_x(v):
        return pltpu.roll(v, shape[0] - 1, 0)

    def prev_x(v):
        return pltpu.roll(v, 1, 0)

    def next_y(vs):
        over = [pltpu.roll(v, 3, 1) for v in vs[1:]] + [nothing]
        return [jnp.where(last, o, pltpu.roll(v, LANES - 1, 1)) for o, v in zip(over, vs)]

    def prev_y(vs):
        over = [nothing] + [pltpu.roll(v, LANES - 3, 1) for v in vs[:-1]]
        return [jnp.where(first, o, pltpu.roll(v, 1, 1)) for o, v in zip(over, vs)]

    half = 0.5 * 0.0625
    coefs = []
    for a, b, b_next, b_prev in zip(alpha, beta, next_y(beta), prev_y(beta)):
        up_x = next_x(b)
        up_z = jnp.where(inside, z_next(b, 4), 0.0)
        down_z = jnp.where(lane >= 4, z_prev(b, 4), 0.0)
        total = (prev_x(b) + up_x) + (b_next + b_prev) + (up_z + down_z)
        diagonal = a + half * (6.0 * b + total)
        inverse = jnp.where(a > 0.0, OMEGA / diagonal, 0.0)
        face_z = jnp.where(inside, half * (b + up_z), 0.0)
        coefs.append((half * (b + up_x), half * (b + b_next), face_z, inverse))
    field = [c[3] * f for c, f in zip(coefs, source)]
    for _ in range(3):
        flux = prev_y([c[1] * v for c, v in zip(coefs, field)])
        new = []
        for (fx, fy, fz, inverse), v, v_next, back, f in zip(coefs, field, next_y(field), flux, source):
            off = fx * next_x(v) + prev_x(fx * v)
            off = off + (fy * v_next + back)
            off = off + (fz * z_next(v, 4) + z_prev(fz * v, 4))
            new.append((1.0 - OMEGA) * v + inverse * (f + off))
        field = new
    return field


def up_kernel(
    near_even, near_odd, far_even, far_odd, own, x_even, x_odd,
    in_v, F, IN, FX, FY, FZ,
    in_v1, F1, IN1, FX1, FY1, FZ1,
    out,
    V, U, V1, U1, C2, P0, result, sems,
):
    group = lax.axis_index("grp")
    position = box_position()
    even = position % 2 == 0
    last_group = lax.axis_size("grp") - 1
    last_block = lax.axis_size("box") - 1
    count, depth = result.shape[:2]

    row2 = lax.broadcasted_iota(jnp.int32, (COARSE_PITCH, LANES), 0) - COARSE_X + group * (count // 4)
    in_x = (row2 >= 0) & (row2 < (last_group + 1) * (count // 4))
    arrays = []
    for k in range(3):
        rows = pl.ds(k * COARSE_PITCH, COARSE_PITCH)
        ne, no, fe, fo = near_even[rows], near_odd[rows], far_even[rows], far_odd[rows]
        near_low, near_high = below_above(even, ne, no)
        far_low, far_high = below_above(even, fe, fo)
        blocks = (far_low, near_low, own[rows], near_high, far_high)
        column = []
        for at, value in enumerate(blocks):
            place = position + (at - 2)
            column.append(jnp.where(in_x & ((place >= 0) & (place <= last_block)), value, 0.0))
        arrays.append(column)
    field2 = coarse_solve(*arrays)
    for at in range(3):
        C2[at] = field2[1 + at]

    first1 = FRAME // 2
    depth1 = depth // 2
    span1 = V1.shape[0]
    rows1 = V1.shape[1]
    own_rows = pl.ds(first1, depth1)

    def own_row(x):
        i = first1 + x
        return [(V1, (i, own_rows), in_v1[i, own_rows])]

    rows_loop(0, span1 - 2 * first1, 16, own_row)
    for k in range(FINE_X):
        tile = pl.ds(3 * COARSE_X + k * depth1, depth1)
        below, above = below_above(even_group(), x_even[tile], x_odd[tile])
        V1[first1 - FINE_X + k, own_rows] = below
        V1[span1 - first1 + k, own_rows] = above

    rim = own.shape[0]

    def rim_row(x):
        i = x + first1 - FINE_X
        part = pl.ds(rim + FINE_X * x, FINE_X)
        near_low, near_high = below_above(even, near_even[part], near_odd[part])
        return [
            (V1, (i, slice(first1 - FINE_X, first1)), jnp.where(position > 0, near_low, 0.0)),
            (
                V1,
                (i, slice(first1 + depth1, first1 + depth1 + FINE_X)),
                jnp.where(position < last_block, near_high, 0.0),
            ),
        ]

    rows_loop(0, span1 - 2 * (first1 - FINE_X), 22, rim_row)
    for edge, rows in ((group == 0, slice(0, first1)), (group == last_group, slice(span1 - first1, span1))):

        @pl.when(edge)
        def _(rows=rows):
            zero(V1, rows)

    sub = lax.broadcasted_iota(jnp.int32, (rows1, LANES), 0)
    lane = lane_ids((rows1, LANES))
    block = (sub + 4) // 8
    mine = lane % 4 == (sub // 2 + 2) % 4
    last_of_four = lane % 4 == 3

    def corrected_row(x):
        row = pl.ds(x + COARSE_X - first1 // 2, 1)
        t = jnp.broadcast_to(C2[0, row], (rows1, LANES))
        for at in range(1, 3):
            t = jnp.where(block == at, jnp.broadcast_to(C2[at, row], (rows1, LANES)), t)
        t = jnp.where(mine, t, 0.0)
        t = t + z_prev(t, 1)
        t = t + z_prev(t, 2)
        t = jnp.where(last_of_four, t, 0.0)
        t = t + z_next(t, 1)
        t = t + z_next(t, 2)
        return [(V1, 2 * x + k, V1[2 * x + k] + t) for k in range(2)]

    rows_loop(0, span1 // 2, 12, corrected_row)
    faces1 = (FX1, FY1, FZ1)

    def sweep_a1(i):
        return [(U1, i, relaxed(i, V1, F1, IN1, faces1, 2))]

    rows_loop(2, span1 - 2, 10, sweep_a1)

    def sweep_b1(i):
        return [(V1, i, relaxed(i, U1, F1, IN1, faces1, 2))]

    rows_loop(3, span1 - 3, 18, sweep_b1)

    span = V.shape[0]
    start = FRAME - 2

    def widen(x):
        row = V1[x + start // 2]
        return [(P0, (x, pl.ds(k, rows1, stride=2)), row) for k in range(2)]

    rows_loop(0, (span - 2 * start) // 2, 18, widen)

    def corrected0(x):
        add = P0[x]
        i = start + 2 * x
        return [(V, i + k, in_v[i + k] + add) for k in range(2)]

    rows_loop(0, (span - 2 * start) // 2, 9, corrected0)
    faces = (FX, FY, FZ)

    def sweep_a(i):
        return [(U, i, relaxed(i, V, F, IN, faces, 1))]

    rows_loop(start + 1, span - start - 1, 17, sweep_a)

    def sweep_b(i):
        rows = pl.ds(FRAME, depth)
        here = U[i, rows]
        fz = FZ[i, rows]
        along_x = FX[i, rows] * U[i + 1, rows] + FX[i - 1, rows] * U[i - 1, rows]
        before = pl.ds(FRAME - 1, depth)
        along_y = FY[i, rows] * U[i, pl.ds(FRAME + 1, depth)] + FY[i, before] * U[i, before]
        along_z = fz * z_next(here, 1) + z_prev(fz * here, 1)
        off = along_x + along_y + along_z
        return [(result, i - FRAME, (1.0 - OMEGA) * here + IN[i, rows] * (F[i, rows] + off))]

    chunk = count // 4
    copies = []
    for k in range(4):
        rows_loop(FRAME + k * chunk, FRAME + (k + 1) * chunk, chunk, sweep_b)
        rows = pl.ds(k * chunk, chunk)
        copies.append(pltpu.make_async_copy(result.at[rows], out.at[rows], sems.at[k]))
        copies[-1].start()
    wait_copies(copies)


def body(source, alpha, beta):
    f = source[:, 0]
    a = alpha[:, 0]
    b = beta[:, 0]
    count, depth, lanes = f.shape
    groups = lax.axis_size("grp")
    blocks = lax.axis_size("box")
    code = [p ^ (p >> 1) for p in range(blocks)]

    def moved(array, target):
        def index(g, p):
            return g * blocks + code[p]

        pairs = [(index(g, p), index(*target(g, p))) for g in range(groups) for p in range(blocks)]
        return lax.ppermute(array, ("grp", "box"), pairs)

    def odd_partner(at, size):
        other = at + 1 if at % 2 else at - 1
        return other if 0 <= other < size else None

    def x_even(g, p):
        return g ^ 1, p

    def x_odd(g, p):
        other = odd_partner(g, groups)
        return (g, p ^ 1) if other is None else (other, p)

    def y_even(g, p):
        return g, p ^ 1

    def y_odd(g, p):
        other = odd_partner(p, blocks)
        return (g ^ (groups // 2), p) if other is None else (g, other)

    def far_even(g, p):
        other = p + 2 if p % 2 else p - 2
        return g, other if 0 <= other < blocks else p ^ 1

    def far_odd(g, p):
        other = p - 2 if p % 2 else p + 2
        return g, other if 0 <= other < blocks else p ^ 1

    def arr(*shape):
        return jax.ShapeDtypeStruct(shape, jnp.float32)

    def vm(*shape):
        return pltpu.VMEM(shape, jnp.float32)

    dma = pltpu.SemaphoreType.DMA
    x_rows = 2 * WIDE_F + WIDE_B
    framed = (count + 2 * FRAME, depth + 2 * FRAME, lanes)
    y_rows = face_pieces(count)[1]
    c_rows = corner_pieces()[1]
    *frames, to_x_even, to_x_odd, to_y_even, to_y_odd = pl.pallas_call(
        pack_faces_kernel,
        out_shape=[arr(*framed)] * 3 + [arr(x_rows, depth, lanes)] * 2 + [arr(y_rows, lanes)] * 2,
        in_specs=[HBM] * 3,
        out_specs=[VMEM] * 7,
        scratch_shapes=[dma((3,))],
        compiler_params=params(),
    )(*[pltpu.with_memory_space_constraint(t, pltpu.HBM) for t in (f, a, b)])
    x_halo = moved(to_x_even, x_even), moved(to_x_odd, x_odd)
    y_halo = moved(to_y_even, y_even), moved(to_y_odd, y_odd)

    to_even, to_odd = pl.pallas_call(
        pack_corners_kernel,
        out_shape=[arr(c_rows, lanes)] * 2,
        in_specs=[VMEM] * 2,
        out_specs=[VMEM] * 2,
        compiler_params=params(),
    )(*x_halo)
    corners = moved(to_even, y_even), moved(to_odd, y_odd)

    framed1 = (framed[0] // 2, framed[1] // 2, lanes)
    count2 = count // 4
    passed = [arr(*framed)] * 10 + [arr(framed1[0], framed[1], lanes)] + [arr(*framed1)] * 9 + [arr(3 * count2, lanes)]
    passed = pl.pallas_call(
        down_inner_kernel,
        out_shape=passed,
        in_specs=[VMEM] * 5,
        out_specs=[VMEM] * 21,
        input_output_aliases={2 + k: k for k in range(3)},
        scratch_shapes=[vm(2 * count2, framed1[1], lanes)],
        compiler_params=params(),
    )(*y_halo, *frames)
    x2_rows = 3 * COARSE_X + FINE_X * depth // 2
    x2_rows += -x2_rows % 8
    results = pl.pallas_call(
        down_kernel,
        out_shape=[arr(*t.shape) for t in passed] + [arr(*framed1)] + [arr(x2_rows, lanes)] * 2,
        in_specs=[VMEM] * 25,
        out_specs=[VMEM] * 24,
        input_output_aliases={4 + k: k for k in range(21)},
        scratch_shapes=[vm(count2, framed1[1], lanes)],
        compiler_params=params(),
    )(*x_halo, *corners, *passed)
    F, _, _, FX, FY, FZ, _, IN, _, U, _, F1, _, _, FX1, FY1, FZ1, _, IN1, _, coarse, V1, to_even, to_odd = results

    x_halo = moved(to_even, x_even), moved(to_odd, x_odd)
    far_rows = 3 * COARSE_PITCH
    near_rows = far_rows + FINE_X * (count // 2 + 2 * FINE_X)
    near_rows += -near_rows % 8
    far, to_even, to_odd = pl.pallas_call(
        pack_coarse_kernel,
        out_shape=[arr(far_rows, lanes)] + [arr(near_rows, lanes)] * 2,
        in_specs=[VMEM] * 4,
        out_specs=[VMEM] * 3,
        scratch_shapes=[vm(x2_rows, lanes)] * 2,
        compiler_params=params(),
    )(coarse, V1, *x_halo)
    near = moved(to_even, y_even), moved(to_odd, y_odd)
    distant = moved(far, far_even), moved(far, far_odd)

    out = pl.pallas_call(
        up_kernel,
        out_shape=arr(count, depth, lanes),
        in_specs=[VMEM] * 19,
        out_specs=HBM,
        scratch_shapes=[vm(*framed)] * 2 + [vm(*framed1)] * 2
        + [vm(3, COARSE_PITCH, lanes), vm(count // 2 + 2, framed[1], lanes), vm(count, depth, lanes), dma((4,))],
        compiler_params=params(),
    )(
        *near, *distant, far, *x_halo,
        U, F, IN, FX, FY, FZ, V1, F1, IN1, FX1, FY1, FZ1,
    )
    return out[:, None]


def solution(mesh):
    spec = P("grp", "box", None, None)
    return jax.shard_map(body, mesh=mesh, in_specs=(spec,) * 3, out_specs=spec, check_vma=False)
```

```python
import jax
import jax.numpy as jnp
from jax import lax
from jax.experimental import pallas as pl
from jax.experimental.pallas import tpu as pltpu
from jax.sharding import PartitionSpec as P

OMEGA = 0.7
FRAME = 8
WIDE_F = 6
WIDE_B = 7
COARSE_PITCH = 24
COARSE_X = 6
FINE_X = 3
LANES = 128
ANY = pl.BlockSpec(memory_space=pl.ANY)
HBM = pl.BlockSpec(memory_space=pltpu.HBM)
VMEM = pl.BlockSpec(memory_space=pltpu.VMEM)
LIMIT = 16 * 1024 * 1024


def params():
    return pltpu.CompilerParams(vmem_limit_bytes=LIMIT)


def gray_position(code, bit_count):
    position = code
    for shift in range(1, bit_count):
        position = position ^ (code >> shift)
    return position


def box_position():
    bit_count = lax.axis_size("box").bit_length() - 1
    return gray_position(lax.axis_index("box"), bit_count)


def even_position():
    return box_position() % 2 == 0


def even_group():
    return lax.axis_index("grp") % 2 == 0


def below_above(even, from_even, from_odd):
    return jnp.where(even, from_odd, from_even), jnp.where(even, from_even, from_odd)


def run_copies(pairs, sems):
    copies = [pltpu.make_async_copy(src, dst, sems.at[at]) for at, (src, dst) in enumerate(pairs)]
    for copy in copies:
        copy.start()
    return copies


def wait_copies(copies):
    for copy in copies:
        copy.wait()


def lane_ids(shape):
    return lax.broadcasted_iota(jnp.int32, shape, 1)


def y_next(row):
    return pltpu.roll(row, row.shape[0] - 1, 0)


def y_prev(row):
    return pltpu.roll(row, 1, 0)


def z_next(row, dist):
    return pltpu.roll(row, LANES - dist, 1)


def z_prev(row, dist):
    return pltpu.roll(row, dist, 1)


def coefficients(alpha, beta, beta_prev, beta_next, dist, scale):
    half = 0.5 * scale
    lane = lane_ids(beta.shape)
    inside = lane < LANES - dist
    up_z = jnp.where(inside, z_next(beta, dist), 0.0)
    down_z = jnp.where(lane >= dist, z_prev(beta, dist), 0.0)
    up_y = y_next(beta)
    face_x = half * (beta + beta_next)
    face_y = half * (beta + up_y)
    face_z = jnp.where(inside, half * (beta + up_z), 0.0)
    total = (beta_prev + beta_next) + (up_y + y_prev(beta)) + (up_z + down_z)
    diagonal = alpha + half * (6.0 * beta + total)
    inverse = jnp.where(alpha > 0.0, OMEGA / diagonal, 0.0)
    return face_x, face_y, face_z, diagonal, inverse


def off_sum(at, v, faces, dist):
    face_x, face_y, face_z = faces
    here = v[at]
    fy = face_y[at]
    fz = face_z[at]
    along_x = face_x[at] * v[at + 1] + face_x[at - 1] * v[at - 1]
    along_y = fy * y_next(here) + y_prev(fy * here)
    along_z = fz * z_next(here, dist) + z_prev(fz * here, dist)
    return here, along_x + along_y + along_z


def relaxed(at, v, f, inverse, faces, dist):
    here, off = off_sum(at, v, faces, dist)
    return (1.0 - OMEGA) * here + inverse[at] * (f[at] + off)


def rows_loop(low, high, step, fn):
    trips = (high - low) // step

    def run(rows):
        stores = [item for row in rows for item in fn(row)]
        for ref, at, value in stores:
            ref[at] = value

    def trip(t, carry):
        base = low + t * step
        run([base + k for k in range(step)])
        return carry

    if trips <= 4:
        for t in range(trips):
            run([low + t * step + k for k in range(step)])
    else:
        lax.fori_loop(0, trips, trip, 0)
    rest = list(range(low + trips * step, high))
    if rest:
        run(rest)


def pair_sum_z(row, dist):
    lane = lane_ids(row.shape)
    return row + jnp.take_along_axis(row, lane ^ dist, axis=1)


def strided_pair(ref, at, count):
    return ref[at, pl.ds(0, count, stride=2), :] + ref[at, pl.ds(1, count, stride=2), :]


def zero(ref, *at):
    ref[at] = jnp.zeros_like(ref[at])


WIDES = (WIDE_F, WIDE_F, WIDE_B)


FACE_PARTS = ((0, 1), (2,))


def face_pieces(count):
    pieces = []
    sizes = []
    for part, arrays in enumerate(FACE_PARTS):
        at = 0
        for k in arrays:
            for x in range(count):
                pieces.append((k, x, WIDES[k], part, at))
                at += WIDES[k]
        sizes.append(at + -at % 8)
    return pieces, sizes


def corner_pieces():
    pieces = []
    at = 0
    for side in range(2):
        start = 0
        for k, wide in enumerate(WIDES):
            for layer in range(wide):
                distance = layer + 1 if side else wide - layer
                layers = min(wide, wide + 2 - distance)
                pieces.append((side, k, start + layer, layers, at))
                at += layers
            start += wide
    return pieces, at + -at % 8


def pack_faces_kernel(f, a, b, F, A, B, x_even, x_odd, *rest):
    *y_faces, sems = rest
    y_even = y_faces[:len(FACE_PARTS)]
    y_odd = y_faces[len(FACE_PARTS):]
    count, depth = f.shape[:2]
    own = (pl.ds(FRAME, count), pl.ds(FRAME, depth))
    frames = (F, A, B)
    copies = run_copies([(src, dst.at[own]) for src, dst in zip((f, a, b), frames)], sems)
    pieces, _ = face_pieces(count)
    even = even_position()
    even_x = even_group()
    row = 0
    for k, (ref, wide) in enumerate(zip(frames, WIDES)):
        copies[k].wait()
        for layer in range(wide):
            up = ref[FRAME + count - wide + layer, FRAME:FRAME + depth]
            down = ref[FRAME + layer, FRAME:FRAME + depth]
            x_odd[row + layer], x_even[row + layer] = below_above(even_x, up, down)
        row += wide
        for at_k, x, layers, part, at in pieces:
            if at_k == k:
                up = ref[FRAME + x, FRAME + depth - layers:FRAME + depth]
                down = ref[FRAME + x, FRAME:FRAME + layers]
                rows = slice(at, at + layers)
                y_odd[part][rows], y_even[part][rows] = below_above(even, up, down)


def pack_corners_kernel(x_even, x_odd, to_even, to_odd):
    depth = x_even.shape[1]
    even = even_position()
    even_x = even_group()
    for side, _, row, layers, at in corner_pieces()[0]:
        up_rows = slice(depth - layers, depth)
        up = below_above(even_x, x_even[row, up_rows], x_odd[row, up_rows])[side]
        down = below_above(even_x, x_even[row, 0:layers], x_odd[row, 0:layers])[side]
        to_odd[at:at + layers], to_even[at:at + layers] = below_above(even, up, down)


def down_rows(F, A, B, FX, FY, FZ, DG, IN, V, U, T, F1, A1, B1, FX1, FY1, FZ1, D1, IN1, W1, coarse):
    faces = (FX, FY, FZ)
    half_rows = F1.shape[1]
    count2 = coarse.shape[0] // 3
    first1 = FRAME // 2
    own2 = FRAME // 4
    depth2 = half_rows // 2 - 2 * own2
    lane = lane_ids((1, LANES))

    def coef_row(i):
        fx, fy, fz, dg, inv = coefficients(A[i], B[i], B[i - 1], B[i + 1], 1, 1.0)
        return [(FX, i, fx), (FY, i, fy), (FZ, i, fz), (DG, i, dg), (IN, i, inv), (V, i, inv * F[i])]

    def sweep_row(i):
        return [(U, i, relaxed(i, V, F, IN, faces, 1))]

    def residual(i):
        here, off = off_sum(i, U, faces, 1)
        return F[i] - DG[i] * here + off

    def restrict_row(j):
        return [(T, j, residual(2 * j) + residual(2 * j + 1))]

    def level1_source(j):
        return [(F1, j, 0.125 * pair_sum_z(strided_pair(T, j, half_rows), 1))]

    def level1_coef(j):
        stores = []
        for src, dst in ((A, A1), (B, B1)):
            both = strided_pair(src, 2 * j, half_rows) + strided_pair(src, 2 * j + 1, half_rows)
            stores.append((dst, j, 0.125 * pair_sum_z(both, 1)))
        return stores

    def coef_row1(i):
        fx, fy, fz, dg, inv = coefficients(A1[i], B1[i], B1[i - 1], B1[i + 1], 2, 0.25)
        return [(FX1, i, fx), (FY1, i, fy), (FZ1, i, fz), (D1, i, dg), (IN1, i, inv), (W1, i, inv * F1[i])]

    def coarse_pack(k, ref, at, x):
        rows = half_rows // 2
        both = ref[at, pl.ds(0, rows, stride=2), :] + ref[at, pl.ds(1, rows, stride=2), :]
        value = 0.125 * pair_sum_z(both, 2)
        packed = jnp.zeros((1, LANES), jnp.float32)
        for y in range(depth2):
            packed = packed + jnp.where(lane % depth2 == y, value[own2 + y:own2 + y + 1], 0.0)
        return (coarse, pl.ds(k * count2 + x, 1), packed)

    return coef_row, sweep_row, restrict_row, level1_source, level1_coef, coef_row1, coarse_pack


def down_inner_kernel(*refs):
    y_even = refs[:len(FACE_PARTS)]
    y_odd = refs[len(FACE_PARTS):2 * len(FACE_PARTS)]
    *refs, T1 = refs[2 * len(FACE_PARTS) + 3:]
    F, A, B = frames = refs[:3]
    A1, B1 = refs[12:14]
    end = F.shape[0]
    depth = F.shape[1] - 2 * FRAME
    count = end - 2 * FRAME
    even = even_position()
    for k, x, layers, part, at in face_pieces(count)[0]:
        rows = slice(at, at + layers)
        below, above = below_above(even, y_even[part][rows], y_odd[part][rows])
        frames[k][FRAME + x, FRAME - layers:FRAME] = below
        frames[k][FRAME + x, FRAME + depth:FRAME + depth + layers] = above
    zero_y_edges(frames, depth)
    coef_row, sweep_row, restrict_row, level1_source, level1_coef, coef_row1, coarse_pack = down_rows(*refs)
    first1 = FRAME // 2
    end1 = end // 2
    rows_loop(FRAME + 1, end - FRAME - 1, 10, coef_row)
    rows_loop(FRAME + 2, end - FRAME - 2, 14, sweep_row)
    rows_loop(first1 + 2, end1 - first1 - 2, 6, restrict_row)
    rows_loop(first1 + 2, end1 - first1 - 2, 12, level1_source)
    rows_loop(first1, end1 - first1, 8, level1_coef)
    rows_loop(first1 + 2, end1 - first1 - 2, 12, coef_row1)
    count2 = count // 4

    def coarse_sum(x):
        i = first1 + 2 * x
        return [(T1, x, A1[i] + A1[i + 1]), (T1, count2 + x, B1[i] + B1[i + 1])]

    rows_loop(0, count2, 8, coarse_sum)

    def coarse_rows(x):
        return [coarse_pack(1, T1, x, x), coarse_pack(2, T1, count2 + x, x)]

    rows_loop(0, count2, 8, coarse_rows)


def zero_y_edges(frames, depth):
    position = box_position()
    for edge, y in (
        (position == 0, slice(0, FRAME)),
        (position == lax.axis_size("box") - 1, slice(FRAME + depth, FRAME + depth + FRAME)),
    ):

        @pl.when(edge)
        def _(y=y):
            for ref in frames:
                zero(ref, slice(None), y)


def down_kernel(x_even, x_odd, c_even, c_odd, *refs):
    refs = refs[21:]
    *refs, V1, to_even, to_odd, T1 = refs
    F, A, B = frames = refs[:3]
    FX = refs[3]
    F1, A1, B1, FX1, FY1, FZ1, D1, IN1, W1, coarse = refs[11:]
    count = F.shape[0] - 2 * FRAME
    depth = F.shape[1] - 2 * FRAME
    even = even_position()
    even_x = even_group()
    start = 0
    for k, wide in enumerate(WIDES):
        for layer in range(wide):
            below, above = below_above(even_x, x_even[start + layer], x_odd[start + layer])
            frames[k][FRAME - wide + layer, FRAME:FRAME + depth] = below
            frames[k][FRAME + count + layer, FRAME:FRAME + depth] = above
        start += wide
    starts = (0, WIDE_F, 2 * WIDE_F)
    for side, k, row, layers, at in corner_pieces()[0]:
        x = row - starts[k] + (FRAME + count if side else FRAME - WIDES[k])
        below, above = below_above(even, c_even[at:at + layers], c_odd[at:at + layers])
        frames[k][x, FRAME - layers:FRAME] = below
        frames[k][x, FRAME + depth:FRAME + depth + layers] = above
    zero_y_edges(frames, depth)
    group = lax.axis_index("grp")
    for edge, x in (
        (group == 0, slice(0, FRAME)),
        (group == lax.axis_size("grp") - 1, slice(FRAME + count, FRAME + count + FRAME)),
    ):

        @pl.when(edge)
        def _(x=x):
            for ref in frames:
                zero(ref, x)

    end = count + 2 * FRAME
    coef_row, sweep_row, restrict_row, level1_source, level1_coef, coef_row1, coarse_pack = down_rows(*refs)
    first1 = FRAME // 2
    end1 = end // 2
    FX[1] = 0.5 * (B[1] + B[2])
    for margin, fn in ((2, coef_row), (3, sweep_row)):
        rows_loop(margin, FRAME + margin - 1, 7, fn)
        rows_loop(end - FRAME - margin + 1, end - margin, 7, fn)
    for fn in (restrict_row, level1_source):
        rows_loop(2, first1 + 2, 4, fn)
        rows_loop(end1 - first1 - 2, end1 - 2, 4, fn)
    rows_loop(1, first1, 3, level1_coef)
    rows_loop(end1 - first1, end1 - 1, 3, level1_coef)
    FX1[1] = 0.125 * (B1[1] + B1[2])
    rows_loop(2, first1 + 2, 4, coef_row1)
    rows_loop(end1 - first1 - 2, end1 - 2, 4, coef_row1)

    faces1 = (FX1, FY1, FZ1)

    def sweep_row1(i):
        return [(V1, i, relaxed(i, W1, F1, IN1, faces1, 2))]

    rows_loop(3, end1 - 3, 18, sweep_row1)

    def residual1(i):
        here, off = off_sum(i, V1, faces1, 2)
        return F1[i] - D1[i] * here + off

    count1 = count // 2
    count2 = count // 4

    def coarse_row(x):
        i = first1 + 2 * x
        return [(T1, x, residual1(i) + residual1(i + 1))]

    rows_loop(0, count2, 8, coarse_row)

    def coarse_source(x):
        return [coarse_pack(0, T1, x, x)]

    rows_loop(0, count2, 8, coarse_source)

    own1 = slice(first1, first1 + depth // 2)
    for k in range(3):
        rows = slice(k * COARSE_X, (k + 1) * COARSE_X)
        up = coarse[(k + 1) * count2 - COARSE_X:(k + 1) * count2]
        down = coarse[k * count2:k * count2 + COARSE_X]
        to_odd[rows], to_even[rows] = below_above(even_x, up, down)
    for k in range(FINE_X):
        rows = slice(3 * COARSE_X + k * depth // 2, 3 * COARSE_X + (k + 1) * depth // 2)
        up = V1[first1 + count1 - FINE_X + k, own1]
        down = V1[first1 + k, own1]
        to_odd[rows], to_even[rows] = below_above(even_x, up, down)


def pack_coarse_kernel(coarse, v1, x_even, x_odd, far, to_even, to_odd, low, high):
    low[...], high[...] = below_above(even_group(), x_even[...], x_odd[...])
    count2 = coarse.shape[0] // 3
    first1 = FRAME // 2
    depth1 = v1.shape[1] - FRAME
    count1 = 2 * count2
    for k in range(3):
        row = k * COARSE_PITCH
        part = slice(k * COARSE_X, (k + 1) * COARSE_X)
        far[row:row + COARSE_X] = low[part]
        far[row + COARSE_X:row + COARSE_X + count2] = coarse[k * count2:(k + 1) * count2]
        far[row + COARSE_X + count2:row + 2 * COARSE_X + count2] = high[part]
    rows = far.shape[0]
    to_even[0:rows] = far[...]
    to_odd[0:rows] = far[...]
    even = even_position()
    tiles = [low[3 * COARSE_X + k * depth1:3 * COARSE_X + (k + 1) * depth1] for k in range(FINE_X)]
    tiles += [v1[first1 + k, first1:first1 + depth1] for k in range(count1)]
    tiles += [high[3 * COARSE_X + k * depth1:3 * COARSE_X + (k + 1) * depth1] for k in range(FINE_X)]
    for k, tile in enumerate(tiles):
        part = slice(rows + k * FINE_X, rows + (k + 1) * FINE_X)
        up = tile[depth1 - FINE_X:]
        down = tile[:FINE_X]
        to_odd[part], to_even[part] = below_above(even, up, down)


def coarse_solve(source, alpha, beta):
    shape = beta[0].shape
    lane = lane_ids(shape)
    first = lane % 4 == 0
    last = lane % 4 == 3
    inside = lane < LANES - 4
    nothing = jnp.zeros(shape, jnp.float32)

    def next_x(v):
        return pltpu.roll(v, shape[0] - 1, 0)

    def prev_x(v):
        return pltpu.roll(v, 1, 0)

    def next_y(vs):
        over = [pltpu.roll(v, 3, 1) for v in vs[1:]] + [nothing]
        return [jnp.where(last, o, pltpu.roll(v, LANES - 1, 1)) for o, v in zip(over, vs)]

    def prev_y(vs):
        over = [nothing] + [pltpu.roll(v, LANES - 3, 1) for v in vs[:-1]]
        return [jnp.where(first, o, pltpu.roll(v, 1, 1)) for o, v in zip(over, vs)]

    half = 0.5 * 0.0625
    coefs = []
    for a, b, b_next, b_prev in zip(alpha, beta, next_y(beta), prev_y(beta)):
        up_x = next_x(b)
        up_z = jnp.where(inside, z_next(b, 4), 0.0)
        down_z = jnp.where(lane >= 4, z_prev(b, 4), 0.0)
        total = (prev_x(b) + up_x) + (b_next + b_prev) + (up_z + down_z)
        diagonal = a + half * (6.0 * b + total)
        inverse = jnp.where(a > 0.0, OMEGA / diagonal, 0.0)
        face_z = jnp.where(inside, half * (b + up_z), 0.0)
        coefs.append((half * (b + up_x), half * (b + b_next), face_z, inverse))
    field = [c[3] * f for c, f in zip(coefs, source)]
    for _ in range(3):
        flux = prev_y([c[1] * v for c, v in zip(coefs, field)])
        new = []
        for (fx, fy, fz, inverse), v, v_next, back, f in zip(coefs, field, next_y(field), flux, source):
            off = fx * next_x(v) + prev_x(fx * v)
            off = off + (fy * v_next + back)
            off = off + (fz * z_next(v, 4) + z_prev(fz * v, 4))
            new.append((1.0 - OMEGA) * v + inverse * (f + off))
        field = new
    return field


def up_kernel(
    near_even, near_odd, far_even, far_odd, own, x_even, x_odd,
    in_v, F, IN, FX, FY, FZ,
    in_v1, F1, IN1, FX1, FY1, FZ1,
    out,
    V, U, V1, U1, C2, P0, result, sems,
):
    group = lax.axis_index("grp")
    position = box_position()
    even = position % 2 == 0
    last_group = lax.axis_size("grp") - 1
    last_block = lax.axis_size("box") - 1
    count, depth = result.shape[:2]

    row2 = lax.broadcasted_iota(jnp.int32, (COARSE_PITCH, LANES), 0) - COARSE_X + group * (count // 4)
    in_x = (row2 >= 0) & (row2 < (last_group + 1) * (count // 4))
    arrays = []
    for k in range(3):
        rows = pl.ds(k * COARSE_PITCH, COARSE_PITCH)
        ne, no, fe, fo = near_even[rows], near_odd[rows], far_even[rows], far_odd[rows]
        near_low, near_high = below_above(even, ne, no)
        far_low, far_high = below_above(even, fe, fo)
        blocks = (far_low, near_low, own[rows], near_high, far_high)
        column = []
        for at, value in enumerate(blocks):
            place = position + (at - 2)
            column.append(jnp.where(in_x & ((place >= 0) & (place <= last_block)), value, 0.0))
        arrays.append(column)
    field2 = coarse_solve(*arrays)
    for at in range(3):
        C2[at] = field2[1 + at]

    first1 = FRAME // 2
    depth1 = depth // 2
    span1 = V1.shape[0]
    rows1 = V1.shape[1]
    own_rows = pl.ds(first1, depth1)

    def own_row(x):
        i = first1 + x
        return [(V1, (i, own_rows), in_v1[i, own_rows])]

    rows_loop(0, span1 - 2 * first1, 16, own_row)
    for k in range(FINE_X):
        tile = pl.ds(3 * COARSE_X + k * depth1, depth1)
        below, above = below_above(even_group(), x_even[tile], x_odd[tile])
        V1[first1 - FINE_X + k, own_rows] = below
        V1[span1 - first1 + k, own_rows] = above

    rim = own.shape[0]

    def rim_row(x):
        i = x + first1 - FINE_X
        part = pl.ds(rim + FINE_X * x, FINE_X)
        near_low, near_high = below_above(even, near_even[part], near_odd[part])
        return [
            (V1, (i, slice(first1 - FINE_X, first1)), jnp.where(position > 0, near_low, 0.0)),
            (
                V1,
                (i, slice(first1 + depth1, first1 + depth1 + FINE_X)),
                jnp.where(position < last_block, near_high, 0.0),
            ),
        ]

    rows_loop(0, span1 - 2 * (first1 - FINE_X), 22, rim_row)
    for edge, rows in ((group == 0, slice(0, first1)), (group == last_group, slice(span1 - first1, span1))):

        @pl.when(edge)
        def _(rows=rows):
            zero(V1, rows)

    sub = lax.broadcasted_iota(jnp.int32, (rows1, LANES), 0)
    lane = lane_ids((rows1, LANES))
    block = (sub + 4) // 8
    spread = lane - lane % 4 + (sub // 2 + 2) % 4

    def corrected_row(x):
        row = pl.ds(x + COARSE_X - first1 // 2, 1)
        t = jnp.broadcast_to(C2[0, row], (rows1, LANES))
        for at in range(1, 3):
            t = jnp.where(block == at, jnp.broadcast_to(C2[at, row], (rows1, LANES)), t)
        t = jnp.take_along_axis(t, spread, axis=1)
        return [(V1, 2 * x + k, V1[2 * x + k] + t) for k in range(2)]

    rows_loop(0, span1 // 2, 12, corrected_row)
    faces1 = (FX1, FY1, FZ1)

    def sweep_a1(i):
        return [(U1, i, relaxed(i, V1, F1, IN1, faces1, 2))]

    rows_loop(2, span1 - 2, 10, sweep_a1)

    def sweep_b1(i):
        return [(V1, i, relaxed(i, U1, F1, IN1, faces1, 2))]

    rows_loop(3, span1 - 3, 18, sweep_b1)

    span = V.shape[0]
    start = FRAME - 2

    def widen(x):
        row = V1[x + start // 2]
        return [(P0, (x, pl.ds(k, rows1, stride=2)), row) for k in range(2)]

    rows_loop(0, (span - 2 * start) // 2, 18, widen)

    def corrected0(x):
        add = P0[x]
        i = start + 2 * x
        return [(V, i + k, in_v[i + k] + add) for k in range(2)]

    rows_loop(0, (span - 2 * start) // 2, 9, corrected0)
    faces = (FX, FY, FZ)

    def sweep_a(i):
        return [(U, i, relaxed(i, V, F, IN, faces, 1))]

    rows_loop(start + 1, span - start - 1, 17, sweep_a)

    def sweep_b(i):
        return [(result, i - FRAME, relaxed(i, U, F, IN, faces, 1)[FRAME:FRAME + depth])]

    chunk = count // 4
    copies = []
    for k in range(4):
        rows_loop(FRAME + k * chunk, FRAME + (k + 1) * chunk, chunk, sweep_b)
        rows = pl.ds(k * chunk, chunk)
        copies.append(pltpu.make_async_copy(result.at[rows], out.at[rows], sems.at[k]))
        copies[-1].start()
    wait_copies(copies)


def body(source, alpha, beta):
    f = source[:, 0]
    a = alpha[:, 0]
    b = beta[:, 0]
    count, depth, lanes = f.shape
    groups = lax.axis_size("grp")
    blocks = lax.axis_size("box")
    code = [p ^ (p >> 1) for p in range(blocks)]

    def moved(array, target):
        def index(g, p):
            return g * blocks + code[p]

        pairs = [(index(g, p), index(*target(g, p))) for g in range(groups) for p in range(blocks)]
        return lax.ppermute(array, ("grp", "box"), pairs)

    def odd_partner(at, size):
        other = at + 1 if at % 2 else at - 1
        return other if 0 <= other < size else None

    def x_even(g, p):
        return g ^ 1, p

    def x_odd(g, p):
        other = odd_partner(g, groups)
        return (g, p ^ 1) if other is None else (other, p)

    def y_even(g, p):
        return g, p ^ 1

    def y_odd(g, p):
        other = odd_partner(p, blocks)
        return (g ^ (groups // 2), p) if other is None else (g, other)

    def far_even(g, p):
        other = p + 2 if p % 2 else p - 2
        return g, other if 0 <= other < blocks else p ^ 1

    def far_odd(g, p):
        other = p - 2 if p % 2 else p + 2
        return g, other if 0 <= other < blocks else p ^ 1

    def arr(*shape):
        return jax.ShapeDtypeStruct(shape, jnp.float32)

    def vm(*shape):
        return pltpu.VMEM(shape, jnp.float32)

    dma = pltpu.SemaphoreType.DMA
    x_rows = 2 * WIDE_F + WIDE_B
    framed = (count + 2 * FRAME, depth + 2 * FRAME, lanes)
    y_parts = [arr(rows, lanes) for rows in face_pieces(count)[1]]
    parts = len(y_parts)
    c_rows = corner_pieces()[1]
    frame_f, frame_a, frame_b, to_x_even, to_x_odd, *to_y = pl.pallas_call(
        pack_faces_kernel,
        out_shape=[arr(*framed)] * 3 + [arr(x_rows, depth, lanes)] * 2 + y_parts * 2,
        in_specs=[HBM] * 3,
        out_specs=[VMEM] * (5 + 2 * parts),
        scratch_shapes=[dma((3,))],
        compiler_params=params(),
    )(*[pltpu.with_memory_space_constraint(t, pltpu.HBM) for t in (f, a, b)])
    x_halo = moved(to_x_even, x_even), moved(to_x_odd, x_odd)
    y_halo = [moved(t, y_even) for t in to_y[:parts]] + [moved(t, y_odd) for t in to_y[parts:]]

    to_even, to_odd = pl.pallas_call(
        pack_corners_kernel,
        out_shape=[arr(c_rows, lanes)] * 2,
        in_specs=[VMEM] * 2,
        out_specs=[VMEM] * 2,
        compiler_params=params(),
    )(*x_halo)
    corners = moved(to_even, y_even), moved(to_odd, y_odd)

    framed1 = (framed[0] // 2, framed[1] // 2, lanes)
    count2 = count // 4
    passed = [arr(*framed)] * 10 + [arr(framed1[0], framed[1], lanes)] + [arr(*framed1)] * 9 + [arr(3 * count2, lanes)]
    passed = pl.pallas_call(
        down_inner_kernel,
        out_shape=passed,
        in_specs=[VMEM] * (2 * parts + 3),
        out_specs=[VMEM] * 21,
        input_output_aliases={2 * parts + k: k for k in range(3)},
        scratch_shapes=[vm(2 * count2, framed1[1], lanes)],
        compiler_params=params(),
    )(*y_halo, frame_f, frame_a, frame_b)
    x2_rows = 3 * COARSE_X + FINE_X * depth // 2
    x2_rows += -x2_rows % 8
    results = pl.pallas_call(
        down_kernel,
        out_shape=[arr(*t.shape) for t in passed] + [arr(*framed1)] + [arr(x2_rows, lanes)] * 2,
        in_specs=[VMEM] * 25,
        out_specs=[VMEM] * 24,
        input_output_aliases={4 + k: k for k in range(21)},
        scratch_shapes=[vm(count2, framed1[1], lanes)],
        compiler_params=params(),
    )(*x_halo, *corners, *passed)
    F, _, _, FX, FY, FZ, _, IN, _, U, _, F1, _, _, FX1, FY1, FZ1, _, IN1, _, coarse, V1, to_even, to_odd = results

    x_halo = moved(to_even, x_even), moved(to_odd, x_odd)
    far_rows = 3 * COARSE_PITCH
    near_rows = far_rows + FINE_X * (count // 2 + 2 * FINE_X)
    near_rows += -near_rows % 8
    far, to_even, to_odd = pl.pallas_call(
        pack_coarse_kernel,
        out_shape=[arr(far_rows, lanes)] + [arr(near_rows, lanes)] * 2,
        in_specs=[VMEM] * 4,
        out_specs=[VMEM] * 3,
        scratch_shapes=[vm(x2_rows, lanes)] * 2,
        compiler_params=params(),
    )(coarse, V1, *x_halo)
    near = moved(to_even, y_even), moved(to_odd, y_odd)
    distant = moved(far, far_even), moved(far, far_odd)

    out = pl.pallas_call(
        up_kernel,
        out_shape=arr(count, depth, lanes),
        in_specs=[VMEM] * 19,
        out_specs=HBM,
        scratch_shapes=[vm(*framed)] * 2 + [vm(*framed1)] * 2
        + [vm(3, COARSE_PITCH, lanes), vm(count // 2 + 2, framed[1], lanes), vm(count, depth, lanes), dma((4,))],
        compiler_params=params(),
    )(
        *near, *distant, far, *x_halo,
        U, F, IN, FX, FY, FZ, V1, F1, IN1, FX1, FY1, FZ1,
    )
    return out[:, None]


def solution(mesh):
    spec = P("grp", "box", None, None)
    return jax.shard_map(body, mesh=mesh, in_specs=(spec,) * 3, out_specs=spec, check_vma=False)
```

```python
import jax
import jax.numpy as jnp
from jax import lax
from jax.experimental import pallas as pl
from jax.experimental.pallas import tpu as pltpu
from jax.sharding import PartitionSpec as P

OMEGA = 0.7
FRAME = 8
WIDE_F = 6
WIDE_B = 7
COARSE_PITCH = 24
FAR_X = 4
COARSE_X = 6
FINE_X = 3
LANES = 128
ANY = pl.BlockSpec(memory_space=pl.ANY)
HBM = pl.BlockSpec(memory_space=pltpu.HBM)
VMEM = pl.BlockSpec(memory_space=pltpu.VMEM)
LIMIT = 16 * 1024 * 1024


def params():
    return pltpu.CompilerParams(vmem_limit_bytes=LIMIT)


def gray_position(code, bit_count):
    position = code
    for shift in range(1, bit_count):
        position = position ^ (code >> shift)
    return position


def box_position():
    bit_count = lax.axis_size("box").bit_length() - 1
    return gray_position(lax.axis_index("box"), bit_count)


def even_position():
    return box_position() % 2 == 0


def even_group():
    return lax.axis_index("grp") % 2 == 0


def below_above(even, from_even, from_odd):
    return jnp.where(even, from_odd, from_even), jnp.where(even, from_even, from_odd)


def run_copies(pairs, sems):
    copies = [pltpu.make_async_copy(src, dst, sems.at[at]) for at, (src, dst) in enumerate(pairs)]
    for copy in copies:
        copy.start()
    return copies


def wait_copies(copies):
    for copy in copies:
        copy.wait()


def lane_ids(shape):
    return lax.broadcasted_iota(jnp.int32, shape, 1)


def y_next(row):
    return pltpu.roll(row, row.shape[0] - 1, 0)


def y_prev(row):
    return pltpu.roll(row, 1, 0)


def z_next(row, dist):
    return pltpu.roll(row, LANES - dist, 1)


def z_prev(row, dist):
    return pltpu.roll(row, dist, 1)


def coefficients(alpha, beta, beta_prev, beta_next, dist, scale):
    half = 0.5 * scale
    lane = lane_ids(beta.shape)
    inside = lane < LANES - dist
    up_z = jnp.where(inside, z_next(beta, dist), 0.0)
    down_z = jnp.where(lane >= dist, z_prev(beta, dist), 0.0)
    up_y = y_next(beta)
    face_x = half * (beta + beta_next)
    face_y = half * (beta + up_y)
    face_z = jnp.where(inside, half * (beta + up_z), 0.0)
    total = (beta_prev + beta_next) + (up_y + y_prev(beta)) + (up_z + down_z)
    diagonal = alpha + half * (6.0 * beta + total)
    inverse = jnp.where(alpha > 0.0, OMEGA / diagonal, 0.0)
    return face_x, face_y, face_z, diagonal, inverse


def off_sum(at, v, faces, dist):
    face_x, face_y, face_z = faces
    here = v[at]
    fy = face_y[at]
    fz = face_z[at]
    along_x = face_x[at] * v[at + 1] + face_x[at - 1] * v[at - 1]
    along_y = fy * y_next(here) + y_prev(fy * here)
    along_z = fz * z_next(here, dist) + z_prev(fz * here, dist)
    return here, along_x + along_y + along_z


def relaxed(at, v, f, inverse, faces, dist):
    here, off = off_sum(at, v, faces, dist)
    return (1.0 - OMEGA) * here + inverse[at] * (f[at] + off)


def rows_loop(low, high, step, fn):
    trips = (high - low) // step

    def run(rows):
        stores = [item for row in rows for item in fn(row)]
        for ref, at, value in stores:
            ref[at] = value

    def trip(t, carry):
        base = low + t * step
        run([base + k for k in range(step)])
        return carry

    if trips <= 4:
        for t in range(trips):
            run([low + t * step + k for k in range(step)])
    else:
        lax.fori_loop(0, trips, trip, 0)
    rest = list(range(low + trips * step, high))
    if rest:
        run(rest)


def pair_sum_z(row, dist):
    lane = lane_ids(row.shape)
    return row + jnp.take_along_axis(row, lane ^ dist, axis=1)


def strided_pair(ref, at, count):
    return ref[at, pl.ds(0, count, stride=2), :] + ref[at, pl.ds(1, count, stride=2), :]


def zero(ref, *at):
    ref[at] = jnp.zeros_like(ref[at])


WIDES = (WIDE_F, WIDE_F, WIDE_B)


FACE_PARTS = ((0, 1), (2,))


def face_pieces(count):
    pieces = []
    sizes = []
    for part, arrays in enumerate(FACE_PARTS):
        at = 0
        for k in arrays:
            for x in range(count):
                pieces.append((k, x, WIDES[k], part, at))
                at += WIDES[k]
        sizes.append(at + -at % 8)
    return pieces, sizes


def corner_pieces():
    pieces = []
    at = 0
    for side in range(2):
        start = 0
        for k, wide in enumerate(WIDES):
            for layer in range(wide):
                distance = layer + 1 if side else wide - layer
                layers = min(wide, wide + 2 - distance)
                pieces.append((side, k, start + layer, layers, at))
                at += layers
            start += wide
    return pieces, at + -at % 8


def pack_faces_kernel(f, a, b, F, A, B, x_even, x_odd, *rest):
    *y_faces, sems = rest
    y_even = y_faces[:len(FACE_PARTS)]
    y_odd = y_faces[len(FACE_PARTS):]
    count, depth = f.shape[:2]
    own = (pl.ds(FRAME, count), pl.ds(FRAME, depth))
    frames = (F, A, B)
    copies = run_copies([(src, dst.at[own]) for src, dst in zip((f, a, b), frames)], sems)
    pieces, _ = face_pieces(count)
    even = even_position()
    even_x = even_group()
    row = 0
    for k, (ref, wide) in enumerate(zip(frames, WIDES)):
        copies[k].wait()
        for layer in range(wide):
            up = ref[FRAME + count - wide + layer, FRAME:FRAME + depth]
            down = ref[FRAME + layer, FRAME:FRAME + depth]
            x_odd[row + layer], x_even[row + layer] = below_above(even_x, up, down)
        row += wide
        for at_k, x, layers, part, at in pieces:
            if at_k == k:
                up = ref[FRAME + x, FRAME + depth - layers:FRAME + depth]
                down = ref[FRAME + x, FRAME:FRAME + layers]
                rows = slice(at, at + layers)
                y_odd[part][rows], y_even[part][rows] = below_above(even, up, down)


def pack_corners_kernel(x_even, x_odd, to_even, to_odd):
    depth = x_even.shape[1]
    even = even_position()
    even_x = even_group()
    for side, _, row, layers, at in corner_pieces()[0]:
        up_rows = slice(depth - layers, depth)
        up = below_above(even_x, x_even[row, up_rows], x_odd[row, up_rows])[side]
        down = below_above(even_x, x_even[row, 0:layers], x_odd[row, 0:layers])[side]
        to_odd[at:at + layers], to_even[at:at + layers] = below_above(even, up, down)


def down_rows(F, A, B, FX, FY, FZ, DG, IN, V, U, T, F1, A1, B1, FX1, FY1, FZ1, D1, IN1, W1, coarse):
    faces = (FX, FY, FZ)
    half_rows = F1.shape[1]
    count2 = coarse.shape[0] // 3
    first1 = FRAME // 2
    own2 = FRAME // 4
    depth2 = half_rows // 2 - 2 * own2
    lane = lane_ids((1, LANES))

    def coef_row(i):
        fx, fy, fz, dg, inv = coefficients(A[i], B[i], B[i - 1], B[i + 1], 1, 1.0)
        return [(FX, i, fx), (FY, i, fy), (FZ, i, fz), (DG, i, dg), (IN, i, inv), (V, i, inv * F[i])]

    def sweep_row(i):
        return [(U, i, relaxed(i, V, F, IN, faces, 1))]

    def residual(i):
        here, off = off_sum(i, U, faces, 1)
        return F[i] - DG[i] * here + off

    def restrict_row(j):
        return [(T, j, residual(2 * j) + residual(2 * j + 1))]

    def level1_source(j):
        return [(F1, j, 0.125 * pair_sum_z(strided_pair(T, j, half_rows), 1))]

    def level1_coef(j):
        stores = []
        for src, dst in ((A, A1), (B, B1)):
            both = strided_pair(src, 2 * j, half_rows) + strided_pair(src, 2 * j + 1, half_rows)
            stores.append((dst, j, 0.125 * pair_sum_z(both, 1)))
        return stores

    def coef_row1(i):
        fx, fy, fz, dg, inv = coefficients(A1[i], B1[i], B1[i - 1], B1[i + 1], 2, 0.25)
        return [(FX1, i, fx), (FY1, i, fy), (FZ1, i, fz), (D1, i, dg), (IN1, i, inv), (W1, i, inv * F1[i])]

    def coarse_pack(k, ref, at, x):
        rows = half_rows // 2
        both = ref[at, pl.ds(0, rows, stride=2), :] + ref[at, pl.ds(1, rows, stride=2), :]
        value = 0.125 * pair_sum_z(both, 2)
        packed = jnp.zeros((1, LANES), jnp.float32)
        for y in range(depth2):
            packed = packed + jnp.where(lane % depth2 == y, value[own2 + y:own2 + y + 1], 0.0)
        return (coarse, pl.ds(k * count2 + x, 1), packed)

    return coef_row, sweep_row, restrict_row, level1_source, level1_coef, coef_row1, coarse_pack


def down_inner_kernel(*refs):
    y_even = refs[:len(FACE_PARTS)]
    y_odd = refs[len(FACE_PARTS):2 * len(FACE_PARTS)]
    *refs, T1 = refs[2 * len(FACE_PARTS) + 3:]
    F, A, B = frames = refs[:3]
    A1, B1 = refs[12:14]
    end = F.shape[0]
    depth = F.shape[1] - 2 * FRAME
    count = end - 2 * FRAME
    even = even_position()
    for k, x, layers, part, at in face_pieces(count)[0]:
        rows = slice(at, at + layers)
        below, above = below_above(even, y_even[part][rows], y_odd[part][rows])
        frames[k][FRAME + x, FRAME - layers:FRAME] = below
        frames[k][FRAME + x, FRAME + depth:FRAME + depth + layers] = above
    zero_y_edges(frames, depth)
    coef_row, sweep_row, restrict_row, level1_source, level1_coef, coef_row1, coarse_pack = down_rows(*refs)
    first1 = FRAME // 2
    end1 = end // 2
    rows_loop(FRAME + 1, end - FRAME - 1, 10, coef_row)
    rows_loop(FRAME + 2, end - FRAME - 2, 14, sweep_row)
    rows_loop(first1 + 2, end1 - first1 - 2, 6, restrict_row)
    rows_loop(first1 + 2, end1 - first1 - 2, 12, level1_source)
    rows_loop(first1, end1 - first1, 8, level1_coef)
    rows_loop(first1 + 2, end1 - first1 - 2, 12, coef_row1)
    count2 = count // 4

    def coarse_sum(x):
        i = first1 + 2 * x
        return [(T1, x, A1[i] + A1[i + 1]), (T1, count2 + x, B1[i] + B1[i + 1])]

    rows_loop(0, count2, 8, coarse_sum)

    def coarse_rows(x):
        return [coarse_pack(1, T1, x, x), coarse_pack(2, T1, count2 + x, x)]

    rows_loop(0, count2, 8, coarse_rows)


def zero_y_edges(frames, depth):
    position = box_position()
    for edge, y in (
        (position == 0, slice(0, FRAME)),
        (position == lax.axis_size("box") - 1, slice(FRAME + depth, FRAME + depth + FRAME)),
    ):

        @pl.when(edge)
        def _(y=y):
            for ref in frames:
                zero(ref, slice(None), y)


def down_kernel(x_even, x_odd, c_even, c_odd, *refs):
    refs = refs[21:]
    *refs, V1, to_even, to_odd, T1 = refs
    F, A, B = frames = refs[:3]
    FX = refs[3]
    F1, A1, B1, FX1, FY1, FZ1, D1, IN1, W1, coarse = refs[11:]
    count = F.shape[0] - 2 * FRAME
    depth = F.shape[1] - 2 * FRAME
    even = even_position()
    even_x = even_group()
    start = 0
    for k, wide in enumerate(WIDES):
        for layer in range(wide):
            below, above = below_above(even_x, x_even[start + layer], x_odd[start + layer])
            frames[k][FRAME - wide + layer, FRAME:FRAME + depth] = below
            frames[k][FRAME + count + layer, FRAME:FRAME + depth] = above
        start += wide
    starts = (0, WIDE_F, 2 * WIDE_F)
    for side, k, row, layers, at in corner_pieces()[0]:
        x = row - starts[k] + (FRAME + count if side else FRAME - WIDES[k])
        below, above = below_above(even, c_even[at:at + layers], c_odd[at:at + layers])
        frames[k][x, FRAME - layers:FRAME] = below
        frames[k][x, FRAME + depth:FRAME + depth + layers] = above
    zero_y_edges(frames, depth)
    group = lax.axis_index("grp")
    for edge, x in (
        (group == 0, slice(0, FRAME)),
        (group == lax.axis_size("grp") - 1, slice(FRAME + count, FRAME + count + FRAME)),
    ):

        @pl.when(edge)
        def _(x=x):
            for ref in frames:
                zero(ref, x)

    end = count + 2 * FRAME
    coef_row, sweep_row, restrict_row, level1_source, level1_coef, coef_row1, coarse_pack = down_rows(*refs)
    first1 = FRAME // 2
    end1 = end // 2
    FX[1] = 0.5 * (B[1] + B[2])
    for margin, fn in ((2, coef_row), (3, sweep_row)):
        rows_loop(margin, FRAME + margin - 1, 7, fn)
        rows_loop(end - FRAME - margin + 1, end - margin, 7, fn)
    for fn in (restrict_row, level1_source):
        rows_loop(2, first1 + 2, 4, fn)
        rows_loop(end1 - first1 - 2, end1 - 2, 4, fn)
    rows_loop(1, first1, 3, level1_coef)
    rows_loop(end1 - first1, end1 - 1, 3, level1_coef)
    FX1[1] = 0.125 * (B1[1] + B1[2])
    rows_loop(2, first1 + 2, 4, coef_row1)
    rows_loop(end1 - first1 - 2, end1 - 2, 4, coef_row1)

    faces1 = (FX1, FY1, FZ1)

    def sweep_row1(i):
        return [(V1, i, relaxed(i, W1, F1, IN1, faces1, 2))]

    rows_loop(3, end1 - 3, 18, sweep_row1)

    def residual1(i):
        here, off = off_sum(i, V1, faces1, 2)
        return F1[i] - D1[i] * here + off

    count1 = count // 2
    count2 = count // 4

    def coarse_row(x):
        i = first1 + 2 * x
        return [(T1, x, residual1(i) + residual1(i + 1))]

    rows_loop(0, count2, 8, coarse_row)

    def coarse_source(x):
        return [coarse_pack(0, T1, x, x)]

    rows_loop(0, count2, 8, coarse_source)

    own1 = slice(first1, first1 + depth // 2)
    for k in range(3):
        rows = slice(k * COARSE_X, (k + 1) * COARSE_X)
        up = coarse[(k + 1) * count2 - COARSE_X:(k + 1) * count2]
        down = coarse[k * count2:k * count2 + COARSE_X]
        to_odd[rows], to_even[rows] = below_above(even_x, up, down)
    for k in range(FINE_X):
        rows = slice(3 * COARSE_X + k * depth // 2, 3 * COARSE_X + (k + 1) * depth // 2)
        up = V1[first1 + count1 - FINE_X + k, own1]
        down = V1[first1 + k, own1]
        to_odd[rows], to_even[rows] = below_above(even_x, up, down)


def pack_coarse_kernel(coarse, v1, x_even, x_odd, far, to_even, to_odd, low, high):
    low[...], high[...] = below_above(even_group(), x_even[...], x_odd[...])
    count2 = coarse.shape[0] // 3
    first1 = FRAME // 2
    depth1 = v1.shape[1] - FRAME
    count1 = 2 * count2
    for k in range(3):
        row = k * COARSE_PITCH
        part = slice(k * COARSE_X, (k + 1) * COARSE_X)
        to_even[row:row + COARSE_X] = low[part]
        to_even[row + COARSE_X:row + COARSE_X + count2] = coarse[k * count2:(k + 1) * count2]
        to_even[row + COARSE_X + count2:row + 2 * COARSE_X + count2] = high[part]
        size = count2 + 2 * FAR_X
        first = row + COARSE_X - FAR_X
        far[k * size:(k + 1) * size] = to_even[first:first + size]
    rows = 3 * COARSE_PITCH
    to_odd[0:rows] = to_even[0:rows]
    even = even_position()
    tiles = [low[3 * COARSE_X + k * depth1:3 * COARSE_X + (k + 1) * depth1] for k in range(FINE_X)]
    tiles += [v1[first1 + k, first1:first1 + depth1] for k in range(count1)]
    tiles += [high[3 * COARSE_X + k * depth1:3 * COARSE_X + (k + 1) * depth1] for k in range(FINE_X)]
    for k, tile in enumerate(tiles):
        part = slice(rows + k * FINE_X, rows + (k + 1) * FINE_X)
        up = tile[depth1 - FINE_X:]
        down = tile[:FINE_X]
        to_odd[part], to_even[part] = below_above(even, up, down)


def coarse_solve(source, alpha, beta):
    shape = beta[0].shape
    lane = lane_ids(shape)
    first = lane % 4 == 0
    last = lane % 4 == 3
    inside = lane < LANES - 4
    nothing = jnp.zeros(shape, jnp.float32)

    def next_x(v):
        return pltpu.roll(v, shape[0] - 1, 0)

    def prev_x(v):
        return pltpu.roll(v, 1, 0)

    def next_y(vs):
        over = [pltpu.roll(v, 3, 1) for v in vs[1:]] + [nothing]
        return [jnp.where(last, o, pltpu.roll(v, LANES - 1, 1)) for o, v in zip(over, vs)]

    def prev_y(vs):
        over = [nothing] + [pltpu.roll(v, LANES - 3, 1) for v in vs[:-1]]
        return [jnp.where(first, o, pltpu.roll(v, 1, 1)) for o, v in zip(over, vs)]

    half = 0.5 * 0.0625
    coefs = []
    for a, b, b_next, b_prev in zip(alpha, beta, next_y(beta), prev_y(beta)):
        up_x = next_x(b)
        up_z = jnp.where(inside, z_next(b, 4), 0.0)
        down_z = jnp.where(lane >= 4, z_prev(b, 4), 0.0)
        total = (prev_x(b) + up_x) + (b_next + b_prev) + (up_z + down_z)
        diagonal = a + half * (6.0 * b + total)
        inverse = jnp.where(a > 0.0, OMEGA / diagonal, 0.0)
        face_z = jnp.where(inside, half * (b + up_z), 0.0)
        coefs.append((half * (b + up_x), half * (b + b_next), face_z, inverse))
    field = [c[3] * f for c, f in zip(coefs, source)]
    for _ in range(3):
        flux = prev_y([c[1] * v for c, v in zip(coefs, field)])
        new = []
        for (fx, fy, fz, inverse), v, v_next, back, f in zip(coefs, field, next_y(field), flux, source):
            off = fx * next_x(v) + prev_x(fx * v)
            off = off + (fy * v_next + back)
            off = off + (fz * z_next(v, 4) + z_prev(fz * v, 4))
            new.append((1.0 - OMEGA) * v + inverse * (f + off))
        field = new
    return field


def up_kernel(
    near_even, near_odd, far_even, far_odd, own, x_even, x_odd,
    in_v, F, IN, FX, FY, FZ,
    in_v1, F1, IN1, FX1, FY1, FZ1,
    out,
    V, U, V1, U1, C2, P0, R2, result, sems,
):
    group = lax.axis_index("grp")
    position = box_position()
    even = position % 2 == 0
    last_group = lax.axis_size("grp") - 1
    last_block = lax.axis_size("box") - 1
    count, depth = result.shape[:2]

    row2 = lax.broadcasted_iota(jnp.int32, (COARSE_PITCH, LANES), 0) - COARSE_X + group * (count // 4)
    in_x = (row2 >= 0) & (row2 < (last_group + 1) * (count // 4))
    arrays = []
    for k in range(3):
        rows = pl.ds(k * COARSE_PITCH, COARSE_PITCH)
        near_low, near_high = below_above(even, near_even[rows], near_odd[rows])
        size = count // 4 + 2 * FAR_X
        far_rows = pl.ds(k * size, size)
        for at, value in enumerate(below_above(even, far_even[far_rows], far_odd[far_rows])):
            R2[at, k] = jnp.zeros((COARSE_PITCH, LANES), jnp.float32)
            R2[at, k, COARSE_X - FAR_X:COARSE_X - FAR_X + size] = value
        blocks = (R2[0, k], near_low, own[rows], near_high, R2[1, k])
        column = []
        for at, value in enumerate(blocks):
            place = position + (at - 2)
            column.append(jnp.where(in_x & ((place >= 0) & (place <= last_block)), value, 0.0))
        arrays.append(column)
    field2 = coarse_solve(*arrays)
    for at in range(3):
        C2[at] = field2[1 + at]

    first1 = FRAME // 2
    depth1 = depth // 2
    span1 = V1.shape[0]
    rows1 = V1.shape[1]
    own_rows = pl.ds(first1, depth1)

    def own_row(x):
        i = first1 + x
        return [(V1, (i, own_rows), in_v1[i, own_rows])]

    rows_loop(0, span1 - 2 * first1, 16, own_row)
    for k in range(FINE_X):
        tile = pl.ds(3 * COARSE_X + k * depth1, depth1)
        below, above = below_above(even_group(), x_even[tile], x_odd[tile])
        V1[first1 - FINE_X + k, own_rows] = below
        V1[span1 - first1 + k, own_rows] = above

    rim = 3 * COARSE_PITCH

    def rim_row(x):
        i = x + first1 - FINE_X
        part = pl.ds(rim + FINE_X * x, FINE_X)
        near_low, near_high = below_above(even, near_even[part], near_odd[part])
        return [
            (V1, (i, slice(first1 - FINE_X, first1)), jnp.where(position > 0, near_low, 0.0)),
            (
                V1,
                (i, slice(first1 + depth1, first1 + depth1 + FINE_X)),
                jnp.where(position < last_block, near_high, 0.0),
            ),
        ]

    rows_loop(0, span1 - 2 * (first1 - FINE_X), 22, rim_row)
    for edge, rows in ((group == 0, slice(0, first1)), (group == last_group, slice(span1 - first1, span1))):

        @pl.when(edge)
        def _(rows=rows):
            zero(V1, rows)

    sub = lax.broadcasted_iota(jnp.int32, (rows1, LANES), 0)
    lane = lane_ids((rows1, LANES))
    block = (sub + 4) // 8
    spread = lane - lane % 4 + (sub // 2 + 2) % 4

    def corrected_row(x):
        row = pl.ds(x + COARSE_X - first1 // 2, 1)
        t = jnp.broadcast_to(C2[0, row], (rows1, LANES))
        for at in range(1, 3):
            t = jnp.where(block == at, jnp.broadcast_to(C2[at, row], (rows1, LANES)), t)
        t = jnp.take_along_axis(t, spread, axis=1)
        return [(V1, 2 * x + k, V1[2 * x + k] + t) for k in range(2)]

    rows_loop(0, span1 // 2, 12, corrected_row)
    faces1 = (FX1, FY1, FZ1)

    def sweep_a1(i):
        return [(U1, i, relaxed(i, V1, F1, IN1, faces1, 2))]

    rows_loop(2, span1 - 2, 10, sweep_a1)

    def sweep_b1(i):
        return [(V1, i, relaxed(i, U1, F1, IN1, faces1, 2))]

    rows_loop(3, span1 - 3, 18, sweep_b1)

    span = V.shape[0]
    start = FRAME - 2

    def widen(x):
        row = V1[x + start // 2]
        return [(P0, (x, pl.ds(k, rows1, stride=2)), row) for k in range(2)]

    rows_loop(0, (span - 2 * start) // 2, 18, widen)

    def corrected0(x):
        add = P0[x]
        i = start + 2 * x
        return [(V, i + k, in_v[i + k] + add) for k in range(2)]

    rows_loop(0, (span - 2 * start) // 2, 9, corrected0)
    faces = (FX, FY, FZ)

    def sweep_a(i):
        return [(U, i, relaxed(i, V, F, IN, faces, 1))]

    rows_loop(start + 1, span - start - 1, 17, sweep_a)

    def sweep_b(i):
        return [(result, i - FRAME, relaxed(i, U, F, IN, faces, 1)[FRAME:FRAME + depth])]

    chunk = count // 4
    copies = []
    for k in range(4):
        rows_loop(FRAME + k * chunk, FRAME + (k + 1) * chunk, chunk, sweep_b)
        rows = pl.ds(k * chunk, chunk)
        copies.append(pltpu.make_async_copy(result.at[rows], out.at[rows], sems.at[k]))
        copies[-1].start()
    wait_copies(copies)


def body(source, alpha, beta):
    f = source[:, 0]
    a = alpha[:, 0]
    b = beta[:, 0]
    count, depth, lanes = f.shape
    groups = lax.axis_size("grp")
    blocks = lax.axis_size("box")
    code = [p ^ (p >> 1) for p in range(blocks)]

    def moved(array, target):
        def index(g, p):
            return g * blocks + code[p]

        pairs = [(index(g, p), index(*target(g, p))) for g in range(groups) for p in range(blocks)]
        return lax.ppermute(array, ("grp", "box"), pairs)

    def odd_partner(at, size):
        other = at + 1 if at % 2 else at - 1
        return other if 0 <= other < size else None

    def x_even(g, p):
        return g ^ 1, p

    def x_odd(g, p):
        other = odd_partner(g, groups)
        return (g, p ^ 1) if other is None else (other, p)

    def y_even(g, p):
        return g, p ^ 1

    def y_odd(g, p):
        other = odd_partner(p, blocks)
        return (g ^ (groups // 2), p) if other is None else (g, other)

    def far_even(g, p):
        other = p + 2 if p % 2 else p - 2
        return g, other if 0 <= other < blocks else p ^ 1

    def far_odd(g, p):
        other = p - 2 if p % 2 else p + 2
        return g, other if 0 <= other < blocks else p ^ 1

    def arr(*shape):
        return jax.ShapeDtypeStruct(shape, jnp.float32)

    def vm(*shape):
        return pltpu.VMEM(shape, jnp.float32)

    dma = pltpu.SemaphoreType.DMA
    x_rows = 2 * WIDE_F + WIDE_B
    framed = (count + 2 * FRAME, depth + 2 * FRAME, lanes)
    y_parts = [arr(rows, lanes) for rows in face_pieces(count)[1]]
    parts = len(y_parts)
    c_rows = corner_pieces()[1]
    frame_f, frame_a, frame_b, to_x_even, to_x_odd, *to_y = pl.pallas_call(
        pack_faces_kernel,
        out_shape=[arr(*framed)] * 3 + [arr(x_rows, depth, lanes)] * 2 + y_parts * 2,
        in_specs=[HBM] * 3,
        out_specs=[VMEM] * (5 + 2 * parts),
        scratch_shapes=[dma((3,))],
        compiler_params=params(),
    )(*[pltpu.with_memory_space_constraint(t, pltpu.HBM) for t in (f, a, b)])
    x_halo = moved(to_x_even, x_even), moved(to_x_odd, x_odd)
    y_halo = [moved(t, y_even) for t in to_y[:parts]] + [moved(t, y_odd) for t in to_y[parts:]]

    to_even, to_odd = pl.pallas_call(
        pack_corners_kernel,
        out_shape=[arr(c_rows, lanes)] * 2,
        in_specs=[VMEM] * 2,
        out_specs=[VMEM] * 2,
        compiler_params=params(),
    )(*x_halo)
    corners = moved(to_even, y_even), moved(to_odd, y_odd)

    framed1 = (framed[0] // 2, framed[1] // 2, lanes)
    count2 = count // 4
    passed = [arr(*framed)] * 10 + [arr(framed1[0], framed[1], lanes)] + [arr(*framed1)] * 9 + [arr(3 * count2, lanes)]
    passed = pl.pallas_call(
        down_inner_kernel,
        out_shape=passed,
        in_specs=[VMEM] * (2 * parts + 3),
        out_specs=[VMEM] * 21,
        input_output_aliases={2 * parts + k: k for k in range(3)},
        scratch_shapes=[vm(2 * count2, framed1[1], lanes)],
        compiler_params=params(),
    )(*y_halo, frame_f, frame_a, frame_b)
    x2_rows = 3 * COARSE_X + FINE_X * depth // 2
    x2_rows += -x2_rows % 8
    results = pl.pallas_call(
        down_kernel,
        out_shape=[arr(*t.shape) for t in passed] + [arr(*framed1)] + [arr(x2_rows, lanes)] * 2,
        in_specs=[VMEM] * 25,
        out_specs=[VMEM] * 24,
        input_output_aliases={4 + k: k for k in range(21)},
        scratch_shapes=[vm(count2, framed1[1], lanes)],
        compiler_params=params(),
    )(*x_halo, *corners, *passed)
    F, _, _, FX, FY, FZ, _, IN, _, U, _, F1, _, _, FX1, FY1, FZ1, _, IN1, _, coarse, V1, to_even, to_odd = results

    x_halo = moved(to_even, x_even), moved(to_odd, x_odd)
    far_rows = 3 * (count2 + 2 * FAR_X)
    near_rows = 3 * COARSE_PITCH + FINE_X * (count // 2 + 2 * FINE_X)
    near_rows += -near_rows % 8
    far, to_even, to_odd = pl.pallas_call(
        pack_coarse_kernel,
        out_shape=[arr(far_rows, lanes)] + [arr(near_rows, lanes)] * 2,
        in_specs=[VMEM] * 4,
        out_specs=[VMEM] * 3,
        scratch_shapes=[vm(x2_rows, lanes)] * 2,
        compiler_params=params(),
    )(coarse, V1, *x_halo)
    near = moved(to_even, y_even), moved(to_odd, y_odd)
    distant = moved(far, far_even), moved(far, far_odd)

    out = pl.pallas_call(
        up_kernel,
        out_shape=arr(count, depth, lanes),
        in_specs=[VMEM] * 19,
        out_specs=HBM,
        scratch_shapes=[vm(*framed)] * 2 + [vm(*framed1)] * 2
        + [vm(3, COARSE_PITCH, lanes), vm(count // 2 + 2, framed[1], lanes),
           vm(2, 3, COARSE_PITCH, lanes), vm(count, depth, lanes), dma((4,))],
        compiler_params=params(),
    )(
        *near, *distant, to_even, *x_halo,
        U, F, IN, FX, FY, FZ, V1, F1, IN1, FX1, FY1, FZ1,
    )
    return out[:, None]


def solution(mesh):
    spec = P("grp", "box", None, None)
    return jax.shard_map(body, mesh=mesh, in_specs=(spec,) * 3, out_specs=spec, check_vma=False)
```

```python
import functools

import jax
import jax.numpy as jnp
from jax import lax
from jax.experimental import pallas as pl
from jax.experimental.pallas import tpu as pltpu
from jax.sharding import PartitionSpec as P

OMEGA = 0.7
FRAME = 8
WIDE_F = 6
WIDE_B = 7
COARSE_PITCH = 24
FAR_X = 4
COARSE_X = 6
FINE_X = 3
LANES = 128
ANY = pl.BlockSpec(memory_space=pl.ANY)
HBM = pl.BlockSpec(memory_space=pltpu.HBM)
VMEM = pl.BlockSpec(memory_space=pltpu.VMEM)
LIMIT = 16 * 1024 * 1024


def params():
    return pltpu.CompilerParams(vmem_limit_bytes=LIMIT)


def gray_position(code, bit_count):
    position = code
    for shift in range(1, bit_count):
        position = position ^ (code >> shift)
    return position


def box_position():
    bit_count = lax.axis_size("box").bit_length() - 1
    return gray_position(lax.axis_index("box"), bit_count)


def even_position():
    return box_position() % 2 == 0


def even_group():
    return lax.axis_index("grp") % 2 == 0


def below_above(even, from_even, from_odd):
    return jnp.where(even, from_odd, from_even), jnp.where(even, from_even, from_odd)


def run_copies(pairs, sems):
    copies = [pltpu.make_async_copy(src, dst, sems.at[at]) for at, (src, dst) in enumerate(pairs)]
    for copy in copies:
        copy.start()
    return copies


def wait_copies(copies):
    for copy in copies:
        copy.wait()


def lane_ids(shape):
    return lax.broadcasted_iota(jnp.int32, shape, 1)


def y_next(row):
    return pltpu.roll(row, row.shape[0] - 1, 0)


def y_prev(row):
    return pltpu.roll(row, 1, 0)


def z_next(row, dist):
    return pltpu.roll(row, LANES - dist, 1)


def z_prev(row, dist):
    return pltpu.roll(row, dist, 1)


def coefficients(alpha, beta, beta_prev, beta_next, dist, scale):
    half = 0.5 * scale
    lane = lane_ids(beta.shape)
    inside = lane < LANES - dist
    up_z = jnp.where(inside, z_next(beta, dist), 0.0)
    down_z = jnp.where(lane >= dist, z_prev(beta, dist), 0.0)
    up_y = y_next(beta)
    face_x = half * (beta + beta_next)
    face_y = half * (beta + up_y)
    face_z = jnp.where(inside, half * (beta + up_z), 0.0)
    total = (beta_prev + beta_next) + (up_y + y_prev(beta)) + (up_z + down_z)
    diagonal = alpha + half * (6.0 * beta + total)
    inverse = jnp.where(alpha > 0.0, OMEGA / diagonal, 0.0)
    return face_x, face_y, face_z, diagonal, inverse


def off_sum(at, v, faces, dist):
    face_x, face_y, face_z = faces
    here = v[at]
    fy = face_y[at]
    fz = face_z[at]
    along_x = face_x[at] * v[at + 1] + face_x[at - 1] * v[at - 1]
    along_y = fy * y_next(here) + y_prev(fy * here)
    along_z = fz * z_next(here, dist) + z_prev(fz * here, dist)
    return here, along_x + along_y + along_z


def relaxed(at, v, f, inverse, faces, dist):
    here, off = off_sum(at, v, faces, dist)
    return (1.0 - OMEGA) * here + inverse[at] * (f[at] + off)


def rows_loop(low, high, step, fn):
    trips = (high - low) // step

    def run(rows):
        stores = [item for row in rows for item in fn(row)]
        for ref, at, value in stores:
            ref[at] = value

    def trip(t, carry):
        base = low + t * step
        run([base + k for k in range(step)])
        return carry

    if trips <= 4:
        for t in range(trips):
            run([low + t * step + k for k in range(step)])
    else:
        lax.fori_loop(0, trips, trip, 0)
    rest = list(range(low + trips * step, high))
    if rest:
        run(rest)


def pair_sum_z(row, dist):
    lane = lane_ids(row.shape)
    return row + jnp.take_along_axis(row, lane ^ dist, axis=1)


def strided_pair(ref, at, count):
    return ref[at, pl.ds(0, count, stride=2), :] + ref[at, pl.ds(1, count, stride=2), :]


def zero(ref, *at):
    ref[at] = jnp.zeros_like(ref[at])


WIDES = (WIDE_F, WIDE_F, WIDE_B)


FACE_PARTS = ((0,), (1, 2))


def face_pieces(count):
    pieces = []
    sizes = []
    for part, arrays in enumerate(FACE_PARTS):
        at = 0
        for k in arrays:
            for x in range(count):
                pieces.append((k, x, WIDES[k], part, at))
                at += WIDES[k]
        sizes.append(at + -at % 8)
    return pieces, sizes


EDGE = 2


def x_layout(depth):
    whole = {}
    for k, wide in enumerate(WIDES):
        for distance in range(1, wide):
            whole[k, distance] = len(whole) * depth
    edges = len(whole) * depth
    swept = edges + 2 * EDGE * len(WIDES)
    rows = swept + depth - 2 * EDGE
    return whole, edges, swept, rows + -rows % 8


def x_rows(depth, k, distance, n, upper):
    whole, edges, _, _ = x_layout(depth)
    if (k, distance) in whole:
        start = whole[k, distance] + (depth - n if upper else 0)
    else:
        assert n == EDGE
        start = edges + 2 * EDGE * k + (EDGE if upper else 0)
    return slice(start, start + n)


def corner_pieces():
    pieces = []
    at = 0
    for side in range(2):
        for k, wide in enumerate(WIDES):
            for distance in range(1, wide + 1):
                layers = min(wide, wide + 2 - distance)
                pieces.append((side, k, distance, layers, at))
                at += layers
    return pieces, at + -at % 8


def pack_faces_kernel(f, a, b, F, A, B, x_even, x_odd, *rest):
    *y_faces, sems = rest
    y_even = y_faces[:len(FACE_PARTS)]
    y_odd = y_faces[len(FACE_PARTS):]
    count, depth = f.shape[:2]
    own = (pl.ds(FRAME, count), pl.ds(FRAME, depth))
    frames = (F, A, B)
    copies = run_copies([(src, dst.at[own]) for src, dst in zip((f, a, b), frames)], sems)
    pieces, _ = face_pieces(count)
    even = even_position()
    even_x = even_group()
    whole, _, swept, _ = x_layout(depth)

    def send_x(rows, up, down):
        x_odd[rows], x_even[rows] = below_above(even_x, up, down)

    for k, (ref, wide) in enumerate(zip(frames, WIDES)):
        copies[k].wait()
        for distance in range(1, wide + 1):
            ends = (FRAME + count - distance, FRAME + distance - 1)
            if distance < wide:
                start = whole[k, distance]
                send_x(slice(start, start + depth), *(ref[x, FRAME:FRAME + depth] for x in ends))
            else:
                for upper, y in ((False, FRAME), (True, FRAME + depth - EDGE)):
                    send_x(x_rows(depth, k, distance, EDGE, upper), *(ref[x, y:y + EDGE] for x in ends))
        for at_k, x, layers, part, at in pieces:
            if at_k == k:
                up = ref[FRAME + x, FRAME + depth - layers:FRAME + depth]
                down = ref[FRAME + x, FRAME:FRAME + layers]
                rows = slice(at, at + layers)
                y_odd[part][rows], y_even[part][rows] = below_above(even, up, down)
    first_sweep = []
    for x in (FRAME + count - WIDE_F, FRAME + WIDE_F - 1):
        rows = slice(FRAME, FRAME + depth)
        inverse = coefficients(A[x, rows], B[x, rows], B[x - 1, rows], B[x + 1, rows], 1, 1.0)[-1]
        first_sweep.append((inverse * F[x, rows])[EDGE:depth - EDGE])
    send_x(slice(swept, swept + depth - 2 * EDGE), *first_sweep)


def pack_corners_kernel(depth, x_even, x_odd, to_even, to_odd):
    even = even_position()
    even_x = even_group()
    for side, k, distance, n, at in corner_pieces()[0]:
        up, down = (
            below_above(even_x, x_even[rows], x_odd[rows])[side]
            for rows in (x_rows(depth, k, distance, n, upper) for upper in (True, False))
        )
        to_odd[at:at + n], to_even[at:at + n] = below_above(even, up, down)


def down_rows(F, A, B, FX, FY, FZ, DG, IN, V, U, T, F1, A1, B1, FX1, FY1, FZ1, D1, IN1, W1, coarse):
    faces = (FX, FY, FZ)
    half_rows = F1.shape[1]
    count2 = coarse.shape[0] // 3
    first1 = FRAME // 2
    own2 = FRAME // 4
    depth2 = half_rows // 2 - 2 * own2
    lane = lane_ids((1, LANES))

    def coef_row(i):
        fx, fy, fz, dg, inv = coefficients(A[i], B[i], B[i - 1], B[i + 1], 1, 1.0)
        return [(FX, i, fx), (FY, i, fy), (FZ, i, fz), (DG, i, dg), (IN, i, inv), (V, i, inv * F[i])]

    def sweep_row(i):
        return [(U, i, relaxed(i, V, F, IN, faces, 1))]

    def residual(i):
        here, off = off_sum(i, U, faces, 1)
        return F[i] - DG[i] * here + off

    def restrict_row(j):
        return [(T, j, residual(2 * j) + residual(2 * j + 1))]

    def level1_source(j):
        return [(F1, j, 0.125 * pair_sum_z(strided_pair(T, j, half_rows), 1))]

    def level1_coef(j):
        stores = []
        for src, dst in ((A, A1), (B, B1)):
            both = strided_pair(src, 2 * j, half_rows) + strided_pair(src, 2 * j + 1, half_rows)
            stores.append((dst, j, 0.125 * pair_sum_z(both, 1)))
        return stores

    def coef_row1(i):
        fx, fy, fz, dg, inv = coefficients(A1[i], B1[i], B1[i - 1], B1[i + 1], 2, 0.25)
        return [(FX1, i, fx), (FY1, i, fy), (FZ1, i, fz), (D1, i, dg), (IN1, i, inv), (W1, i, inv * F1[i])]

    def coarse_pack(k, ref, at, x):
        rows = half_rows // 2
        both = ref[at, pl.ds(0, rows, stride=2), :] + ref[at, pl.ds(1, rows, stride=2), :]
        value = 0.125 * pair_sum_z(both, 2)
        packed = jnp.zeros((1, LANES), jnp.float32)
        for y in range(depth2):
            packed = packed + jnp.where(lane % depth2 == y, value[own2 + y:own2 + y + 1], 0.0)
        return (coarse, pl.ds(k * count2 + x, 1), packed)

    return coef_row, sweep_row, restrict_row, level1_source, level1_coef, coef_row1, coarse_pack


def down_inner_kernel(*refs):
    y_even = refs[:len(FACE_PARTS)]
    y_odd = refs[len(FACE_PARTS):2 * len(FACE_PARTS)]
    *refs, T1 = refs[2 * len(FACE_PARTS) + 3:]
    F, A, B = frames = refs[:3]
    A1, B1 = refs[12:14]
    end = F.shape[0]
    depth = F.shape[1] - 2 * FRAME
    count = end - 2 * FRAME
    even = even_position()
    for k, x, layers, part, at in face_pieces(count)[0]:
        rows = slice(at, at + layers)
        below, above = below_above(even, y_even[part][rows], y_odd[part][rows])
        frames[k][FRAME + x, FRAME - layers:FRAME] = below
        frames[k][FRAME + x, FRAME + depth:FRAME + depth + layers] = above
    zero_y_edges(frames, depth)
    coef_row, sweep_row, restrict_row, level1_source, level1_coef, coef_row1, coarse_pack = down_rows(*refs)
    first1 = FRAME // 2
    end1 = end // 2
    rows_loop(FRAME + 1, end - FRAME - 1, 10, coef_row)
    rows_loop(FRAME + 2, end - FRAME - 2, 14, sweep_row)
    rows_loop(first1 + 2, end1 - first1 - 2, 6, restrict_row)
    rows_loop(first1 + 2, end1 - first1 - 2, 12, level1_source)
    rows_loop(first1, end1 - first1, 8, level1_coef)
    rows_loop(first1 + 2, end1 - first1 - 2, 12, coef_row1)
    count2 = count // 4

    def coarse_sum(x):
        i = first1 + 2 * x
        return [(T1, x, A1[i] + A1[i + 1]), (T1, count2 + x, B1[i] + B1[i + 1])]

    rows_loop(0, count2, 8, coarse_sum)

    def coarse_rows(x):
        return [coarse_pack(1, T1, x, x), coarse_pack(2, T1, count2 + x, x)]

    rows_loop(0, count2, 8, coarse_rows)


def zero_y_edges(frames, depth):
    position = box_position()
    for edge, y in (
        (position == 0, slice(0, FRAME)),
        (position == lax.axis_size("box") - 1, slice(FRAME + depth, FRAME + depth + FRAME)),
    ):

        @pl.when(edge)
        def _(y=y):
            for ref in frames:
                zero(ref, slice(None), y)


def down_kernel(x_even, x_odd, c_even, c_odd, *refs):
    refs = refs[21:]
    *refs, V1, to_even, to_odd, T1 = refs
    F, A, B = frames = refs[:3]
    FX = refs[3]
    F1, A1, B1, FX1, FY1, FZ1, D1, IN1, W1, coarse = refs[11:]
    count = F.shape[0] - 2 * FRAME
    depth = F.shape[1] - 2 * FRAME
    even = even_position()
    even_x = even_group()
    whole, _, swept, _ = x_layout(depth)
    for k, wide in enumerate(WIDES):
        for distance in range(1, wide + 1):
            ends = (FRAME - distance, FRAME + count + distance - 1)
            if distance < wide:
                parts = [(slice(whole[k, distance], whole[k, distance] + depth), FRAME)]
            else:
                parts = [
                    (x_rows(depth, k, distance, EDGE, False), FRAME),
                    (x_rows(depth, k, distance, EDGE, True), FRAME + depth - EDGE),
                ]
            for rows, y in parts:
                size = rows.stop - rows.start
                for x, value in zip(ends, below_above(even_x, x_even[rows], x_odd[rows])):
                    frames[k][x, y:y + size] = value
    for side, k, distance, layers, at in corner_pieces()[0]:
        x = FRAME + count + distance - 1 if side else FRAME - distance
        below, above = below_above(even, c_even[at:at + layers], c_odd[at:at + layers])
        frames[k][x, FRAME - layers:FRAME] = below
        frames[k][x, FRAME + depth:FRAME + depth + layers] = above
    zero_y_edges(frames, depth)
    group = lax.axis_index("grp")
    for edge, x in (
        (group == 0, slice(0, FRAME)),
        (group == lax.axis_size("grp") - 1, slice(FRAME + count, FRAME + count + FRAME)),
    ):

        @pl.when(edge)
        def _(x=x):
            for ref in frames:
                zero(ref, x)

    end = count + 2 * FRAME
    coef_row, sweep_row, restrict_row, level1_source, level1_coef, coef_row1, coarse_pack = down_rows(*refs)
    first1 = FRAME // 2
    end1 = end // 2
    FX[1] = 0.5 * (B[1] + B[2])
    V = refs[8]
    rows = slice(swept, swept + depth - 2 * EDGE)
    below, above = below_above(even_x, x_even[rows], x_odd[rows])
    for margin, fn in ((2, coef_row), (3, sweep_row)):
        rows_loop(margin, FRAME + margin - 1, 7, fn)
        rows_loop(end - FRAME - margin + 1, end - margin, 7, fn)
        if fn is coef_row:
            middle = slice(FRAME + EDGE, FRAME + depth - EDGE)
            V[FRAME - WIDE_F, middle] = jnp.where(group > 0, below, 0.0)
            V[FRAME + count + WIDE_F - 1, middle] = jnp.where(group < lax.axis_size("grp") - 1, above, 0.0)
    for fn in (restrict_row, level1_source):
        rows_loop(2, first1 + 2, 4, fn)
        rows_loop(end1 - first1 - 2, end1 - 2, 4, fn)
    rows_loop(1, first1, 3, level1_coef)
    rows_loop(end1 - first1, end1 - 1, 3, level1_coef)
    FX1[1] = 0.125 * (B1[1] + B1[2])
    rows_loop(2, first1 + 2, 4, coef_row1)
    rows_loop(end1 - first1 - 2, end1 - 2, 4, coef_row1)

    faces1 = (FX1, FY1, FZ1)

    def sweep_row1(i):
        return [(V1, i, relaxed(i, W1, F1, IN1, faces1, 2))]

    rows_loop(3, end1 - 3, 18, sweep_row1)

    def residual1(i):
        here, off = off_sum(i, V1, faces1, 2)
        return F1[i] - D1[i] * here + off

    count1 = count // 2
    count2 = count // 4

    def coarse_row(x):
        i = first1 + 2 * x
        return [(T1, x, residual1(i) + residual1(i + 1))]

    rows_loop(0, count2, 8, coarse_row)

    def coarse_source(x):
        return [coarse_pack(0, T1, x, x)]

    rows_loop(0, count2, 8, coarse_source)

    own1 = slice(first1, first1 + depth // 2)
    for k in range(3):
        rows = slice(k * COARSE_X, (k + 1) * COARSE_X)
        up = coarse[(k + 1) * count2 - COARSE_X:(k + 1) * count2]
        down = coarse[k * count2:k * count2 + COARSE_X]
        to_odd[rows], to_even[rows] = below_above(even_x, up, down)
    for k in range(FINE_X):
        rows = slice(3 * COARSE_X + k * depth // 2, 3 * COARSE_X + (k + 1) * depth // 2)
        up = V1[first1 + count1 - FINE_X + k, own1]
        down = V1[first1 + k, own1]
        to_odd[rows], to_even[rows] = below_above(even_x, up, down)


def pack_coarse_kernel(coarse, v1, x_even, x_odd, far, to_even, to_odd, low, high):
    low[...], high[...] = below_above(even_group(), x_even[...], x_odd[...])
    count2 = coarse.shape[0] // 3
    first1 = FRAME // 2
    depth1 = v1.shape[1] - FRAME
    count1 = 2 * count2
    for k in range(3):
        row = k * COARSE_PITCH
        part = slice(k * COARSE_X, (k + 1) * COARSE_X)
        to_even[row:row + COARSE_X] = low[part]
        to_even[row + COARSE_X:row + COARSE_X + count2] = coarse[k * count2:(k + 1) * count2]
        to_even[row + COARSE_X + count2:row + 2 * COARSE_X + count2] = high[part]
        size = count2 + 2 * FAR_X
        first = row + COARSE_X - FAR_X
        far[k * size:(k + 1) * size] = to_even[first:first + size]
    rows = 3 * COARSE_PITCH
    to_odd[0:rows] = to_even[0:rows]
    even = even_position()
    tiles = [low[3 * COARSE_X + k * depth1:3 * COARSE_X + (k + 1) * depth1] for k in range(FINE_X)]
    tiles += [v1[first1 + k, first1:first1 + depth1] for k in range(count1)]
    tiles += [high[3 * COARSE_X + k * depth1:3 * COARSE_X + (k + 1) * depth1] for k in range(FINE_X)]
    for k, tile in enumerate(tiles):
        part = slice(rows + k * FINE_X, rows + (k + 1) * FINE_X)
        up = tile[depth1 - FINE_X:]
        down = tile[:FINE_X]
        to_odd[part], to_even[part] = below_above(even, up, down)


def coarse_solve(source, alpha, beta):
    shape = beta[0].shape
    lane = lane_ids(shape)
    first = lane % 4 == 0
    last = lane % 4 == 3
    inside = lane < LANES - 4
    nothing = jnp.zeros(shape, jnp.float32)

    def next_x(v):
        return pltpu.roll(v, shape[0] - 1, 0)

    def prev_x(v):
        return pltpu.roll(v, 1, 0)

    def next_y(vs):
        over = [pltpu.roll(v, 3, 1) for v in vs[1:]] + [nothing]
        return [jnp.where(last, o, pltpu.roll(v, LANES - 1, 1)) for o, v in zip(over, vs)]

    def prev_y(vs):
        over = [nothing] + [pltpu.roll(v, LANES - 3, 1) for v in vs[:-1]]
        return [jnp.where(first, o, pltpu.roll(v, 1, 1)) for o, v in zip(over, vs)]

    half = 0.5 * 0.0625
    coefs = []
    for a, b, b_next, b_prev in zip(alpha, beta, next_y(beta), prev_y(beta)):
        up_x = next_x(b)
        up_z = jnp.where(inside, z_next(b, 4), 0.0)
        down_z = jnp.where(lane >= 4, z_prev(b, 4), 0.0)
        total = (prev_x(b) + up_x) + (b_next + b_prev) + (up_z + down_z)
        diagonal = a + half * (6.0 * b + total)
        inverse = jnp.where(a > 0.0, OMEGA / diagonal, 0.0)
        face_z = jnp.where(inside, half * (b + up_z), 0.0)
        coefs.append((half * (b + up_x), half * (b + b_next), face_z, inverse))
    field = [c[3] * f for c, f in zip(coefs, source)]
    for _ in range(3):
        flux = prev_y([c[1] * v for c, v in zip(coefs, field)])
        new = []
        for (fx, fy, fz, inverse), v, v_next, back, f in zip(coefs, field, next_y(field), flux, source):
            off = fx * next_x(v) + prev_x(fx * v)
            off = off + (fy * v_next + back)
            off = off + (fz * z_next(v, 4) + z_prev(fz * v, 4))
            new.append((1.0 - OMEGA) * v + inverse * (f + off))
        field = new
    return field


def up_kernel(
    near_even, near_odd, far_even, far_odd, own, x_even, x_odd,
    in_v, F, IN, FX, FY, FZ,
    in_v1, F1, IN1, FX1, FY1, FZ1,
    out,
    V, U, V1, U1, C2, P0, R2, result, sems,
):
    group = lax.axis_index("grp")
    position = box_position()
    even = position % 2 == 0
    last_group = lax.axis_size("grp") - 1
    last_block = lax.axis_size("box") - 1
    count, depth = result.shape[:2]

    row2 = lax.broadcasted_iota(jnp.int32, (COARSE_PITCH, LANES), 0) - COARSE_X + group * (count // 4)
    in_x = (row2 >= 0) & (row2 < (last_group + 1) * (count // 4))
    arrays = []
    for k in range(3):
        rows = pl.ds(k * COARSE_PITCH, COARSE_PITCH)
        near_low, near_high = below_above(even, near_even[rows], near_odd[rows])
        size = count // 4 + 2 * FAR_X
        far_rows = pl.ds(k * size, size)
        for at, value in enumerate(below_above(even, far_even[far_rows], far_odd[far_rows])):
            R2[at, k] = jnp.zeros((COARSE_PITCH, LANES), jnp.float32)
            R2[at, k, COARSE_X - FAR_X:COARSE_X - FAR_X + size] = value
        blocks = (R2[0, k], near_low, own[rows], near_high, R2[1, k])
        column = []
        for at, value in enumerate(blocks):
            place = position + (at - 2)
            column.append(jnp.where(in_x & ((place >= 0) & (place <= last_block)), value, 0.0))
        arrays.append(column)
    field2 = coarse_solve(*arrays)
    for at in range(3):
        C2[at] = field2[1 + at]

    first1 = FRAME // 2
    depth1 = depth // 2
    span1 = V1.shape[0]
    rows1 = V1.shape[1]
    own_rows = pl.ds(first1, depth1)

    def own_row(x):
        i = first1 + x
        return [(V1, (i, own_rows), in_v1[i, own_rows])]

    rows_loop(0, span1 - 2 * first1, 16, own_row)
    for k in range(FINE_X):
        tile = pl.ds(3 * COARSE_X + k * depth1, depth1)
        below, above = below_above(even_group(), x_even[tile], x_odd[tile])
        V1[first1 - FINE_X + k, own_rows] = below
        V1[span1 - first1 + k, own_rows] = above

    rim = 3 * COARSE_PITCH

    def rim_row(x):
        i = x + first1 - FINE_X
        part = pl.ds(rim + FINE_X * x, FINE_X)
        near_low, near_high = below_above(even, near_even[part], near_odd[part])
        return [
            (V1, (i, slice(first1 - FINE_X, first1)), jnp.where(position > 0, near_low, 0.0)),
            (
                V1,
                (i, slice(first1 + depth1, first1 + depth1 + FINE_X)),
                jnp.where(position < last_block, near_high, 0.0),
            ),
        ]

    rows_loop(0, span1 - 2 * (first1 - FINE_X), 22, rim_row)
    for edge, rows in ((group == 0, slice(0, first1)), (group == last_group, slice(span1 - first1, span1))):

        @pl.when(edge)
        def _(rows=rows):
            zero(V1, rows)

    sub = lax.broadcasted_iota(jnp.int32, (rows1, LANES), 0)
    lane = lane_ids((rows1, LANES))
    block = (sub + 4) // 8
    spread = lane - lane % 4 + (sub // 2 + 2) % 4

    def corrected_row(x):
        row = pl.ds(x + COARSE_X - first1 // 2, 1)
        t = jnp.broadcast_to(C2[0, row], (rows1, LANES))
        for at in range(1, 3):
            t = jnp.where(block == at, jnp.broadcast_to(C2[at, row], (rows1, LANES)), t)
        t = jnp.take_along_axis(t, spread, axis=1)
        return [(V1, 2 * x + k, V1[2 * x + k] + t) for k in range(2)]

    rows_loop(0, span1 // 2, 12, corrected_row)
    faces1 = (FX1, FY1, FZ1)

    def sweep_a1(i):
        return [(U1, i, relaxed(i, V1, F1, IN1, faces1, 2))]

    rows_loop(2, span1 - 2, 10, sweep_a1)

    def sweep_b1(i):
        return [(V1, i, relaxed(i, U1, F1, IN1, faces1, 2))]

    rows_loop(3, span1 - 3, 18, sweep_b1)

    span = V.shape[0]
    start = FRAME - 2

    def widen(x):
        row = V1[x + start // 2]
        return [(P0, (x, pl.ds(k, rows1, stride=2)), row) for k in range(2)]

    rows_loop(0, (span - 2 * start) // 2, 18, widen)

    def corrected0(x):
        add = P0[x]
        i = start + 2 * x
        return [(V, i + k, in_v[i + k] + add) for k in range(2)]

    rows_loop(0, (span - 2 * start) // 2, 9, corrected0)
    faces = (FX, FY, FZ)

    def sweep_a(i):
        return [(U, i, relaxed(i, V, F, IN, faces, 1))]

    rows_loop(start + 1, span - start - 1, 17, sweep_a)

    def sweep_b(i):
        return [(result, i - FRAME, relaxed(i, U, F, IN, faces, 1)[FRAME:FRAME + depth])]

    chunk = count // 4
    copies = []
    for k in range(4):
        rows_loop(FRAME + k * chunk, FRAME + (k + 1) * chunk, chunk, sweep_b)
        rows = pl.ds(k * chunk, chunk)
        copies.append(pltpu.make_async_copy(result.at[rows], out.at[rows], sems.at[k]))
        copies[-1].start()
    wait_copies(copies)


def body(source, alpha, beta):
    f = source[:, 0]
    a = alpha[:, 0]
    b = beta[:, 0]
    count, depth, lanes = f.shape
    groups = lax.axis_size("grp")
    blocks = lax.axis_size("box")
    code = [p ^ (p >> 1) for p in range(blocks)]

    def moved(array, target):
        def index(g, p):
            return g * blocks + code[p]

        pairs = [(index(g, p), index(*target(g, p))) for g in range(groups) for p in range(blocks)]
        return lax.ppermute(array, ("grp", "box"), pairs)

    def odd_partner(at, size):
        other = at + 1 if at % 2 else at - 1
        return other if 0 <= other < size else None

    def x_even(g, p):
        return g ^ 1, p

    def x_odd(g, p):
        other = odd_partner(g, groups)
        return (g, p ^ 1) if other is None else (other, p)

    def y_even(g, p):
        return g, p ^ 1

    def y_odd(g, p):
        other = odd_partner(p, blocks)
        return (g ^ (groups // 2), p) if other is None else (g, other)

    def far_even(g, p):
        other = p + 2 if p % 2 else p - 2
        return g, other if 0 <= other < blocks else p ^ 1

    def far_odd(g, p):
        other = p - 2 if p % 2 else p + 2
        return g, other if 0 <= other < blocks else p ^ 1

    def arr(*shape):
        return jax.ShapeDtypeStruct(shape, jnp.float32)

    def vm(*shape):
        return pltpu.VMEM(shape, jnp.float32)

    dma = pltpu.SemaphoreType.DMA
    framed = (count + 2 * FRAME, depth + 2 * FRAME, lanes)
    y_parts = [arr(rows, lanes) for rows in face_pieces(count)[1]]
    parts = len(y_parts)
    c_rows = corner_pieces()[1]
    frame_f, frame_a, frame_b, to_x_even, to_x_odd, *to_y = pl.pallas_call(
        pack_faces_kernel,
        out_shape=[arr(*framed)] * 3 + [arr(x_layout(depth)[-1], lanes)] * 2 + y_parts * 2,
        in_specs=[HBM] * 3,
        out_specs=[VMEM] * (5 + 2 * parts),
        scratch_shapes=[dma((3,))],
        compiler_params=params(),
    )(*[pltpu.with_memory_space_constraint(t, pltpu.HBM) for t in (f, a, b)])
    x_halo = moved(to_x_even, x_even), moved(to_x_odd, x_odd)
    y_halo = [moved(t, y_even) for t in to_y[:parts]] + [moved(t, y_odd) for t in to_y[parts:]]

    to_even, to_odd = pl.pallas_call(
        functools.partial(pack_corners_kernel, depth),
        out_shape=[arr(c_rows, lanes)] * 2,
        in_specs=[VMEM] * 2,
        out_specs=[VMEM] * 2,
        compiler_params=params(),
    )(*x_halo)
    corners = moved(to_even, y_even), moved(to_odd, y_odd)

    framed1 = (framed[0] // 2, framed[1] // 2, lanes)
    count2 = count // 4
    passed = [arr(*framed)] * 10 + [arr(framed1[0], framed[1], lanes)] + [arr(*framed1)] * 9 + [arr(3 * count2, lanes)]
    passed = pl.pallas_call(
        down_inner_kernel,
        out_shape=passed,
        in_specs=[VMEM] * (2 * parts + 3),
        out_specs=[VMEM] * 21,
        input_output_aliases={2 * parts + k: k for k in range(3)},
        scratch_shapes=[vm(2 * count2, framed1[1], lanes)],
        compiler_params=params(),
    )(*y_halo, frame_f, frame_a, frame_b)
    x2_rows = 3 * COARSE_X + FINE_X * depth // 2
    x2_rows += -x2_rows % 8
    results = pl.pallas_call(
        down_kernel,
        out_shape=[arr(*t.shape) for t in passed] + [arr(*framed1)] + [arr(x2_rows, lanes)] * 2,
        in_specs=[VMEM] * 25,
        out_specs=[VMEM] * 24,
        input_output_aliases={4 + k: k for k in range(21)},
        scratch_shapes=[vm(count2, framed1[1], lanes)],
        compiler_params=params(),
    )(*x_halo, *corners, *passed)
    F, _, _, FX, FY, FZ, _, IN, _, U, _, F1, _, _, FX1, FY1, FZ1, _, IN1, _, coarse, V1, to_even, to_odd = results

    x_halo = moved(to_even, x_even), moved(to_odd, x_odd)
    far_rows = 3 * (count2 + 2 * FAR_X)
    near_rows = 3 * COARSE_PITCH + FINE_X * (count // 2 + 2 * FINE_X)
    near_rows += -near_rows % 8
    far, to_even, to_odd = pl.pallas_call(
        pack_coarse_kernel,
        out_shape=[arr(far_rows, lanes)] + [arr(near_rows, lanes)] * 2,
        in_specs=[VMEM] * 4,
        out_specs=[VMEM] * 3,
        scratch_shapes=[vm(x2_rows, lanes)] * 2,
        compiler_params=params(),
    )(coarse, V1, *x_halo)
    near = moved(to_even, y_even), moved(to_odd, y_odd)
    distant = moved(far, far_even), moved(far, far_odd)

    out = pl.pallas_call(
        up_kernel,
        out_shape=arr(count, depth, lanes),
        in_specs=[VMEM] * 19,
        out_specs=HBM,
        scratch_shapes=[vm(*framed)] * 2 + [vm(*framed1)] * 2
        + [vm(3, COARSE_PITCH, lanes), vm(count // 2 + 2, framed[1], lanes),
           vm(2, 3, COARSE_PITCH, lanes), vm(count, depth, lanes), dma((4,))],
        compiler_params=params(),
    )(
        *near, *distant, to_even, *x_halo,
        U, F, IN, FX, FY, FZ, V1, F1, IN1, FX1, FY1, FZ1,
    )
    return out[:, None]


def solution(mesh):
    spec = P("grp", "box", None, None)
    return jax.shard_map(body, mesh=mesh, in_specs=(spec,) * 3, out_specs=spec, check_vma=False)
```

```python
import functools

import jax
import jax.numpy as jnp
from jax import lax
from jax.experimental import pallas as pl
from jax.experimental.pallas import tpu as pltpu
from jax.sharding import PartitionSpec as P

OMEGA = 0.7
FRAME = 8
WIDE_F = 6
WIDE_B = 7
COARSE_PITCH = 24
FAR_X = 4
COARSE_X = 6
FINE_X = 3
LANES = 128
ANY = pl.BlockSpec(memory_space=pl.ANY)
HBM = pl.BlockSpec(memory_space=pltpu.HBM)
VMEM = pl.BlockSpec(memory_space=pltpu.VMEM)
LIMIT = 16 * 1024 * 1024


def params():
    return pltpu.CompilerParams(vmem_limit_bytes=LIMIT)


def gray_position(code, bit_count):
    position = code
    for shift in range(1, bit_count):
        position = position ^ (code >> shift)
    return position


def box_position():
    bit_count = lax.axis_size("box").bit_length() - 1
    return gray_position(lax.axis_index("box"), bit_count)


def even_position():
    return box_position() % 2 == 0


def even_group():
    return lax.axis_index("grp") % 2 == 0


def below_above(even, from_even, from_odd):
    return jnp.where(even, from_odd, from_even), jnp.where(even, from_even, from_odd)


def run_copies(pairs, sems):
    copies = [pltpu.make_async_copy(src, dst, sems.at[at]) for at, (src, dst) in enumerate(pairs)]
    for copy in copies:
        copy.start()
    return copies


def wait_copies(copies):
    for copy in copies:
        copy.wait()


def lane_ids(shape):
    return lax.broadcasted_iota(jnp.int32, shape, 1)


def y_next(row):
    return pltpu.roll(row, row.shape[0] - 1, 0)


def y_prev(row):
    return pltpu.roll(row, 1, 0)


def z_next(row, dist):
    return pltpu.roll(row, LANES - dist, 1)


def z_prev(row, dist):
    return pltpu.roll(row, dist, 1)


def coefficients(alpha, beta, beta_prev, beta_next, dist, scale):
    half = 0.5 * scale
    lane = lane_ids(beta.shape)
    inside = lane < LANES - dist
    up_z = jnp.where(inside, z_next(beta, dist), 0.0)
    down_z = jnp.where(lane >= dist, z_prev(beta, dist), 0.0)
    up_y = y_next(beta)
    face_x = half * (beta + beta_next)
    face_y = half * (beta + up_y)
    face_z = jnp.where(inside, half * (beta + up_z), 0.0)
    total = (beta_prev + beta_next) + (up_y + y_prev(beta)) + (up_z + down_z)
    diagonal = alpha + half * (6.0 * beta + total)
    inverse = jnp.where(alpha > 0.0, OMEGA / diagonal, 0.0)
    return face_x, face_y, face_z, diagonal, inverse


def off_sum(at, v, faces, dist):
    face_x, face_y, face_z = faces
    here = v[at]
    fy = face_y[at]
    fz = face_z[at]
    along_x = face_x[at] * v[at + 1] + face_x[at - 1] * v[at - 1]
    along_y = fy * y_next(here) + y_prev(fy * here)
    along_z = fz * z_next(here, dist) + z_prev(fz * here, dist)
    return here, along_x + along_y + along_z


def relaxed(at, v, f, inverse, faces, dist):
    here, off = off_sum(at, v, faces, dist)
    return (1.0 - OMEGA) * here + inverse[at] * (f[at] + off)


def rows_loop(low, high, step, fn):
    trips = (high - low) // step

    def run(rows):
        stores = [item for row in rows for item in fn(row)]
        for ref, at, value in stores:
            ref[at] = value

    def trip(t, carry):
        base = low + t * step
        run([base + k for k in range(step)])
        return carry

    if trips <= 4:
        for t in range(trips):
            run([low + t * step + k for k in range(step)])
    else:
        lax.fori_loop(0, trips, trip, 0)
    rest = list(range(low + trips * step, high))
    if rest:
        run(rest)


def pair_sum_z(row, dist):
    lane = lane_ids(row.shape)
    return row + jnp.take_along_axis(row, lane ^ dist, axis=1)


def strided_pair(ref, at, count):
    return ref[at, pl.ds(0, count, stride=2), :] + ref[at, pl.ds(1, count, stride=2), :]


def zero(ref, *at):
    ref[at] = jnp.zeros_like(ref[at])


WIDES = (WIDE_F, WIDE_F, WIDE_B)


FACE_PARTS = ((0,), (1, 2))


def face_pieces(count):
    pieces = []
    sizes = []
    for part, arrays in enumerate(FACE_PARTS):
        at = 0
        for k in arrays:
            for x in range(count):
                pieces.append((k, x, WIDES[k], part, at))
                at += WIDES[k]
        sizes.append(at + -at % 8)
    return pieces, sizes


EDGE = 2


def x_layout(depth):
    whole = {}
    for k, wide in enumerate(WIDES):
        for distance in range(1, wide):
            whole[k, distance] = len(whole) * depth
    edges = len(whole) * depth
    swept = edges + 2 * EDGE * len(WIDES)
    rows = swept + depth - 2 * EDGE
    return whole, edges, swept, rows + -rows % 8


def x_rows(depth, k, distance, n, upper):
    whole, edges, _, _ = x_layout(depth)
    if (k, distance) in whole:
        start = whole[k, distance] + (depth - n if upper else 0)
    else:
        assert n == EDGE
        start = edges + 2 * EDGE * k + (EDGE if upper else 0)
    return slice(start, start + n)


def corner_pieces():
    pieces = []
    at = 0
    for side in range(2):
        for k, wide in enumerate(WIDES):
            for distance in range(1, wide + 1):
                layers = min(wide, wide + 2 - distance)
                pieces.append((side, k, distance, layers, at))
                at += layers
    return pieces, at + -at % 8


def pack_faces_kernel(f, a, b, F, A, B, x_even, x_odd, *rest):
    *y_faces, sems = rest
    y_even = y_faces[:len(FACE_PARTS)]
    y_odd = y_faces[len(FACE_PARTS):]
    count, depth = f.shape[:2]
    own = (pl.ds(FRAME, count), pl.ds(FRAME, depth))
    frames = (F, A, B)
    copies = run_copies([(src, dst.at[own]) for src, dst in zip((f, a, b), frames)], sems)
    pieces, _ = face_pieces(count)
    even = even_position()
    even_x = even_group()
    whole, _, swept, _ = x_layout(depth)

    def send_x(rows, up, down):
        x_odd[rows], x_even[rows] = below_above(even_x, up, down)

    for k, (ref, wide) in enumerate(zip(frames, WIDES)):
        copies[k].wait()
        for distance in range(1, wide + 1):
            ends = (FRAME + count - distance, FRAME + distance - 1)
            if distance < wide:
                start = whole[k, distance]
                send_x(slice(start, start + depth), *(ref[x, FRAME:FRAME + depth] for x in ends))
            else:
                for upper, y in ((False, FRAME), (True, FRAME + depth - EDGE)):
                    send_x(x_rows(depth, k, distance, EDGE, upper), *(ref[x, y:y + EDGE] for x in ends))
        for at_k, x, layers, part, at in pieces:
            if at_k == k:
                up = ref[FRAME + x, FRAME + depth - layers:FRAME + depth]
                down = ref[FRAME + x, FRAME:FRAME + layers]
                rows = slice(at, at + layers)
                y_odd[part][rows], y_even[part][rows] = below_above(even, up, down)
    first_sweep = []
    for x in (FRAME + count - WIDE_F, FRAME + WIDE_F - 1):
        rows = slice(FRAME, FRAME + depth)
        inverse = coefficients(A[x, rows], B[x, rows], B[x - 1, rows], B[x + 1, rows], 1, 1.0)[-1]
        first_sweep.append((inverse * F[x, rows])[EDGE:depth - EDGE])
    send_x(slice(swept, swept + depth - 2 * EDGE), *first_sweep)


def pack_corners_kernel(depth, x_even, x_odd, to_even, to_odd):
    even = even_position()
    even_x = even_group()
    for side, k, distance, n, at in corner_pieces()[0]:
        up, down = (
            below_above(even_x, x_even[rows], x_odd[rows])[side]
            for rows in (x_rows(depth, k, distance, n, upper) for upper in (True, False))
        )
        to_odd[at:at + n], to_even[at:at + n] = below_above(even, up, down)


def down_rows(F, A, B, FX, FY, FZ, DG, IN, V, U, T, F1, A1, B1, FX1, FY1, FZ1, D1, IN1, W1, coarse):
    faces = (FX, FY, FZ)
    half_rows = F1.shape[1]
    count2 = coarse.shape[0] // 3
    first1 = FRAME // 2
    own2 = FRAME // 4
    depth2 = half_rows // 2 - 2 * own2
    lane = lane_ids((1, LANES))

    def coef_row(i):
        fx, fy, fz, dg, inv = coefficients(A[i], B[i], B[i - 1], B[i + 1], 1, 1.0)
        return [(FX, i, fx), (FY, i, fy), (FZ, i, fz), (DG, i, dg), (IN, i, inv), (V, i, inv * F[i])]

    def sweep_row(i):
        return [(U, i, relaxed(i, V, F, IN, faces, 1))]

    def residual(i):
        here, off = off_sum(i, U, faces, 1)
        return F[i] - DG[i] * here + off

    def restrict_row(j):
        return [(T, j, residual(2 * j) + residual(2 * j + 1))]

    def level1_source(j):
        return [(F1, j, 0.125 * pair_sum_z(strided_pair(T, j, half_rows), 1))]

    def level1_coef(j):
        stores = []
        for src, dst in ((A, A1), (B, B1)):
            both = strided_pair(src, 2 * j, half_rows) + strided_pair(src, 2 * j + 1, half_rows)
            stores.append((dst, j, 0.125 * pair_sum_z(both, 1)))
        return stores

    def coef_row1(i):
        fx, fy, fz, dg, inv = coefficients(A1[i], B1[i], B1[i - 1], B1[i + 1], 2, 0.25)
        return [(FX1, i, fx), (FY1, i, fy), (FZ1, i, fz), (D1, i, dg), (IN1, i, inv), (W1, i, inv * F1[i])]

    def coarse_pack(k, ref, at, x):
        rows = half_rows // 2
        both = ref[at, pl.ds(0, rows, stride=2), :] + ref[at, pl.ds(1, rows, stride=2), :]
        value = 0.125 * pair_sum_z(both, 2)
        packed = jnp.zeros((1, LANES), jnp.float32)
        for y in range(depth2):
            packed = packed + jnp.where(lane % depth2 == y, value[own2 + y:own2 + y + 1], 0.0)
        return (coarse, pl.ds(k * count2 + x, 1), packed)

    return coef_row, sweep_row, restrict_row, level1_source, level1_coef, coef_row1, coarse_pack


def down_inner_kernel(*refs):
    y_even = refs[:len(FACE_PARTS)]
    y_odd = refs[len(FACE_PARTS):2 * len(FACE_PARTS)]
    *refs, T1 = refs[2 * len(FACE_PARTS) + 3:]
    F, A, B = frames = refs[:3]
    A1, B1 = refs[12:14]
    end = F.shape[0]
    depth = F.shape[1] - 2 * FRAME
    count = end - 2 * FRAME
    even = even_position()
    for k, x, layers, part, at in face_pieces(count)[0]:
        rows = slice(at, at + layers)
        below, above = below_above(even, y_even[part][rows], y_odd[part][rows])
        frames[k][FRAME + x, FRAME - layers:FRAME] = below
        frames[k][FRAME + x, FRAME + depth:FRAME + depth + layers] = above
    zero_y_edges(frames, depth)
    coef_row, sweep_row, restrict_row, level1_source, level1_coef, coef_row1, coarse_pack = down_rows(*refs)
    first1 = FRAME // 2
    end1 = end // 2
    rows_loop(FRAME + 1, end - FRAME - 1, 10, coef_row)
    rows_loop(FRAME + 2, end - FRAME - 2, 14, sweep_row)
    rows_loop(first1 + 2, end1 - first1 - 2, 6, restrict_row)
    rows_loop(first1 + 2, end1 - first1 - 2, 12, level1_source)
    rows_loop(first1, end1 - first1, 8, level1_coef)
    rows_loop(first1 + 2, end1 - first1 - 2, 12, coef_row1)
    count2 = count // 4

    def coarse_sum(x):
        i = first1 + 2 * x
        return [(T1, x, A1[i] + A1[i + 1]), (T1, count2 + x, B1[i] + B1[i + 1])]

    rows_loop(0, count2, 8, coarse_sum)

    def coarse_rows(x):
        return [coarse_pack(1, T1, x, x), coarse_pack(2, T1, count2 + x, x)]

    rows_loop(0, count2, 8, coarse_rows)


def zero_y_edges(frames, depth):
    position = box_position()
    for edge, y in (
        (position == 0, slice(0, FRAME)),
        (position == lax.axis_size("box") - 1, slice(FRAME + depth, FRAME + depth + FRAME)),
    ):

        @pl.when(edge)
        def _(y=y):
            for ref in frames:
                zero(ref, slice(None), y)


def down_kernel(x_even, x_odd, c_even, c_odd, *refs):
    refs = refs[21:]
    *refs, V1, to_even, to_odd, T1 = refs
    F, A, B = frames = refs[:3]
    FX = refs[3]
    F1, A1, B1, FX1, FY1, FZ1, D1, IN1, W1, coarse = refs[11:]
    count = F.shape[0] - 2 * FRAME
    depth = F.shape[1] - 2 * FRAME
    even = even_position()
    even_x = even_group()
    whole, _, swept, _ = x_layout(depth)
    for k, wide in enumerate(WIDES):
        for distance in range(1, wide + 1):
            ends = (FRAME - distance, FRAME + count + distance - 1)
            if distance < wide:
                parts = [(slice(whole[k, distance], whole[k, distance] + depth), FRAME)]
            else:
                parts = [
                    (x_rows(depth, k, distance, EDGE, False), FRAME),
                    (x_rows(depth, k, distance, EDGE, True), FRAME + depth - EDGE),
                ]
            for rows, y in parts:
                size = rows.stop - rows.start
                for x, value in zip(ends, below_above(even_x, x_even[rows], x_odd[rows])):
                    frames[k][x, y:y + size] = value
    for side, k, distance, layers, at in corner_pieces()[0]:
        x = FRAME + count + distance - 1 if side else FRAME - distance
        below, above = below_above(even, c_even[at:at + layers], c_odd[at:at + layers])
        frames[k][x, FRAME - layers:FRAME] = below
        frames[k][x, FRAME + depth:FRAME + depth + layers] = above
    zero_y_edges(frames, depth)
    group = lax.axis_index("grp")
    for edge, x in (
        (group == 0, slice(0, FRAME)),
        (group == lax.axis_size("grp") - 1, slice(FRAME + count, FRAME + count + FRAME)),
    ):

        @pl.when(edge)
        def _(x=x):
            for ref in frames:
                zero(ref, x)

    end = count + 2 * FRAME
    coef_row, sweep_row, restrict_row, level1_source, level1_coef, coef_row1, coarse_pack = down_rows(*refs)
    first1 = FRAME // 2
    end1 = end // 2
    FX[1] = 0.5 * (B[1] + B[2])
    V = refs[8]
    rows = slice(swept, swept + depth - 2 * EDGE)
    below, above = below_above(even_x, x_even[rows], x_odd[rows])
    for margin, fn in ((2, coef_row), (3, sweep_row)):
        rows_loop(margin, FRAME + margin - 1, 7, fn)
        rows_loop(end - FRAME - margin + 1, end - margin, 7, fn)
        if fn is coef_row:
            middle = slice(FRAME + EDGE, FRAME + depth - EDGE)
            V[FRAME - WIDE_F, middle] = jnp.where(group > 0, below, 0.0)
            V[FRAME + count + WIDE_F - 1, middle] = jnp.where(group < lax.axis_size("grp") - 1, above, 0.0)
    for fn in (restrict_row, level1_source):
        rows_loop(2, first1 + 2, 4, fn)
        rows_loop(end1 - first1 - 2, end1 - 2, 4, fn)
    rows_loop(1, first1, 3, level1_coef)
    rows_loop(end1 - first1, end1 - 1, 3, level1_coef)
    FX1[1] = 0.125 * (B1[1] + B1[2])
    rows_loop(2, first1 + 2, 4, coef_row1)
    rows_loop(end1 - first1 - 2, end1 - 2, 4, coef_row1)

    faces1 = (FX1, FY1, FZ1)

    def sweep_row1(i):
        return [(V1, i, relaxed(i, W1, F1, IN1, faces1, 2))]

    rows_loop(3, end1 - 3, 18, sweep_row1)

    def residual1(i):
        here, off = off_sum(i, V1, faces1, 2)
        return F1[i] - D1[i] * here + off

    count1 = count // 2
    count2 = count // 4

    def coarse_row(x):
        i = first1 + 2 * x
        return [(T1, x, residual1(i) + residual1(i + 1))]

    rows_loop(0, count2, 8, coarse_row)

    def coarse_source(x):
        return [coarse_pack(0, T1, x, x)]

    rows_loop(0, count2, 8, coarse_source)

    own1 = slice(first1, first1 + depth // 2)
    for k in range(3):
        rows = slice(k * COARSE_X, (k + 1) * COARSE_X)
        up = coarse[(k + 1) * count2 - COARSE_X:(k + 1) * count2]
        down = coarse[k * count2:k * count2 + COARSE_X]
        to_odd[rows], to_even[rows] = below_above(even_x, up, down)
    for k in range(FINE_X):
        rows = slice(3 * COARSE_X + k * depth // 2, 3 * COARSE_X + (k + 1) * depth // 2)
        up = V1[first1 + count1 - FINE_X + k, own1]
        down = V1[first1 + k, own1]
        to_odd[rows], to_even[rows] = below_above(even_x, up, down)


def pack_coarse_kernel(coarse, v1, x_even, x_odd, far, to_even, to_odd, low, high):
    low[...], high[...] = below_above(even_group(), x_even[...], x_odd[...])
    count2 = coarse.shape[0] // 3
    first1 = FRAME // 2
    depth1 = v1.shape[1] - FRAME
    count1 = 2 * count2
    for k in range(3):
        row = k * COARSE_PITCH
        part = slice(k * COARSE_X, (k + 1) * COARSE_X)
        to_even[row:row + COARSE_X] = low[part]
        to_even[row + COARSE_X:row + COARSE_X + count2] = coarse[k * count2:(k + 1) * count2]
        to_even[row + COARSE_X + count2:row + 2 * COARSE_X + count2] = high[part]
        size = count2 + 2 * FAR_X
        first = row + COARSE_X - FAR_X
        far[k * size:(k + 1) * size] = to_even[first:first + size]
    rows = 3 * COARSE_PITCH
    to_odd[0:rows] = to_even[0:rows]
    even = even_position()
    tiles = [low[3 * COARSE_X + k * depth1:3 * COARSE_X + (k + 1) * depth1] for k in range(FINE_X)]
    tiles += [v1[first1 + k, first1:first1 + depth1] for k in range(count1)]
    tiles += [high[3 * COARSE_X + k * depth1:3 * COARSE_X + (k + 1) * depth1] for k in range(FINE_X)]
    for k, tile in enumerate(tiles):
        part = slice(rows + k * FINE_X, rows + (k + 1) * FINE_X)
        up = tile[depth1 - FINE_X:]
        down = tile[:FINE_X]
        to_odd[part], to_even[part] = below_above(even, up, down)


def coarse_solve(source, alpha, beta):
    shape = beta[0].shape
    lane = lane_ids(shape)
    first = lane % 4 == 0
    last = lane % 4 == 3
    inside = lane < LANES - 4
    nothing = jnp.zeros(shape, jnp.float32)

    def next_x(v):
        return pltpu.roll(v, shape[0] - 1, 0)

    def prev_x(v):
        return pltpu.roll(v, 1, 0)

    def next_y(vs):
        over = [pltpu.roll(v, 3, 1) for v in vs[1:]] + [nothing]
        return [jnp.where(last, o, pltpu.roll(v, LANES - 1, 1)) for o, v in zip(over, vs)]

    def prev_y(vs):
        over = [nothing] + [pltpu.roll(v, LANES - 3, 1) for v in vs[:-1]]
        return [jnp.where(first, o, pltpu.roll(v, 1, 1)) for o, v in zip(over, vs)]

    half = 0.5 * 0.0625
    coefs = []
    for a, b, b_next, b_prev in zip(alpha, beta, next_y(beta), prev_y(beta)):
        up_x = next_x(b)
        up_z = jnp.where(inside, z_next(b, 4), 0.0)
        down_z = jnp.where(lane >= 4, z_prev(b, 4), 0.0)
        total = (prev_x(b) + up_x) + (b_next + b_prev) + (up_z + down_z)
        diagonal = a + half * (6.0 * b + total)
        inverse = jnp.where(a > 0.0, OMEGA / diagonal, 0.0)
        face_z = jnp.where(inside, half * (b + up_z), 0.0)
        coefs.append((half * (b + up_x), half * (b + b_next), face_z, inverse))
    field = [c[3] * f for c, f in zip(coefs, source)]
    for _ in range(3):
        flux = prev_y([c[1] * v for c, v in zip(coefs, field)])
        new = []
        for (fx, fy, fz, inverse), v, v_next, back, f in zip(coefs, field, next_y(field), flux, source):
            off = fx * next_x(v) + prev_x(fx * v)
            off = off + (fy * v_next + back)
            off = off + (fz * z_next(v, 4) + z_prev(fz * v, 4))
            new.append((1.0 - OMEGA) * v + inverse * (f + off))
        field = new
    return field


def up_kernel(
    near_even, near_odd, far_even, far_odd, own, x_even, x_odd,
    in_v, F, IN, FX, FY, FZ,
    in_v1, F1, IN1, FX1, FY1, FZ1,
    out,
    V, U, V1, U1, C2, P0, R2, result, sems,
):
    group = lax.axis_index("grp")
    position = box_position()
    even = position % 2 == 0
    last_group = lax.axis_size("grp") - 1
    last_block = lax.axis_size("box") - 1
    count, depth = result.shape[:2]

    row2 = lax.broadcasted_iota(jnp.int32, (COARSE_PITCH, LANES), 0) - COARSE_X + group * (count // 4)
    in_x = (row2 >= 0) & (row2 < (last_group + 1) * (count // 4))
    arrays = []
    for k in range(3):
        rows = pl.ds(k * COARSE_PITCH, COARSE_PITCH)
        near_low, near_high = below_above(even, near_even[rows], near_odd[rows])
        size = count // 4 + 2 * FAR_X
        far_rows = pl.ds(k * size, size)
        for at, value in enumerate(below_above(even, far_even[far_rows], far_odd[far_rows])):
            R2[at, k] = jnp.zeros((COARSE_PITCH, LANES), jnp.float32)
            R2[at, k, COARSE_X - FAR_X:COARSE_X - FAR_X + size] = value
        blocks = (R2[0, k], near_low, own[rows], near_high, R2[1, k])
        column = []
        for at, value in enumerate(blocks):
            place = position + (at - 2)
            column.append(jnp.where(in_x & ((place >= 0) & (place <= last_block)), value, 0.0))
        arrays.append(column)
    field2 = coarse_solve(*arrays)
    for at in range(3):
        C2[at] = field2[1 + at]

    first1 = FRAME // 2
    depth1 = depth // 2
    span1 = V1.shape[0]
    rows1 = V1.shape[1]
    own_rows = pl.ds(first1, depth1)

    def own_row(x):
        i = first1 + x
        return [(V1, (i, own_rows), in_v1[i, own_rows])]

    rows_loop(0, span1 - 2 * first1, 16, own_row)
    for k in range(FINE_X):
        tile = pl.ds(3 * COARSE_X + k * depth1, depth1)
        below, above = below_above(even_group(), x_even[tile], x_odd[tile])
        V1[first1 - FINE_X + k, own_rows] = below
        V1[span1 - first1 + k, own_rows] = above

    rim = 3 * COARSE_PITCH

    def rim_row(x):
        i = x + first1 - FINE_X
        part = pl.ds(rim + FINE_X * x, FINE_X)
        near_low, near_high = below_above(even, near_even[part], near_odd[part])
        return [
            (V1, (i, slice(first1 - FINE_X, first1)), jnp.where(position > 0, near_low, 0.0)),
            (
                V1,
                (i, slice(first1 + depth1, first1 + depth1 + FINE_X)),
                jnp.where(position < last_block, near_high, 0.0),
            ),
        ]

    rows_loop(0, span1 - 2 * (first1 - FINE_X), 22, rim_row)
    for edge, rows in ((group == 0, slice(0, first1)), (group == last_group, slice(span1 - first1, span1))):

        @pl.when(edge)
        def _(rows=rows):
            zero(V1, rows)

    sub = lax.broadcasted_iota(jnp.int32, (rows1, LANES), 0)
    lane = lane_ids((rows1, LANES))
    block = (sub + 4) // 8
    spread = lane - lane % 4 + (sub // 2 + 2) % 4

    def corrected_row(x):
        row = pl.ds(x + COARSE_X - first1 // 2, 1)
        t = jnp.broadcast_to(C2[0, row], (rows1, LANES))
        for at in range(1, 3):
            t = jnp.where(block == at, jnp.broadcast_to(C2[at, row], (rows1, LANES)), t)
        t = jnp.take_along_axis(t, spread, axis=1)
        return [(V1, 2 * x + k, V1[2 * x + k] + t) for k in range(2)]

    rows_loop(0, span1 // 2, 12, corrected_row)
    faces1 = (FX1, FY1, FZ1)

    def sweep_a1(i):
        return [(U1, i, relaxed(i, V1, F1, IN1, faces1, 2))]

    rows_loop(2, span1 - 2, 10, sweep_a1)

    def sweep_b1(i):
        return [(V1, i, relaxed(i, U1, F1, IN1, faces1, 2))]

    rows_loop(3, span1 - 3, 18, sweep_b1)

    span = V.shape[0]
    start = FRAME - 2

    def widen(x):
        row = V1[x + start // 2]
        return [(P0, (x, pl.ds(k, rows1, stride=2)), row) for k in range(2)]

    rows_loop(0, (span - 2 * start) // 2, 18, widen)

    def corrected0(x):
        add = P0[x]
        i = start + 2 * x
        return [(V, i + k, in_v[i + k] + add) for k in range(2)]

    rows_loop(0, (span - 2 * start) // 2, 9, corrected0)
    faces = (FX, FY, FZ)

    def sweep_a(i):
        return [(U, i, relaxed(i, V, F, IN, faces, 1))]

    rows_loop(start + 1, span - start - 1, 17, sweep_a)

    def sweep_b(i):
        return [(result, i - FRAME, relaxed(i, U, F, IN, faces, 1)[FRAME:FRAME + depth])]

    chunk = count // 4
    copies = []
    for k in range(4):
        rows_loop(FRAME + k * chunk, FRAME + (k + 1) * chunk, chunk, sweep_b)
        rows = pl.ds(k * chunk, chunk)
        copies.append(pltpu.make_async_copy(result.at[rows], out.at[rows], sems.at[k]))
        copies[-1].start()
    wait_copies(copies)


def body(source, alpha, beta):
    f = source[:, 0]
    a = alpha[:, 0]
    b = beta[:, 0]
    count, depth, lanes = f.shape
    groups = lax.axis_size("grp")
    blocks = lax.axis_size("box")
    code = [p ^ (p >> 1) for p in range(blocks)]

    def moved(array, target):
        def index(g, p):
            return g * blocks + code[p]

        pairs = [(index(g, p), index(*target(g, p))) for g in range(groups) for p in range(blocks)]
        return lax.ppermute(array, ("grp", "box"), pairs)

    def odd_partner(at, size):
        other = at + 1 if at % 2 else at - 1
        return other if 0 <= other < size else None

    def x_even(g, p):
        return g ^ 1, p

    def x_odd(g, p):
        other = odd_partner(g, groups)
        return (g, p ^ 1) if other is None else (other, p)

    def y_even(g, p):
        return g, p ^ 1

    def y_odd(g, p):
        other = odd_partner(p, blocks)
        return (g ^ (groups // 2), p) if other is None else (g, other)

    def far_even(g, p):
        other = p + 2 if p % 2 else p - 2
        return g, other if 0 <= other < blocks else p ^ 1

    def far_odd(g, p):
        other = p - 2 if p % 2 else p + 2
        return g, other if 0 <= other < blocks else p ^ 1

    def arr(*shape):
        return jax.ShapeDtypeStruct(shape, jnp.float32)

    def in_vmem(array):
        return pltpu.VMEM(array.shape, jnp.float32)

    def vm(*shape):
        return pltpu.VMEM(shape, jnp.float32)

    dma = pltpu.SemaphoreType.DMA
    framed = (count + 2 * FRAME, depth + 2 * FRAME, lanes)
    y_parts = [arr(rows, lanes) for rows in face_pieces(count)[1]]
    parts = len(y_parts)
    c_rows = corner_pieces()[1]
    frame_f, frame_a, frame_b, to_x_even, to_x_odd, *to_y = pl.pallas_call(
        pack_faces_kernel,
        out_shape=[in_vmem(arr(*framed))] * 3 + [arr(x_layout(depth)[-1], lanes)] * 2 + y_parts * 2,
        in_specs=[HBM] * 3,
        out_specs=[VMEM] * (5 + 2 * parts),
        scratch_shapes=[dma((3,))],
        compiler_params=params(),
    )(*[pltpu.with_memory_space_constraint(t, pltpu.HBM) for t in (f, a, b)])
    x_halo = moved(to_x_even, x_even), moved(to_x_odd, x_odd)
    y_halo = [moved(t, y_even) for t in to_y[:parts]] + [moved(t, y_odd) for t in to_y[parts:]]

    to_even, to_odd = pl.pallas_call(
        functools.partial(pack_corners_kernel, depth),
        out_shape=[arr(c_rows, lanes)] * 2,
        in_specs=[VMEM] * 2,
        out_specs=[VMEM] * 2,
        compiler_params=params(),
    )(*x_halo)
    corners = moved(to_even, y_even), moved(to_odd, y_odd)

    framed1 = (framed[0] // 2, framed[1] // 2, lanes)
    count2 = count // 4
    passed = [arr(*framed)] * 10 + [arr(framed1[0], framed[1], lanes)] + [arr(*framed1)] * 9 + [arr(3 * count2, lanes)]
    passed = pl.pallas_call(
        down_inner_kernel,
        out_shape=[in_vmem(t) for t in passed],
        in_specs=[VMEM] * (2 * parts + 3),
        out_specs=[VMEM] * 21,
        input_output_aliases={2 * parts + k: k for k in range(3)},
        scratch_shapes=[vm(2 * count2, framed1[1], lanes)],
        compiler_params=params(),
    )(*y_halo, frame_f, frame_a, frame_b)
    x2_rows = 3 * COARSE_X + FINE_X * depth // 2
    x2_rows += -x2_rows % 8
    results = pl.pallas_call(
        down_kernel,
        out_shape=[in_vmem(t) for t in passed] + [arr(*framed1)] + [arr(x2_rows, lanes)] * 2,
        in_specs=[VMEM] * 25,
        out_specs=[VMEM] * 24,
        input_output_aliases={4 + k: k for k in range(21)},
        scratch_shapes=[vm(count2, framed1[1], lanes)],
        compiler_params=params(),
    )(*x_halo, *corners, *passed)
    F, _, _, FX, FY, FZ, _, IN, _, U, _, F1, _, _, FX1, FY1, FZ1, _, IN1, _, coarse, V1, to_even, to_odd = results

    x_halo = moved(to_even, x_even), moved(to_odd, x_odd)
    far_rows = 3 * (count2 + 2 * FAR_X)
    near_rows = 3 * COARSE_PITCH + FINE_X * (count // 2 + 2 * FINE_X)
    near_rows += -near_rows % 8
    far, to_even, to_odd = pl.pallas_call(
        pack_coarse_kernel,
        out_shape=[arr(far_rows, lanes)] + [arr(near_rows, lanes)] * 2,
        in_specs=[VMEM] * 4,
        out_specs=[VMEM] * 3,
        scratch_shapes=[vm(x2_rows, lanes)] * 2,
        compiler_params=params(),
    )(coarse, V1, *x_halo)
    near = moved(to_even, y_even), moved(to_odd, y_odd)
    distant = moved(far, far_even), moved(far, far_odd)

    out = pl.pallas_call(
        up_kernel,
        out_shape=arr(count, depth, lanes),
        in_specs=[VMEM] * 19,
        out_specs=HBM,
        scratch_shapes=[vm(*framed)] * 2 + [vm(*framed1)] * 2
        + [vm(3, COARSE_PITCH, lanes), vm(count // 2 + 2, framed[1], lanes),
           vm(2, 3, COARSE_PITCH, lanes), vm(count, depth, lanes), dma((4,))],
        compiler_params=params(),
    )(
        *near, *distant, to_even, *x_halo,
        U, F, IN, FX, FY, FZ, V1, F1, IN1, FX1, FY1, FZ1,
    )
    return out[:, None]


def solution(mesh):
    spec = P("grp", "box", None, None)
    return jax.shard_map(body, mesh=mesh, in_specs=(spec,) * 3, out_specs=spec, check_vma=False)
```

```python
import functools

import jax
import jax.numpy as jnp
from jax import lax
from jax.experimental import pallas as pl
from jax.experimental.pallas import tpu as pltpu
from jax.sharding import PartitionSpec as P

OMEGA = 0.7
FRAME = 8
WIDE_F = 6
WIDE_B = 7
COARSE_PITCH = 24
FAR_X = 4
COARSE_X = 6
FINE_X = 3
LANES = 128
ANY = pl.BlockSpec(memory_space=pl.ANY)
HBM = pl.BlockSpec(memory_space=pltpu.HBM)
VMEM = pl.BlockSpec(memory_space=pltpu.VMEM)
LIMIT = 16 * 1024 * 1024


def params():
    return pltpu.CompilerParams(vmem_limit_bytes=LIMIT)


def gray_position(code, bit_count):
    position = code
    for shift in range(1, bit_count):
        position = position ^ (code >> shift)
    return position


def box_position():
    bit_count = lax.axis_size("box").bit_length() - 1
    return gray_position(lax.axis_index("box"), bit_count)


def even_position():
    return box_position() % 2 == 0


def even_group():
    return lax.axis_index("grp") % 2 == 0


def below_above(even, from_even, from_odd):
    return jnp.where(even, from_odd, from_even), jnp.where(even, from_even, from_odd)


def run_copies(pairs, sems):
    copies = [pltpu.make_async_copy(src, dst, sems.at[at]) for at, (src, dst) in enumerate(pairs)]
    for copy in copies:
        copy.start()
    return copies


def wait_copies(copies):
    for copy in copies:
        copy.wait()


def lane_ids(shape):
    return lax.broadcasted_iota(jnp.int32, shape, 1)


def y_next(row):
    return pltpu.roll(row, row.shape[0] - 1, 0)


def y_prev(row):
    return pltpu.roll(row, 1, 0)


def z_next(row, dist):
    return pltpu.roll(row, LANES - dist, 1)


def z_prev(row, dist):
    return pltpu.roll(row, dist, 1)


def coefficients(alpha, beta, beta_prev, beta_next, dist, scale):
    half = 0.5 * scale
    lane = lane_ids(beta.shape)
    inside = lane < LANES - dist
    up_z = jnp.where(inside, z_next(beta, dist), 0.0)
    down_z = jnp.where(lane >= dist, z_prev(beta, dist), 0.0)
    up_y = y_next(beta)
    face_x = half * (beta + beta_next)
    face_y = half * (beta + up_y)
    face_z = jnp.where(inside, half * (beta + up_z), 0.0)
    total = (beta_prev + beta_next) + (up_y + y_prev(beta)) + (up_z + down_z)
    diagonal = alpha + half * (6.0 * beta + total)
    inverse = jnp.where(alpha > 0.0, OMEGA / diagonal, 0.0)
    return face_x, face_y, face_z, diagonal, inverse


def off_sum(at, v, faces, dist):
    face_x, face_y, face_z = faces
    here = v[at]
    fy = face_y[at]
    fz = face_z[at]
    along_x = face_x[at] * v[at + 1] + face_x[at - 1] * v[at - 1]
    along_y = fy * y_next(here) + y_prev(fy * here)
    along_z = fz * z_next(here, dist) + z_prev(fz * here, dist)
    return here, along_x + along_y + along_z


def relaxed(at, v, f, inverse, faces, dist):
    here, off = off_sum(at, v, faces, dist)
    return (1.0 - OMEGA) * here + inverse[at] * (f[at] + off)


def rows_loop(low, high, step, fn):
    trips = (high - low) // step

    def run(rows):
        stores = [item for row in rows for item in fn(row)]
        for ref, at, value in stores:
            ref[at] = value

    def trip(t, carry):
        base = low + t * step
        run([base + k for k in range(step)])
        return carry

    if trips <= 4:
        for t in range(trips):
            run([low + t * step + k for k in range(step)])
    else:
        lax.fori_loop(0, trips, trip, 0)
    rest = list(range(low + trips * step, high))
    if rest:
        run(rest)


def pair_sum_z(row, dist):
    lane = lane_ids(row.shape)
    return row + jnp.take_along_axis(row, lane ^ dist, axis=1)


def strided_pair(ref, at, count):
    return ref[at, pl.ds(0, count, stride=2), :] + ref[at, pl.ds(1, count, stride=2), :]


def zero(ref, *at):
    ref[at] = jnp.zeros_like(ref[at])


WIDES = (WIDE_F, WIDE_F, WIDE_B)


FACE_PARTS = ((0,), (1, 2))


def face_pieces(count):
    pieces = []
    sizes = []
    for part, arrays in enumerate(FACE_PARTS):
        at = 0
        for k in arrays:
            for x in range(count):
                pieces.append((k, x, WIDES[k], part, at))
                at += WIDES[k]
        sizes.append(at + -at % 8)
    return pieces, sizes


EDGE = 2


def x_layout(depth):
    whole = {}
    for k, wide in enumerate(WIDES):
        for distance in range(1, wide):
            whole[k, distance] = len(whole) * depth
    edges = len(whole) * depth
    swept = edges + 2 * EDGE * len(WIDES)
    rows = swept + depth - 2 * EDGE
    return whole, edges, swept, rows + -rows % 8


def x_rows(depth, k, distance, n, upper):
    whole, edges, _, _ = x_layout(depth)
    if (k, distance) in whole:
        start = whole[k, distance] + (depth - n if upper else 0)
    else:
        assert n == EDGE
        start = edges + 2 * EDGE * k + (EDGE if upper else 0)
    return slice(start, start + n)


def corner_pieces():
    pieces = []
    at = 0
    for side in range(2):
        for k, wide in enumerate(WIDES):
            for distance in range(1, wide + 1):
                layers = min(wide, wide + 2 - distance)
                pieces.append((side, k, distance, layers, at))
                at += layers
    return pieces, at + -at % 8


def pack_faces_kernel(f, a, b, F, A, B, x_even, x_odd, *rest):
    *y_faces, sems = rest
    y_even = y_faces[:len(FACE_PARTS)]
    y_odd = y_faces[len(FACE_PARTS):]
    count, depth = f.shape[:2]
    own = (pl.ds(FRAME, count), pl.ds(FRAME, depth))
    frames = (F, A, B)
    copies = run_copies([(src, dst.at[own]) for src, dst in zip((f, a, b), frames)], sems)
    pieces, _ = face_pieces(count)
    even = even_position()
    even_x = even_group()
    whole, _, swept, _ = x_layout(depth)

    def send_x(rows, up, down):
        x_odd[rows], x_even[rows] = below_above(even_x, up, down)

    for k, (ref, wide) in enumerate(zip(frames, WIDES)):
        copies[k].wait()
        for distance in range(1, wide + 1):
            ends = (FRAME + count - distance, FRAME + distance - 1)
            if distance < wide:
                start = whole[k, distance]
                send_x(slice(start, start + depth), *(ref[x, FRAME:FRAME + depth] for x in ends))
            else:
                for upper, y in ((False, FRAME), (True, FRAME + depth - EDGE)):
                    send_x(x_rows(depth, k, distance, EDGE, upper), *(ref[x, y:y + EDGE] for x in ends))
        for at_k, x, layers, part, at in pieces:
            if at_k == k:
                up = ref[FRAME + x, FRAME + depth - layers:FRAME + depth]
                down = ref[FRAME + x, FRAME:FRAME + layers]
                rows = slice(at, at + layers)
                y_odd[part][rows], y_even[part][rows] = below_above(even, up, down)
    first_sweep = []
    for x in (FRAME + count - WIDE_F, FRAME + WIDE_F - 1):
        rows = slice(FRAME, FRAME + depth)
        inverse = coefficients(A[x, rows], B[x, rows], B[x - 1, rows], B[x + 1, rows], 1, 1.0)[-1]
        first_sweep.append((inverse * F[x, rows])[EDGE:depth - EDGE])
    send_x(slice(swept, swept + depth - 2 * EDGE), *first_sweep)


def pack_corners_kernel(depth, x_even, x_odd, to_even, to_odd):
    even = even_position()
    even_x = even_group()
    for side, k, distance, n, at in corner_pieces()[0]:
        up, down = (
            below_above(even_x, x_even[rows], x_odd[rows])[side]
            for rows in (x_rows(depth, k, distance, n, upper) for upper in (True, False))
        )
        to_odd[at:at + n], to_even[at:at + n] = below_above(even, up, down)


def down_rows(F, A, B, FX, FY, FZ, DG, IN, V, U, T, F1, A1, B1, FX1, FY1, FZ1, D1, IN1, W1, coarse):
    faces = (FX, FY, FZ)
    half_rows = F1.shape[1]
    count2 = coarse.shape[0] // 3
    first1 = FRAME // 2
    own2 = FRAME // 4
    depth2 = half_rows // 2 - 2 * own2
    lane = lane_ids((1, LANES))

    def coef_row(i):
        fx, fy, fz, dg, inv = coefficients(A[i], B[i], B[i - 1], B[i + 1], 1, 1.0)
        return [(FX, i, fx), (FY, i, fy), (FZ, i, fz), (DG, i, dg), (IN, i, inv), (V, i, inv * F[i])]

    def sweep_row(i):
        return [(U, i, relaxed(i, V, F, IN, faces, 1))]

    def residual(i):
        here, off = off_sum(i, U, faces, 1)
        return F[i] - DG[i] * here + off

    def restrict_row(j):
        return [(T, j, residual(2 * j) + residual(2 * j + 1))]

    def level1_source(j):
        return [(F1, j, 0.125 * pair_sum_z(strided_pair(T, j, half_rows), 1))]

    def level1_coef(j):
        stores = []
        for src, dst in ((A, A1), (B, B1)):
            both = strided_pair(src, 2 * j, half_rows) + strided_pair(src, 2 * j + 1, half_rows)
            stores.append((dst, j, 0.125 * pair_sum_z(both, 1)))
        return stores

    def coef_row1(i):
        fx, fy, fz, dg, inv = coefficients(A1[i], B1[i], B1[i - 1], B1[i + 1], 2, 0.25)
        return [(FX1, i, fx), (FY1, i, fy), (FZ1, i, fz), (D1, i, dg), (IN1, i, inv), (W1, i, inv * F1[i])]

    def coarse_pack(k, ref, at, x):
        rows = half_rows // 2
        both = ref[at, pl.ds(0, rows, stride=2), :] + ref[at, pl.ds(1, rows, stride=2), :]
        value = 0.125 * pair_sum_z(both, 2)
        packed = jnp.zeros((1, LANES), jnp.float32)
        for y in range(depth2):
            packed = packed + jnp.where(lane % depth2 == y, value[own2 + y:own2 + y + 1], 0.0)
        return (coarse, pl.ds(k * count2 + x, 1), packed)

    return coef_row, sweep_row, restrict_row, level1_source, level1_coef, coef_row1, coarse_pack


def down_inner_kernel(*refs):
    y_even = refs[:len(FACE_PARTS)]
    y_odd = refs[len(FACE_PARTS):2 * len(FACE_PARTS)]
    *refs, T1 = refs[2 * len(FACE_PARTS) + 3:]
    F, A, B = frames = refs[:3]
    A1, B1 = refs[12:14]
    end = F.shape[0]
    depth = F.shape[1] - 2 * FRAME
    count = end - 2 * FRAME
    even = even_position()
    for k, x, layers, part, at in face_pieces(count)[0]:
        rows = slice(at, at + layers)
        below, above = below_above(even, y_even[part][rows], y_odd[part][rows])
        frames[k][FRAME + x, FRAME - layers:FRAME] = below
        frames[k][FRAME + x, FRAME + depth:FRAME + depth + layers] = above
    zero_y_edges(frames, depth)
    coef_row, sweep_row, restrict_row, level1_source, level1_coef, coef_row1, coarse_pack = down_rows(*refs)
    first1 = FRAME // 2
    end1 = end // 2
    rows_loop(FRAME + 1, end - FRAME - 1, 10, coef_row)
    rows_loop(FRAME + 2, end - FRAME - 2, 14, sweep_row)
    rows_loop(first1 + 2, end1 - first1 - 2, 6, restrict_row)
    rows_loop(first1 + 2, end1 - first1 - 2, 12, level1_source)
    rows_loop(first1, end1 - first1, 8, level1_coef)
    rows_loop(first1 + 2, end1 - first1 - 2, 12, coef_row1)
    count2 = count // 4

    def coarse_sum(x):
        i = first1 + 2 * x
        return [(T1, x, A1[i] + A1[i + 1]), (T1, count2 + x, B1[i] + B1[i + 1])]

    rows_loop(0, count2, 8, coarse_sum)

    def coarse_rows(x):
        return [coarse_pack(1, T1, x, x), coarse_pack(2, T1, count2 + x, x)]

    rows_loop(0, count2, 8, coarse_rows)


def zero_y_edges(frames, depth):
    position = box_position()
    for edge, y in (
        (position == 0, slice(0, FRAME)),
        (position == lax.axis_size("box") - 1, slice(FRAME + depth, FRAME + depth + FRAME)),
    ):

        @pl.when(edge)
        def _(y=y):
            for ref in frames:
                zero(ref, slice(None), y)


def down_kernel(x_even, x_odd, c_even, c_odd, *refs):
    refs = refs[21:]
    *refs, V1, to_even, to_odd, T1 = refs
    F, A, B = frames = refs[:3]
    FX = refs[3]
    F1, A1, B1, FX1, FY1, FZ1, D1, IN1, W1, coarse = refs[11:]
    count = F.shape[0] - 2 * FRAME
    depth = F.shape[1] - 2 * FRAME
    even = even_position()
    even_x = even_group()
    whole, _, swept, _ = x_layout(depth)
    for k, wide in enumerate(WIDES):
        for distance in range(1, wide + 1):
            ends = (FRAME - distance, FRAME + count + distance - 1)
            if distance < wide:
                parts = [(slice(whole[k, distance], whole[k, distance] + depth), FRAME)]
            else:
                parts = [
                    (x_rows(depth, k, distance, EDGE, False), FRAME),
                    (x_rows(depth, k, distance, EDGE, True), FRAME + depth - EDGE),
                ]
            for rows, y in parts:
                size = rows.stop - rows.start
                for x, value in zip(ends, below_above(even_x, x_even[rows], x_odd[rows])):
                    frames[k][x, y:y + size] = value
    for side, k, distance, layers, at in corner_pieces()[0]:
        x = FRAME + count + distance - 1 if side else FRAME - distance
        below, above = below_above(even, c_even[at:at + layers], c_odd[at:at + layers])
        frames[k][x, FRAME - layers:FRAME] = below
        frames[k][x, FRAME + depth:FRAME + depth + layers] = above
    zero_y_edges(frames, depth)
    group = lax.axis_index("grp")
    for edge, x in (
        (group == 0, slice(0, FRAME)),
        (group == lax.axis_size("grp") - 1, slice(FRAME + count, FRAME + count + FRAME)),
    ):

        @pl.when(edge)
        def _(x=x):
            for ref in frames:
                zero(ref, x)

    end = count + 2 * FRAME
    coef_row, sweep_row, restrict_row, level1_source, level1_coef, coef_row1, coarse_pack = down_rows(*refs)
    first1 = FRAME // 2
    end1 = end // 2
    FX[1] = 0.5 * (B[1] + B[2])
    V = refs[8]
    rows = slice(swept, swept + depth - 2 * EDGE)
    below, above = below_above(even_x, x_even[rows], x_odd[rows])
    for margin, fn in ((2, coef_row), (3, sweep_row)):
        rows_loop(margin, FRAME + margin - 1, 7, fn)
        rows_loop(end - FRAME - margin + 1, end - margin, 7, fn)
        if fn is coef_row:
            middle = slice(FRAME + EDGE, FRAME + depth - EDGE)
            V[FRAME - WIDE_F, middle] = jnp.where(group > 0, below, 0.0)
            V[FRAME + count + WIDE_F - 1, middle] = jnp.where(group < lax.axis_size("grp") - 1, above, 0.0)
    for fn in (restrict_row, level1_source):
        rows_loop(2, first1 + 2, 4, fn)
        rows_loop(end1 - first1 - 2, end1 - 2, 4, fn)
    rows_loop(1, first1, 3, level1_coef)
    rows_loop(end1 - first1, end1 - 1, 3, level1_coef)
    FX1[1] = 0.125 * (B1[1] + B1[2])
    rows_loop(2, first1 + 2, 4, coef_row1)
    rows_loop(end1 - first1 - 2, end1 - 2, 4, coef_row1)

    faces1 = (FX1, FY1, FZ1)

    def sweep_row1(i):
        return [(V1, i, relaxed(i, W1, F1, IN1, faces1, 2))]

    rows_loop(3, end1 - 3, 18, sweep_row1)

    def residual1(i):
        here, off = off_sum(i, V1, faces1, 2)
        return F1[i] - D1[i] * here + off

    count1 = count // 2
    count2 = count // 4

    def coarse_row(x):
        i = first1 + 2 * x
        return [(T1, x, residual1(i) + residual1(i + 1))]

    rows_loop(0, count2, 8, coarse_row)

    def coarse_source(x):
        return [coarse_pack(0, T1, x, x)]

    rows_loop(0, count2, 8, coarse_source)

    own1 = slice(first1, first1 + depth // 2)
    for k in range(3):
        rows = slice(k * COARSE_X, (k + 1) * COARSE_X)
        up = coarse[(k + 1) * count2 - COARSE_X:(k + 1) * count2]
        down = coarse[k * count2:k * count2 + COARSE_X]
        to_odd[rows], to_even[rows] = below_above(even_x, up, down)
    for k in range(FINE_X):
        rows = slice(3 * COARSE_X + k * depth // 2, 3 * COARSE_X + (k + 1) * depth // 2)
        up = V1[first1 + count1 - FINE_X + k, own1]
        down = V1[first1 + k, own1]
        to_odd[rows], to_even[rows] = below_above(even_x, up, down)


def pack_coarse_kernel(coarse, v1, x_even, x_odd, far, to_even, to_odd, low, high):
    low[...], high[...] = below_above(even_group(), x_even[...], x_odd[...])
    count2 = coarse.shape[0] // 3
    first1 = FRAME // 2
    depth1 = v1.shape[1] - FRAME
    count1 = 2 * count2
    for k in range(3):
        row = k * COARSE_PITCH
        part = slice(k * COARSE_X, (k + 1) * COARSE_X)
        to_even[row:row + COARSE_X] = low[part]
        to_even[row + COARSE_X:row + COARSE_X + count2] = coarse[k * count2:(k + 1) * count2]
        to_even[row + COARSE_X + count2:row + 2 * COARSE_X + count2] = high[part]
        size = count2 + 2 * FAR_X
        first = row + COARSE_X - FAR_X
        far[k * size:(k + 1) * size] = to_even[first:first + size]
    rows = 3 * COARSE_PITCH
    to_odd[0:rows] = to_even[0:rows]
    even = even_position()
    tiles = [low[3 * COARSE_X + k * depth1:3 * COARSE_X + (k + 1) * depth1] for k in range(FINE_X)]
    tiles += [v1[first1 + k, first1:first1 + depth1] for k in range(count1)]
    tiles += [high[3 * COARSE_X + k * depth1:3 * COARSE_X + (k + 1) * depth1] for k in range(FINE_X)]
    for k, tile in enumerate(tiles):
        part = slice(rows + k * FINE_X, rows + (k + 1) * FINE_X)
        up = tile[depth1 - FINE_X:]
        down = tile[:FINE_X]
        to_odd[part], to_even[part] = below_above(even, up, down)


def coarse_solve(source, alpha, beta):
    shape = beta[0].shape
    lane = lane_ids(shape)
    first = lane % 4 == 0
    last = lane % 4 == 3
    inside = lane < LANES - 4
    nothing = jnp.zeros(shape, jnp.float32)

    def next_x(v):
        return pltpu.roll(v, shape[0] - 1, 0)

    def prev_x(v):
        return pltpu.roll(v, 1, 0)

    def next_y(vs):
        over = [pltpu.roll(v, 3, 1) for v in vs[1:]] + [nothing]
        return [jnp.where(last, o, pltpu.roll(v, LANES - 1, 1)) for o, v in zip(over, vs)]

    def prev_y(vs):
        over = [nothing] + [pltpu.roll(v, LANES - 3, 1) for v in vs[:-1]]
        return [jnp.where(first, o, pltpu.roll(v, 1, 1)) for o, v in zip(over, vs)]

    half = 0.5 * 0.0625
    coefs = []
    for a, b, b_next, b_prev in zip(alpha, beta, next_y(beta), prev_y(beta)):
        up_x = next_x(b)
        up_z = jnp.where(inside, z_next(b, 4), 0.0)
        down_z = jnp.where(lane >= 4, z_prev(b, 4), 0.0)
        total = (prev_x(b) + up_x) + (b_next + b_prev) + (up_z + down_z)
        diagonal = a + half * (6.0 * b + total)
        inverse = jnp.where(a > 0.0, OMEGA / diagonal, 0.0)
        face_z = jnp.where(inside, half * (b + up_z), 0.0)
        coefs.append((half * (b + up_x), half * (b + b_next), face_z, inverse))
    field = [c[3] * f for c, f in zip(coefs, source)]
    for _ in range(3):
        flux = prev_y([c[1] * v for c, v in zip(coefs, field)])
        new = []
        for (fx, fy, fz, inverse), v, v_next, back, f in zip(coefs, field, next_y(field), flux, source):
            off = fx * next_x(v) + prev_x(fx * v)
            off = off + (fy * v_next + back)
            off = off + (fz * z_next(v, 4) + z_prev(fz * v, 4))
            new.append((1.0 - OMEGA) * v + inverse * (f + off))
        field = new
    return field


def up_kernel(
    near_even, near_odd, far_even, far_odd, own, x_even, x_odd,
    in_v, F, IN, FX, FY, FZ,
    in_v1, F1, IN1, FX1, FY1, FZ1,
    out,
    V, U, V1, U1, C2, P0, R2, result, sems,
):
    group = lax.axis_index("grp")
    position = box_position()
    even = position % 2 == 0
    last_group = lax.axis_size("grp") - 1
    last_block = lax.axis_size("box") - 1
    count, depth = result.shape[:2]

    row2 = lax.broadcasted_iota(jnp.int32, (COARSE_PITCH, LANES), 0) - COARSE_X + group * (count // 4)
    in_x = (row2 >= 0) & (row2 < (last_group + 1) * (count // 4))
    arrays = []
    for k in range(3):
        rows = pl.ds(k * COARSE_PITCH, COARSE_PITCH)
        near_low, near_high = below_above(even, near_even[rows], near_odd[rows])
        size = count // 4 + 2 * FAR_X
        far_rows = pl.ds(k * size, size)
        for at, value in enumerate(below_above(even, far_even[far_rows], far_odd[far_rows])):
            R2[at, k] = jnp.zeros((COARSE_PITCH, LANES), jnp.float32)
            R2[at, k, COARSE_X - FAR_X:COARSE_X - FAR_X + size] = value
        blocks = (R2[0, k], near_low, own[rows], near_high, R2[1, k])
        column = []
        for at, value in enumerate(blocks):
            place = position + (at - 2)
            column.append(jnp.where(in_x & ((place >= 0) & (place <= last_block)), value, 0.0))
        arrays.append(column)
    field2 = coarse_solve(*arrays)
    for at in range(3):
        C2[at] = field2[1 + at]

    first1 = FRAME // 2
    depth1 = depth // 2
    span1 = V1.shape[0]
    rows1 = V1.shape[1]
    own_rows = pl.ds(first1, depth1)

    def own_row(x):
        i = first1 + x
        return [(V1, (i, own_rows), in_v1[i, own_rows])]

    rows_loop(0, span1 - 2 * first1, 16, own_row)
    for k in range(FINE_X):
        tile = pl.ds(3 * COARSE_X + k * depth1, depth1)
        below, above = below_above(even_group(), x_even[tile], x_odd[tile])
        V1[first1 - FINE_X + k, own_rows] = below
        V1[span1 - first1 + k, own_rows] = above

    rim = 3 * COARSE_PITCH

    def rim_row(x):
        i = x + first1 - FINE_X
        part = pl.ds(rim + FINE_X * x, FINE_X)
        near_low, near_high = below_above(even, near_even[part], near_odd[part])
        return [
            (V1, (i, slice(first1 - FINE_X, first1)), jnp.where(position > 0, near_low, 0.0)),
            (
                V1,
                (i, slice(first1 + depth1, first1 + depth1 + FINE_X)),
                jnp.where(position < last_block, near_high, 0.0),
            ),
        ]

    rows_loop(0, span1 - 2 * (first1 - FINE_X), 22, rim_row)
    for edge, rows in ((group == 0, slice(0, first1)), (group == last_group, slice(span1 - first1, span1))):

        @pl.when(edge)
        def _(rows=rows):
            zero(V1, rows)

    sub = lax.broadcasted_iota(jnp.int32, (rows1, LANES), 0)
    lane = lane_ids((rows1, LANES))
    block = (sub + 4) // 8
    spread = lane - lane % 4 + (sub // 2 + 2) % 4

    def corrected_row(x):
        row = pl.ds(x + COARSE_X - first1 // 2, 1)
        t = jnp.broadcast_to(C2[0, row], (rows1, LANES))
        for at in range(1, 3):
            t = jnp.where(block == at, jnp.broadcast_to(C2[at, row], (rows1, LANES)), t)
        t = jnp.take_along_axis(t, spread, axis=1)
        return [(V1, 2 * x + k, V1[2 * x + k] + t) for k in range(2)]

    rows_loop(0, span1 // 2, 12, corrected_row)
    faces1 = (FX1, FY1, FZ1)

    def sweep_a1(i):
        return [(U1, i, relaxed(i, V1, F1, IN1, faces1, 2))]

    rows_loop(2, span1 - 2, 10, sweep_a1)

    def sweep_b1(i):
        return [(V1, i, relaxed(i, U1, F1, IN1, faces1, 2))]

    rows_loop(3, span1 - 3, 18, sweep_b1)

    span = V.shape[0]
    start = FRAME - 2

    def widen(x):
        row = V1[x + start // 2]
        return [(P0, (x, pl.ds(k, rows1, stride=2)), row) for k in range(2)]

    rows_loop(0, (span - 2 * start) // 2, 18, widen)

    def corrected0(x):
        add = P0[x]
        i = start + 2 * x
        return [(V, i + k, in_v[i + k] + add) for k in range(2)]

    rows_loop(0, (span - 2 * start) // 2, 9, corrected0)
    faces = (FX, FY, FZ)

    def sweep_a(i):
        return [(U, i, relaxed(i, V, F, IN, faces, 1))]

    rows_loop(start + 1, span - start - 1, 17, sweep_a)

    def sweep_b(i):
        return [(result, i - FRAME, relaxed(i, U, F, IN, faces, 1)[FRAME:FRAME + depth])]

    chunk = count // 8
    copies = []
    for k in range(8):
        rows_loop(FRAME + k * chunk, FRAME + (k + 1) * chunk, chunk, sweep_b)
        rows = pl.ds(k * chunk, chunk)
        copies.append(pltpu.make_async_copy(result.at[rows], out.at[rows], sems.at[k]))
        copies[-1].start()
    wait_copies(copies)


def body(source, alpha, beta):
    f = source[:, 0]
    a = alpha[:, 0]
    b = beta[:, 0]
    count, depth, lanes = f.shape
    groups = lax.axis_size("grp")
    blocks = lax.axis_size("box")
    code = [p ^ (p >> 1) for p in range(blocks)]

    def moved(array, target):
        def index(g, p):
            return g * blocks + code[p]

        pairs = [(index(g, p), index(*target(g, p))) for g in range(groups) for p in range(blocks)]
        return lax.ppermute(array, ("grp", "box"), pairs)

    def odd_partner(at, size):
        other = at + 1 if at % 2 else at - 1
        return other if 0 <= other < size else None

    def x_even(g, p):
        return g ^ 1, p

    def x_odd(g, p):
        other = odd_partner(g, groups)
        return (g, p ^ 1) if other is None else (other, p)

    def y_even(g, p):
        return g, p ^ 1

    def y_odd(g, p):
        other = odd_partner(p, blocks)
        return (g ^ (groups // 2), p) if other is None else (g, other)

    def far_even(g, p):
        other = p + 2 if p % 2 else p - 2
        return g, other if 0 <= other < blocks else p ^ 1

    def far_odd(g, p):
        other = p - 2 if p % 2 else p + 2
        return g, other if 0 <= other < blocks else p ^ 1

    def arr(*shape):
        return jax.ShapeDtypeStruct(shape, jnp.float32)

    def in_vmem(array):
        return pltpu.VMEM(array.shape, jnp.float32)

    def vm(*shape):
        return pltpu.VMEM(shape, jnp.float32)

    dma = pltpu.SemaphoreType.DMA
    framed = (count + 2 * FRAME, depth + 2 * FRAME, lanes)
    y_parts = [arr(rows, lanes) for rows in face_pieces(count)[1]]
    parts = len(y_parts)
    c_rows = corner_pieces()[1]
    frame_f, frame_a, frame_b, to_x_even, to_x_odd, *to_y = pl.pallas_call(
        pack_faces_kernel,
        out_shape=[in_vmem(arr(*framed))] * 3 + [arr(x_layout(depth)[-1], lanes)] * 2 + y_parts * 2,
        in_specs=[HBM] * 3,
        out_specs=[VMEM] * (5 + 2 * parts),
        scratch_shapes=[dma((3,))],
        compiler_params=params(),
    )(*[pltpu.with_memory_space_constraint(t, pltpu.HBM) for t in (f, a, b)])
    x_halo = moved(to_x_even, x_even), moved(to_x_odd, x_odd)
    y_halo = [moved(t, y_even) for t in to_y[:parts]] + [moved(t, y_odd) for t in to_y[parts:]]

    to_even, to_odd = pl.pallas_call(
        functools.partial(pack_corners_kernel, depth),
        out_shape=[arr(c_rows, lanes)] * 2,
        in_specs=[VMEM] * 2,
        out_specs=[VMEM] * 2,
        compiler_params=params(),
    )(*x_halo)
    corners = moved(to_even, y_even), moved(to_odd, y_odd)

    framed1 = (framed[0] // 2, framed[1] // 2, lanes)
    count2 = count // 4
    passed = [arr(*framed)] * 10 + [arr(framed1[0], framed[1], lanes)] + [arr(*framed1)] * 9 + [arr(3 * count2, lanes)]
    passed = pl.pallas_call(
        down_inner_kernel,
        out_shape=[in_vmem(t) for t in passed],
        in_specs=[VMEM] * (2 * parts + 3),
        out_specs=[VMEM] * 21,
        input_output_aliases={2 * parts + k: k for k in range(3)},
        scratch_shapes=[vm(2 * count2, framed1[1], lanes)],
        compiler_params=params(),
    )(*y_halo, frame_f, frame_a, frame_b)
    x2_rows = 3 * COARSE_X + FINE_X * depth // 2
    x2_rows += -x2_rows % 8
    results = pl.pallas_call(
        down_kernel,
        out_shape=[in_vmem(t) for t in passed] + [arr(*framed1)] + [arr(x2_rows, lanes)] * 2,
        in_specs=[VMEM] * 25,
        out_specs=[VMEM] * 24,
        input_output_aliases={4 + k: k for k in range(21)},
        scratch_shapes=[vm(count2, framed1[1], lanes)],
        compiler_params=params(),
    )(*x_halo, *corners, *passed)
    F, _, _, FX, FY, FZ, _, IN, _, U, _, F1, _, _, FX1, FY1, FZ1, _, IN1, _, coarse, V1, to_even, to_odd = results

    x_halo = moved(to_even, x_even), moved(to_odd, x_odd)
    far_rows = 3 * (count2 + 2 * FAR_X)
    near_rows = 3 * COARSE_PITCH + FINE_X * (count // 2 + 2 * FINE_X)
    near_rows += -near_rows % 8
    far, to_even, to_odd = pl.pallas_call(
        pack_coarse_kernel,
        out_shape=[arr(far_rows, lanes)] + [arr(near_rows, lanes)] * 2,
        in_specs=[VMEM] * 4,
        out_specs=[VMEM] * 3,
        scratch_shapes=[vm(x2_rows, lanes)] * 2,
        compiler_params=params(),
    )(coarse, V1, *x_halo)
    near = moved(to_even, y_even), moved(to_odd, y_odd)
    distant = moved(far, far_even), moved(far, far_odd)

    out = pl.pallas_call(
        up_kernel,
        out_shape=arr(count, depth, lanes),
        in_specs=[VMEM] * 19,
        out_specs=HBM,
        scratch_shapes=[vm(*framed)] * 2 + [vm(*framed1)] * 2
        + [vm(3, COARSE_PITCH, lanes), vm(count // 2 + 2, framed[1], lanes),
           vm(2, 3, COARSE_PITCH, lanes), vm(count, depth, lanes), dma((8,))],
        compiler_params=params(),
    )(
        *near, *distant, to_even, *x_halo,
        U, F, IN, FX, FY, FZ, V1, F1, IN1, FX1, FY1, FZ1,
    )
    return out[:, None]


def solution(mesh):
    spec = P("grp", "box", None, None)
    return jax.shard_map(body, mesh=mesh, in_specs=(spec,) * 3, out_specs=spec, check_vma=False)
```
